32 devices in a mesh: dp: 4 (over z), context: 2 (over core), tensor: 4 (over y, x).
Axes of the slice: x: 2, y: 2, z: 4, core: 2. Of those that a mesh axis runs over, the one named last changes fastest.
Arguments:
- tokens: bfloat16 [8192, 2048], P(('dp', 'context')), may hold values from -6 to 6
- cotangent: bfloat16 [8192, 2048], P(('dp', 'context')), may hold values from -6 to 6
- lengths: int32 [4, 4], P('dp'), may hold values from 1 to 1024, as said below
- in_weight: float32 [2048, 7, 2048], P('dp', None, 'tensor'), may hold values from -0.125 to 0.125
- out_weight: float32 [5, 2048, 2048], P(None, 'tensor', 'dp')
- vectors: float32 [10, 2048], replicated
- in_first: float32 [2048, 7, 2048], P('dp', None, 'tensor'), may hold values from -27.1529 to 27.1529
- in_second: float32 [2048, 7, 2048], P('dp', None, 'tensor'), may hold values from 57.344 to 409.6
- out_first: float32 [5, 2048, 2048], P(None, 'tensor', 'dp'), may hold values from -27.1529 to 27.1529
- out_second: float32 [5, 2048, 2048], P(None, 'tensor', 'dp'), may hold values from 57.344 to 409.6
- vec_first: float32 [10, 2048], replicated, may hold values from -27.1529 to 27.1529
- vec_second: float32 [10, 2048], replicated, may hold values from 57.344 to 409.6
Outputs:
- result: bfloat16 [8192, 2048], P(('dp', 'context'), 'tensor')
- token_grad: float32 [8192, 2048], P(('dp', 'context'), 'tensor')
- new_in: float32 [2048, 7, 2048], P('dp', None, 'tensor')
- new_in_first: float32 [2048, 7, 2048], P('dp', None, 'tensor')
- new_in_second: float32 [2048, 7, 2048], P('dp', None, 'tensor')
- new_out: float32 [5, 2048, 2048], P(None, 'tensor', 'dp')
- new_out_first: float32 [5, 2048, 2048], P(None, 'tensor', 'dp')
- new_out_second: float32 [5, 2048, 2048], P(None, 'tensor', 'dp')
- new_vectors: float32 [10, 2048], replicated
- new_vec_first: float32 [10, 2048], replicated
- new_vec_second: float32 [10, 2048], replicated
The draws below stay inside these ranges and needn't reach their ends.
Inputs may be any that keep to these rules, and one draw needn't show every extreme that they name: `lengths`: each row sums to 2048; its largest length is 1024.
All inputs are finite; a program needn't handle non-finite values.
Results may differ from the reference program's by a relative error of at most 0.0044.
The reference program's roundings to bfloat16 on the way count: a program that leaves them out, or rounds other values in their place, can miss the bound.
Values may be sent and summed in bfloat16 or wider, within the bound.
A program may use at most 384 MiB of HBM per device.

```python
import math
import jax
import jax.numpy as jnp
from jax import lax

D = 2048
HD = 64
ROT = 32
FF = 8192
TOK_DEV = 1024
STEP = 10
NIN = 7
NOUT = 5
VROWS = 10
ROW = 2048
PACKS = 4
TOKENS = 8192
N_CONTEXT = 2


def draw_lengths(key, part):
    key = jax.random.fold_in(key, 11)
    key_first = jax.random.fold_in(key, 1)
    key_third = jax.random.fold_in(key, 2)
    key_flip = jax.random.fold_in(key, 3)
    first_len = jax.random.randint(key_first, (PACKS,), 1, TOK_DEV - 1)
    rest_len = TOK_DEV * N_CONTEXT - TOK_DEV - first_len
    low_end = jnp.maximum(1, rest_len - TOK_DEV)
    high_end = jnp.minimum(TOK_DEV, rest_len - 1)
    third_len = jax.random.randint(key_third, (PACKS,), low_end, high_end + 1)
    fourth_len = rest_len - third_len
    long_len = jnp.full((PACKS,), TOK_DEV, jnp.int32)
    packed = jnp.stack([first_len, long_len, third_len, fourth_len], 1).astype(jnp.int32)
    flip_bit = jax.random.randint(key_flip, (PACKS, 1), 0, 2)
    return jnp.where(flip_bit == 1, packed[:, ::-1], packed).astype(jnp.int32)


def draw_out_weight(key, part):
    key = jax.random.fold_in(key, 5)
    raw_values = jax.random.normal(key, (NOUT, D, D), jnp.float32)
    group_index = jnp.arange(NOUT)[:, None, None]
    scaling = jnp.where(group_index == 0, 8.0 / math.sqrt(D), 1.0 / math.sqrt(FF))
    return raw_values * scaling


def draw_vectors(key, part):
    key = jax.random.fold_in(key, 7)
    key_base = jax.random.fold_in(key, 1)
    key_gain = jax.random.fold_in(key, 2)
    base_values = jax.random.normal(key_base, (VROWS, D), jnp.float32)
    gain_values = 1.0 + 0.4 * jax.random.uniform(key_gain, (VROWS, D), jnp.float32, -1.0, 1.0)
    row_index = jnp.arange(VROWS)[:, None]
    return jnp.where(row_index == NIN + 1, gain_values, 0.3 * base_values)


def levels(key, dims, split, least, top_value):
    loudness, own = 1.0, jax.random.fold_in(key, 6)
    for axis_at, shards_of in split:
        heights = jnp.exp(jax.random.uniform(jax.random.fold_in(own, axis_at), (shards_of,), jnp.float32, least / len(split), top_value / len(split)))
        loudness = loudness * jnp.repeat(heights, dims[axis_at] // shards_of).reshape([-1 if axis == axis_at else 1 for axis in range(len(dims))])
    return loudness


def bell_draw(rng, extent, deviation, bound, cuts=(), kind=jnp.bfloat16):
    array = deviation * jax.random.normal(rng, extent, jnp.float32)
    if cuts:
        array = array * levels(rng, extent, cuts, -0.22, 0.18)
    return jnp.clip(array, -bound, bound).astype(kind)


def setup_inputs(seed: int = 0) -> dict:
    seeds = jax.random.split(jax.random.key(seed), 13)
    return {
        "tokens": bell_draw(seeds[0], (TOKENS, D), 1.0, 6.0, ((0, 8),)),
        "cotangent": bell_draw(seeds[1], (TOKENS, D), 1.0, 6.0, ((0, 8),)),
        "lengths": draw_lengths(jax.random.fold_in(seeds[12], 71), 0),
        "in_weight": bell_draw(seeds[3], (D, NIN, D), D ** -0.5, 0.125, ((0, 4), (2, 4)), jnp.float32),
        "out_weight": draw_out_weight(jax.random.fold_in(seeds[12], 71), 0),
        "vectors": draw_vectors(jax.random.fold_in(seeds[12], 71), 0),
        "in_first": bell_draw(seeds[6], (D, NIN, D), (0.055 * TOKENS ** 0.5), 27.1529, ((0, 4), (2, 4)), jnp.float32),
        "in_second": jnp.clip(jnp.exp(math.log(409.6) - 1.9661128 * jax.random.uniform(seeds[7], (D, NIN, D), jnp.float32) ** levels(seeds[7], (D, NIN, D), ((0, 4), (2, 4)), -0.2, 0.2)), 57.344, 409.6),
        "out_first": bell_draw(seeds[8], (NOUT, D, D), (0.055 * TOKENS ** 0.5), 27.1529, ((1, 4), (2, 4)), jnp.float32),
        "out_second": jnp.clip(jnp.exp(math.log(409.6) - 1.9661128 * jax.random.uniform(seeds[9], (NOUT, D, D), jnp.float32) ** levels(seeds[9], (NOUT, D, D), ((1, 4), (2, 4)), -0.2, 0.2)), 57.344, 409.6),
        "vec_first": bell_draw(seeds[10], (VROWS, D), (0.055 * TOKENS ** 0.5), 27.1529, (), jnp.float32),
        "vec_second": jnp.clip(jnp.exp(jax.random.uniform(seeds[11], (VROWS, D), jnp.float32, math.log(57.344), math.log(409.6))), 57.344, 409.6),
    }


norm_eps = 1e-05
beta_one = 0.9
beta_two = 0.95
adam_eps = 1e-08
weight_decay = 0.1
rate_matrix = 0.02
rate_vector = 0.4

@jax.custom_vjp
def low(v):
    return lax.optimization_barrier(v.astype(jnp.bfloat16)).astype(jnp.float32)

@jax.custom_vjp
def low_back(v):
    return v

def low_keep(v):
    return (low(v), None)

def low_pass(kept, grad):
    return (grad,)

def back_keep(v):
    return (v, None)

def back_low(kept, grad):
    return (low(grad),)
low.defvjp(low_keep, low_pass)
low_back.defvjp(back_keep, back_low)

def layout(lengths_row, row_span):
    seg_ends = jnp.cumsum(lengths_row).astype(jnp.int32)
    seg_starts = (seg_ends - lengths_row).astype(jnp.int32)
    places = jnp.arange(row_span, dtype=jnp.int32)
    segment = lax.optimization_barrier(jnp.sum((places[:, None] >= seg_ends[None, :]).astype(jnp.int32), 1)).astype(jnp.int32)
    numbers = jnp.arange(lengths_row.shape[0], dtype=jnp.int32)
    seg_begin = lax.optimization_barrier(jnp.sum(jnp.where(segment[:, None] == numbers[None, :], seg_starts[None, :], 0), 1)).astype(jnp.int32)
    return (segment, (places - seg_begin).astype(jnp.int32))

def rotate(flat_in, places, turn_sign):
    row_count = flat_in.shape[0]
    per_head = flat_in.reshape(row_count, flat_in.shape[1] // HD, HD)
    half_rot = ROT // 2
    frequency = 10000.0 ** (-2.0 * jnp.arange(half_rot, dtype=jnp.float32) / ROT)
    angles = turn_sign * places.astype(jnp.float32)[:, None] * frequency[None, :]
    cosine = jnp.cos(angles)[:, None, :]
    sine_part = jnp.sin(angles)[:, None, :]
    first_half = per_head[:, :, :half_rot]
    second_half = per_head[:, :, half_rot:ROT]
    turned = jnp.concatenate([first_half * cosine - second_half * sine_part, second_half * cosine + first_half * sine_part, per_head[:, :, ROT:]], 2)
    return turned.reshape(row_count, flat_in.shape[1])

def attend_row(queries, keys_row, values_row, segment):
    row_span = queries.shape[0]
    block_rows = min(512, row_span)
    blocks = row_span // block_rows
    head_count = queries.shape[1] // HD
    key_heads = keys_row.reshape(row_span, head_count, HD)
    value_heads = values_row.reshape(row_span, head_count, HD)
    key_index = jnp.arange(row_span, dtype=jnp.int32)

    def one_block(block_item):
        query_block, segment_block, index_block = block_item
        scores = jnp.einsum('qhe,khe->hqk', query_block, key_heads, precision=lax.Precision.HIGHEST) * HD ** (-0.5)
        scores = low_back(scores)
        allowed = (segment_block[:, None] == segment[None, :]) & (key_index[None, :] <= index_block[:, None])
        scores = jnp.where(allowed[None], scores, -1e+30)
        probs = low(jax.nn.softmax(scores, axis=-1))
        return jnp.einsum('hqk,khe->qhe', probs, value_heads, precision=lax.Precision.HIGHEST)
    block_outs = lax.map(jax.checkpoint(one_block), (queries.reshape(blocks, block_rows, head_count, HD), segment.reshape(blocks, block_rows), key_index.reshape(blocks, block_rows)))
    return block_outs.reshape(row_span, queries.shape[1])

def row_forward(row_in, segment, places, in_low, out_low, vector_master):
    centered = row_in - lax.optimization_barrier(jnp.mean(row_in, 1, keepdims=True))
    inv_dev = lax.rsqrt(lax.optimization_barrier(jnp.mean(centered * centered, 1, keepdims=True)) + norm_eps)
    unit_rows = centered * inv_dev
    normed = low(unit_rows * vector_master[NIN + 1] + vector_master[NIN + 2])
    projected = jnp.einsum('td,dgc->tgc', normed, in_low, precision=lax.Precision.HIGHEST) + vector_master[:NIN][None]
    projected = low_back(projected)
    queries = low(rotate(projected[:, 0], places, 1.0))
    keys_row = low(rotate(projected[:, 1], places, 1.0))
    values_row = low(projected[:, 2])
    activated = low(jax.nn.gelu(projected[:, 3:], approximate=True))
    attended = low(low_back(attend_row(queries, keys_row, values_row, segment)))
    branch_in = jnp.concatenate([attended[:, None], activated], 1)
    branch_out = jnp.einsum('tgc,gcd->td', branch_in, out_low, precision=lax.Precision.HIGHEST) + vector_master[NIN][None]
    return row_in + branch_out

def adamw(master, gradient, moment_one, moment_two, step_rate, decay_rate):
    first_new = beta_one * moment_one + (1.0 - beta_one) * gradient
    second_new = beta_two * moment_two + (1.0 - beta_two) * gradient * gradient
    first_hat = first_new / (1.0 - beta_one ** STEP)
    second_hat = second_new / (1.0 - beta_two ** STEP)
    updated = master - step_rate * (first_hat / (jnp.sqrt(second_hat) + adam_eps) + decay_rate * master)
    return (updated, first_new, second_new)

def row_layout(lengths_row):
    return layout(lengths_row, ROW)

def reference(tokens, cotangent, lengths, in_weight, out_weight, vectors, in_first, in_second, out_first, out_second, vec_first, vec_second):
    segments, places = jax.vmap(row_layout)(lengths)

    def forward(inputs, in_master, out_master, vector_master):
        in_low = low(in_master)
        out_low = low(out_master)

        def one_row(row_carry, row_item):
            row_in, row_segment, row_places = row_item
            return (row_carry, jax.checkpoint(row_forward)(row_in, row_segment, row_places, in_low, out_low, vector_master))
        carry_end, rows_out = lax.scan(one_row, jnp.zeros((), jnp.float32), (inputs.reshape(PACKS, ROW, D), segments, places))
        return rows_out.reshape(TOKENS, D)
    result, pull_back = jax.vjp(forward, tokens.astype(jnp.float32), in_weight, out_weight, vectors)
    token_grad, in_grad, out_grad, vector_grad = pull_back(cotangent.astype(jnp.float32))
    new_in, new_in_first, new_in_second = adamw(in_weight, in_grad, in_first, in_second, rate_matrix, weight_decay)
    new_out, new_out_first, new_out_second = adamw(out_weight, out_grad, out_first, out_second, rate_matrix, weight_decay)
    new_vectors, new_vec_first, new_vec_second = adamw(vectors, vector_grad, vec_first, vec_second, rate_vector, 0.0)
    return (result.astype(jnp.bfloat16), token_grad, new_in, new_in_first, new_in_second, new_out, new_out_first, new_out_second, new_vectors, new_vec_first, new_vec_second)
```

```python
import functools

import jax
import jax.numpy as jnp
from jax import lax
from jax.experimental import pallas as pl
from jax.experimental.pallas import tpu as pltpu
from jax.sharding import PartitionSpec as P

HD = 64
ROT = 32
STEP = 10
NIN = 7
MESH = pl.DeviceIdType.MESH
VMEM_LIMIT = 60 * 2**20

norm_eps = 1e-05
beta_one = 0.9
beta_two = 0.95
adam_eps = 1e-08
weight_decay = 0.1
rate_matrix = 0.02
rate_vector = 0.4


def adamw(master, gradient, moment_one, moment_two, step_rate, decay_rate):
    first_new = beta_one * moment_one + (1.0 - beta_one) * gradient
    second_new = beta_two * moment_two + (1.0 - beta_two) * gradient * gradient
    first_hat = first_new / (1.0 - beta_one**STEP)
    second_hat = second_new / (1.0 - beta_two**STEP)
    updated = master - step_rate * (
        first_hat / (jnp.sqrt(second_hat) + adam_eps) + decay_rate * master
    )
    return (updated, first_new, second_new)


def gelu_tanh(hidden_in):
    return jax.nn.gelu(hidden_in, approximate=True)


LANES = 2 * HD
WIDE = 4 * LANES
HID = WIDE // 2
ATT = 3 * LANES
LAG = 2

NT = (((1,), (1,)), ((), ()))
NN = (((1,), (0,)), ((), ()))
TN = (((0,), (0,)), ((), ()))


def dot(x, y, dims=NN):
    return lax.dot_general(x, y, dims, preferred_element_type=jnp.float32)


def line_barrier(n):
    z = lax.axis_index("dp")
    k = lax.axis_index("context")
    barrier = pltpu.get_barrier_semaphore()
    pl.semaphore_signal(barrier, inc=1, device_id={"context": 1 - k}, device_id_type=MESH)

    @pl.when(z < n - 1)
    def _():
        pl.semaphore_signal(barrier, inc=1, device_id={"dp": z + 1}, device_id_type=MESH)

    @pl.when(z > 0)
    def _():
        pl.semaphore_signal(barrier, inc=1, device_id={"dp": z - 1}, device_id_type=MESH)

    inner = jnp.where(z > 0, 1, 0) + jnp.where(z < n - 1, 1, 0)
    pl.semaphore_wait(barrier, 1 + inner)


def gelu_both(v):
    rate = 0.7978845608028654
    t = jnp.tanh(rate * (v + 0.044715 * (v * v * v)))
    value = 0.5 * v * (1.0 + t)
    slope = 0.5 * (1.0 + t) + 0.5 * v * (1.0 - t * t) * (rate * (1.0 + 3.0 * 0.044715 * (v * v)))
    return value, slope


def block_kernel(
    n, steps,
    own, tokens, cot_hbm, bias_ref, gain_ref, cos_ref, sin_ref, begin_ref,
    full, saved, total, swap, dkv_other,
    normed, cot, stage, wbuf, x, q_s, g_s, kv, dkv, dkv_tmp, mask, held, outgoing, swap_in, line, outbox,
    own_sem, send_sem, recv_sem, psend_sem, precv_sem,
    xsend_sem, xrecv_sem, lsend_sem, lrecv_sem, keep_sem, fsend_sem, frecv_sem,
    kvsend_sem, kvrecv_sem, dsend_sem, drecv_sem, load_sem, save_sem,
):
    units = 3 * steps
    size = own.shape[1]
    half = size // 2
    rows_all, width = normed.shape
    last = n - 1
    z = lax.axis_index("dp")
    k = lax.axis_index("context")
    mine = pl.ds(pl.multiple_of(k * half, half), half)
    theirs = pl.ds(pl.multiple_of((1 - k) * half, half), half)
    other_core = {"context": 1 - k}
    line_barrier(n)


    def hop(way, g, h, shard):
        source = own.at[g, mine] if isinstance(h, int) and h == 0 else full.at[g, shard, mine]
        return pltpu.make_async_remote_copy(
            src_ref=source,
            dst_ref=full.at[g, shard, mine],
            send_sem=send_sem.at[way, g, h],
            recv_sem=recv_sem.at[way, g, h],
            device_id={"dp": z + 1 - 2 * way},
            device_id_type=MESH,
        )

    def across(way, g, h, shard, rows):
        return pltpu.make_async_remote_copy(
            src_ref=full.at[g, shard, rows],
            dst_ref=full.at[g, shard, rows],
            send_sem=psend_sem.at[way, g, h],
            recv_sem=precv_sem.at[way, g, h],
            device_id=other_core,
            device_id_type=MESH,
        )

    def own_copy(g):
        return pltpu.make_async_copy(own.at[g], full.at[g, z], own_sem.at[g])

    def send_own(g):
        own_copy(g).start()

        @pl.when(z < last)
        def _():
            hop(0, g, 0, z).start()

        @pl.when(z > 0)
        def _():
            hop(1, g, 0, z).start()

    def gather_tick(m):
        @pl.when(m < units * last)
        def _():
            g, s = m // last, m % last + 1

            @pl.when((s == 1) & (g < units - 1))
            def _():
                send_own(g + 1)

            @pl.when(z >= s)
            def _():
                hop(0, g, s - 1, z - s).wait_recv()

                @pl.when(z < last)
                def _():
                    hop(0, g, s, z - s).start()

                across(0, g, s - 1, z - s, mine).start()

            @pl.when(z + s <= last)
            def _():
                hop(1, g, s - 1, z + s).wait_recv()

                @pl.when(z > 0)
                def _():
                    hop(1, g, s, z + s).start()

                across(1, g, s - 1, z + s, mine).start()

    def need(u):
        own_copy(u).wait()

        def one(i, carry):
            s = i + 1

            @pl.when(z >= s)
            def _():
                across(0, u, s - 1, z - s, theirs).wait_recv()

            @pl.when(z + s <= last)
            def _():
                across(1, u, s - 1, z + s, theirs).wait_recv()

            return carry

        lax.fori_loop(0, last, one, 0)
        pltpu.make_async_copy(full.at[u], wbuf, load_sem).start()
        pltpu.make_async_copy(full.at[u], wbuf, load_sem).wait()


    def exchange(g):
        return pltpu.make_async_remote_copy(
            src_ref=outgoing.at[g % 2],
            dst_ref=swap.at[g],
            send_sem=xsend_sem.at[g],
            recv_sem=xrecv_sem.at[g],
            device_id=other_core,
            device_id_type=MESH,
        )

    def slot_of(way, i):
        return i if way == 0 else n - i

    def pass_on(way, g, i):
        slot = slot_of(way, i)
        return pltpu.make_async_remote_copy(
            src_ref=line.at[g, slot],
            dst_ref=line.at[g, slot],
            send_sem=lsend_sem.at[way, g, i],
            recv_sem=lrecv_sem.at[way, g, i],
            device_id={"dp": z + 1 - 2 * way},
            device_id_type=MESH,
        )

    def keep(g):
        return pltpu.make_async_copy(outbox.at[g % (LAG + 3)], total.at[g, mine], keep_sem.at[g])

    def share(g, rows):
        return pltpu.make_async_remote_copy(
            src_ref=outbox.at[g % (LAG + 3)],
            dst_ref=total.at[g, rows],
            send_sem=fsend_sem.at[g],
            recv_sem=frecv_sem.at[g],
            device_id=other_core,
            device_id_type=MESH,
        )

    def prepare(g):
        exchange(g).wait_recv()
        pltpu.make_async_copy(swap.at[g], swap_in, load_sem).start()
        pltpu.make_async_copy(swap.at[g], swap_in, load_sem).wait()
        box = g % (LAG + 3)

        @pl.when(g >= LAG + 3)
        def _():
            keep(g - (LAG + 3)).wait()
            share(g - (LAG + 3), mine).wait_send()

        def one(j, carry):
            held[g % 3, j] += swap_in[j].astype(jnp.float32)
            return carry

        lax.fori_loop(0, n, one, 0)
        outbox[box] = held[g % 3, z]

    def scatter_step(way, m, distance):
        @pl.when((m >= 0) & (m < units * last))
        def _():
            g, i = m // last, m % last
            shard = n - 1 - i if way == 0 else i
            slot = slot_of(way, i)

            @pl.when(distance == 0)
            def _():
                line[g, slot] = held[g % 3, shard].astype(jnp.bfloat16)
                pass_on(way, g, i).start()

            @pl.when((distance > 0) & (distance <= last - i))
            def _():
                pass_on(way, g, i).wait_recv()

                @pl.when(distance < last - i)
                def _():
                    line[g, slot] = (line[g, slot].astype(jnp.float32) + held[g % 3, shard]).astype(
                        jnp.bfloat16
                    )
                    pass_on(way, g, i).start()

    def finish(g):
        box = g % (LAG + 3)

        @pl.when(z > 0)
        def _():
            outbox[box] += line[g, slot_of(0, n - 1 - z)].astype(jnp.float32)

        @pl.when(z < last)
        def _():
            outbox[box] += line[g, slot_of(1, z)].astype(jnp.float32)

        keep(g).start()
        share(g, mine).start()

    def scatter_tick(t):
        @pl.when((t >= 0) & (t % last == 0) & (t < units * last))
        def _():
            prepare(t // last)

        scatter_step(0, t - LAG * z, z)
        scatter_step(1, t - LAG * (last - z), last - z)
        done = t - last * (LAG + 1)

        @pl.when((done >= 0) & (done % last == 0))
        def _():
            finish(done // last)

    def ticks(gather_from, gather_count, scatter_from, scatter_count):
        def one_gather(i, carry):
            gather_tick(gather_from + i)
            return carry

        def one_scatter(i, carry):
            scatter_tick(scatter_from + i)
            return carry

        lax.fori_loop(0, gather_count, one_gather, 0)
        lax.fori_loop(0, scatter_count, one_scatter, 0)


    def normalize(i, carry):
        part = stage.shape[0]
        rows = pl.ds(pl.multiple_of(i * part, part), part)
        copy = pltpu.make_async_copy(tokens.at[rows], stage, load_sem)
        copy.start()
        copy.wait()

        def few(r, c):
            sub = pl.ds(pl.multiple_of(r * 64, 64), 64)
            there = pl.ds(pl.multiple_of(i * part + r * 64, 64), 64)
            inputs = stage[sub, :].astype(jnp.float32)
            centered = inputs - jnp.mean(inputs, 1, keepdims=True)
            inv_dev = lax.rsqrt(jnp.mean(centered * centered, 1, keepdims=True) + norm_eps)
            normed[there, :] = (centered * inv_dev * gain_ref[0:1, :] + gain_ref[1:2, :]).astype(
                jnp.bfloat16
            )
            return c

        lax.fori_loop(0, part // 64, few, 0)
        return carry

    def save(u):
        return pltpu.make_async_copy(x, saved.at[u], save_sem)

    def wait_saved(u):
        @pl.when(u > 0)
        def _():
            save(u - 1).wait()

    def gradients(u, split):
        @pl.when(u >= 2)
        def _():
            exchange(u - 2).wait_send()

        def one(j, carry):
            for core, place in ((k, None), (1 - k, outgoing)):
                cols = pl.ds(pl.multiple_of(j * size + core * half, half), half)
                into = dot(normed[:, cols], x[:, :split], TN)
                outof = dot(cot[:, cols], x[:, split:], TN)
                if place is None:
                    held[u % 3, j, :, :split] = into
                    held[u % 3, j, :, split:] = outof
                else:
                    place[u % 2, j, :, :split] = into.astype(jnp.bfloat16)
                    place[u % 2, j, :, split:] = outof.astype(jnp.bfloat16)
            return carry

        lax.fori_loop(0, n, one, 0)
        exchange(u).start()

    block = min(512, rows_all)

    def hidden_unit(u, gather_from, gather_count):
        need(u)
        wait_saved(u)

        def one(i, carry):
            rows = pl.ds(pl.multiple_of(i * block, block), block)
            pre = dot(normed[rows, :], wbuf[:, :, :HID].reshape(width, HID)) + bias_ref[u][:, :HID]
            value, slope = gelu_both(pre)
            x[rows, HID:] = value.astype(jnp.bfloat16)
            grad = dot(cot[rows, :], wbuf[:, :, HID:].reshape(width, HID))
            x[rows, :HID] = (grad * slope).astype(jnp.bfloat16)
            return carry

        lax.fori_loop(0, rows_all // block, one, 0)
        save(u).start()
        early = gather_count // 2
        scatter_from = (u - 1) * last
        ticks(gather_from, early, scatter_from, last // 2)
        gradients(u, HID)
        ticks(gather_from + early, gather_count - early, scatter_from + last // 2, last - last // 2)

    qblock = mask.shape[1]
    window = mask.shape[0]
    qblocks = rows_all // qblock

    def rope(v, rows, sign):
        half_rot = ROT // 2
        lane = lax.broadcasted_iota(jnp.int32, v.shape, 1) % HD
        ahead = pltpu.roll(v, LANES - half_rot, 1)
        behind = pltpu.roll(v, half_rot, 1)
        other = jnp.where(lane < half_rot, -ahead, behind)
        return v * cos_ref[rows, :] + other * (sign * sin_ref[rows, :])

    def send_kv(s):
        rows = pl.ds(pl.multiple_of(k * rows_all, rows_all), rows_all)
        return pltpu.make_async_remote_copy(
            src_ref=kv.at[s, :, rows],
            dst_ref=kv.at[s, :, rows],
            send_sem=kvsend_sem.at[s],
            recv_sem=kvrecv_sem.at[s],
            device_id=other_core,
            device_id_type=MESH,
        )

    def recv_kv(s):
        rows = pl.ds(pl.multiple_of((1 - k) * rows_all, rows_all), rows_all)
        return pltpu.make_async_remote_copy(
            src_ref=kv.at[s, :, rows],
            dst_ref=kv.at[s, :, rows],
            send_sem=kvsend_sem.at[s],
            recv_sem=kvrecv_sem.at[s],
            device_id=other_core,
            device_id_type=MESH,
        )

    def send_dkv(s):
        return pltpu.make_async_remote_copy(
            src_ref=dkv.at[:, pl.ds(0, rows_all)],
            dst_ref=dkv_other.at[s],
            send_sem=dsend_sem.at[s],
            recv_sem=drecv_sem.at[s],
            device_id=other_core,
            device_id_type=MESH,
        )

    def attention_unit(u, s, gather_from, gather_count):
        need(u)
        wait_saved(u)

        @pl.when((s > 0) & (k == 1))
        def _():
            send_dkv(s - 1).wait_send()

        def project(i, carry):
            rows = pl.ds(pl.multiple_of(i * block, block), block)
            there = pl.ds(pl.multiple_of(k * rows_all + i * block, block), block)
            pre = dot(normed[rows, :], wbuf[:, :, :ATT].reshape(width, ATT)) + bias_ref[u][:, :ATT]
            grad = dot(cot[rows, :], wbuf[:, :, ATT:].reshape(width, LANES))
            g_s[rows, :] = grad.astype(jnp.bfloat16)
            query = rope(pre[:, :LANES], rows, 1.0).astype(jnp.bfloat16)
            q_s[rows, :] = query * jnp.bfloat16(HD**-0.5)
            kv[s, 0, there, :] = rope(pre[:, LANES : 2 * LANES], rows, 1.0).astype(jnp.bfloat16)
            kv[s, 1, there, :] = pre[:, 2 * LANES :].astype(jnp.bfloat16)
            return carry

        lax.fori_loop(0, rows_all // block, project, 0)
        send_kv(s).start()
        dkv[...] = jnp.zeros_like(dkv)
        scatter_from = (u - 1) * last
        per_block = gather_count // qblocks
        early = gather_count - per_block * qblocks
        ticks(gather_from, early, scatter_from, 0)
        recv_kv(s).wait_recv()

        def queries(b, carry):
            first_query = k * rows_all + b * qblock
            first_key = pl.multiple_of(jnp.maximum(first_query + qblock - window, 0), qblock)
            rows = pl.ds(pl.multiple_of(b * qblock, qblock), qblock)
            keys = pl.ds(first_key, window)
            key_at = first_key + lax.broadcasted_iota(jnp.int32, (window, qblock), 0)
            query_at = first_query + lax.broadcasted_iota(jnp.int32, (window, qblock), 1)
            begin = begin_ref[0:1, rows]
            mask[...] = jnp.where((key_at >= begin) & (key_at <= query_at), 0.0, -1e30)
            lane = lax.broadcasted_iota(jnp.int32, (qblock, LANES), 1)
            att = jnp.zeros((qblock, LANES), jnp.float32)
            dq = jnp.zeros((qblock, LANES), jnp.float32)
            for head in range(2):
                inside = (lane >= head * HD) & (lane < (head + 1) * HD)
                q_own = jnp.where(inside, q_s[rows, :], jnp.zeros((qblock, LANES), jnp.bfloat16))
                g_own = jnp.where(inside, g_s[rows, :], jnp.zeros((qblock, LANES), jnp.bfloat16))
                scores = dot(kv[s, 0, keys, :], q_own, NT) + mask[...]
                weights = jnp.exp(scores - jnp.max(scores, 0, keepdims=True))
                probs = weights * (1.0 / jnp.sum(weights, 0, keepdims=True))
                probs_low = probs.astype(jnp.bfloat16)
                grad_probs = dot(kv[s, 1, keys, :], g_own, NT)
                inner = jnp.sum(probs * grad_probs, 0, keepdims=True)
                grad_scores = (probs * (grad_probs - inner)).astype(jnp.bfloat16)
                att = jnp.where(inside, dot(probs_low, kv[s, 1, keys, :], TN), att)
                dq = jnp.where(inside, dot(grad_scores, kv[s, 0, keys, :], TN), dq)
                dkv[1, keys, :] += dot(probs_low, g_own)
                dkv[0, keys, :] += dot(grad_scores, q_own)
            x[rows, ATT:] = att.astype(jnp.bfloat16)
            x[rows, :LANES] = rope(dq * HD**-0.5, rows, -1.0).astype(jnp.bfloat16)
            low, high = b * last // qblocks, (b + 1) * last // qblocks
            ticks(gather_from + early + b * per_block, per_block, scatter_from + low, high - low)
            return carry

        lax.fori_loop(0, qblocks, queries, 0)

        @pl.when(k == 1)
        def _():
            send_dkv(s).start()

        @pl.when(k == 0)
        def _():
            send_dkv(s).wait_recv()
            copy = pltpu.make_async_copy(dkv_other.at[s], dkv_tmp, load_sem)
            copy.start()
            copy.wait()

        @pl.when(k == 1)
        def _():
            dkv_tmp[...] = jnp.zeros_like(dkv_tmp)

        def turn(i, carry):
            rows = pl.ds(pl.multiple_of(i * qblock, qblock), qblock)
            there = pl.ds(pl.multiple_of(k * rows_all + i * qblock, qblock), qblock)
            x[rows, LANES : 2 * LANES] = rope(
                dkv[0, there, :] + dkv_tmp[0, rows, :], rows, -1.0
            ).astype(jnp.bfloat16)
            x[rows, 2 * LANES : ATT] = (dkv[1, there, :] + dkv_tmp[1, rows, :]).astype(jnp.bfloat16)
            return carry

        lax.fori_loop(0, qblocks, turn, 0)
        save(u).start()
        gradients(u, ATT)


    cot_copy = pltpu.make_async_copy(cot_hbm, cot, save_sem)
    cot_copy.start()
    send_own(0)
    lax.fori_loop(0, rows_all // stage.shape[0], normalize, 0)
    cot_copy.wait()
    per_step = 3 * last
    in_hidden = 2 * per_step // 9
    in_attention = per_step - 2 * in_hidden
    lead = max(last, 2 * last - in_hidden)
    ticks(0, lead, 0, 0)

    def super_step(s, carry):
        base = s * per_step + lead
        hidden_unit(3 * s, base, in_hidden)
        attention_unit(3 * s + 1, s, base + in_hidden, in_attention)
        hidden_unit(3 * s + 2, base + in_hidden + in_attention, in_hidden)
        return carry

    lax.fori_loop(0, steps, super_step, 0)
    ticks(0, 0, (units - 1) * last, last * (LAG + 1) + 1)


    save(units - 1).wait()
    exchange(units - 2).wait_send()
    exchange(units - 1).wait_send()

    @pl.when(k == 1)
    def _():
        send_dkv(steps - 1).wait_send()

    def drain_kv(s, carry):
        send_kv(s).wait_send()
        return carry

    lax.fori_loop(0, steps, drain_kv, 0)

    def drain(m, carry):
        g, s = m // last, m % last + 1

        @pl.when(s == 1)
        def _():
            @pl.when(z < last)
            def _():
                hop(0, g, 0, z).wait_send()

            @pl.when(z > 0)
            def _():
                hop(1, g, 0, z).wait_send()

            @pl.when(g >= units - (LAG + 3))
            def _():
                keep(g).wait()
                share(g, mine).wait_send()

            share(g, theirs).wait_recv()

        @pl.when(z >= s)
        def _():
            @pl.when(z < last)
            def _():
                hop(0, g, s, z - s).wait_send()

            across(0, g, s - 1, z - s, mine).wait_send()

        @pl.when(z + s <= last)
        def _():
            @pl.when(z > 0)
            def _():
                hop(1, g, s, z + s).wait_send()

            across(1, g, s - 1, z + s, mine).wait_send()

        for way in range(2):
            distance = z if way == 0 else last - z

            @pl.when(distance < last - (s - 1))
            def _():
                pass_on(way, g, s - 1).wait_send()

        return carry

    lax.fori_loop(0, units * last, drain, 0)


def run_block(own, tokens, cotangent, bias, gain, cosine, sine, begin):
    n = lax.axis_size("dp")
    units, size = own.shape[0], own.shape[1]
    steps = units // 3
    half = size // 2
    rows, width = tokens.shape
    qblock = min(256, rows)
    span = 2 * rows
    window = min(span, rows + qblock)
    low, full_type = jnp.bfloat16, jnp.float32
    anywhere = pl.BlockSpec(memory_space=pl.ANY)
    vm = pl.BlockSpec(memory_space=pltpu.VMEM)
    dma = pltpu.SemaphoreType.DMA
    return pl.pallas_call(
        functools.partial(block_kernel, n, steps),
        out_shape=(
            jax.ShapeDtypeStruct((units, n, size, WIDE), low),
            jax.ShapeDtypeStruct((units, rows, WIDE), low),
            jax.ShapeDtypeStruct((units, size, WIDE), full_type),
            jax.ShapeDtypeStruct((units, n, half, WIDE), low),
            jax.ShapeDtypeStruct((steps, 2, rows, LANES), full_type),
        ),
        in_specs=[anywhere] * 3 + [vm] * 5,
        out_specs=[anywhere] * 5,
        scratch_shapes=[
            pltpu.VMEM((rows, width), low),
            pltpu.VMEM((rows, width), low),
            pltpu.VMEM((256, width), low),
            pltpu.VMEM((n, size, WIDE), low),
            pltpu.VMEM((rows, WIDE), low),
            pltpu.VMEM((rows, LANES), low),
            pltpu.VMEM((rows, LANES), low),
            pltpu.VMEM((steps, 2, span, LANES), low),
            pltpu.VMEM((2, span, LANES), full_type),
            pltpu.VMEM((2, rows, LANES), full_type),
            pltpu.VMEM((window, qblock), full_type),
            pltpu.VMEM((3, n, half, WIDE), full_type),
            pltpu.VMEM((2, n, half, WIDE), low),
            pltpu.VMEM((n, half, WIDE), low),
            pltpu.VMEM((units, n + 1, half, WIDE), low),
            pltpu.VMEM((LAG + 3, half, WIDE), full_type),
            dma((units,)),
            dma((2, units, n)),
            dma((2, units, n)),
            dma((2, units, n)),
            dma((2, units, n)),
            dma((units,)),
            dma((units,)),
            dma((2, units, n - 1)),
            dma((2, units, n - 1)),
            dma((units,)),
            dma((units,)),
            dma((units,)),
            dma((steps,)),
            dma((steps,)),
            dma((steps,)),
            dma((steps,)),
            dma,
            dma,
        ],
        compiler_params=pltpu.CompilerParams(
            collective_id=1, has_side_effects=True, vmem_limit_bytes=VMEM_LIMIT
        ),
        name="parallel_block",
    )(own, tokens, cotangent, bias, gain, cosine, sine, begin)


def pack_weights(in_weight, out_weight):
    size, _, cols = in_weight.shape
    steps = cols // LANES
    into = jnp.transpose(in_weight, (1, 0, 2)).astype(jnp.bfloat16)
    outof = jnp.transpose(out_weight.astype(jnp.bfloat16), (0, 2, 1))
    per = cols // HID
    hid_in = into[3:].reshape(4, size, per, HID).transpose(0, 2, 1, 3).reshape(steps, 2, size, HID)
    hid_out = outof[1:].reshape(4, size, per, HID).transpose(0, 2, 1, 3).reshape(steps, 2, size, HID)
    hid = jnp.concatenate([hid_in, hid_out], 3)
    att_in = into[:3].reshape(3, size, steps, LANES).transpose(2, 1, 0, 3).reshape(steps, size, ATT)
    att_out = outof[0].reshape(size, steps, LANES).transpose(1, 0, 2)
    att = jnp.concatenate([att_in, att_out], 2)
    return jnp.stack([hid[:, 0], att, hid[:, 1]], 1).reshape(3 * steps, size, WIDE)


def unpack_columns(packed, lead):
    steps = packed.shape[0] // 3
    per = steps * LANES // HID
    by_step = packed.reshape((steps, 3) + lead + (WIDE,))
    hid = jnp.stack([by_step[:, 0], by_step[:, 2]], 1).reshape((4, per) + lead + (WIDE,))
    att = by_step[:, 1]
    axes = len(lead)

    def widen(v):
        order = (0,) + tuple(range(2, 2 + axes)) + (1, 2 + axes)
        return v.transpose(order).reshape((v.shape[0],) + lead + (v.shape[1] * v.shape[-1],))

    att_parts = jnp.stack([att[..., i * LANES : (i + 1) * LANES] for i in range(4)], 0)
    att_wide = widen(att_parts)
    into = jnp.concatenate([att_wide[:3], widen(hid[..., :HID])], 0)
    outof = jnp.concatenate([att_wide[3:], widen(hid[..., HID:])], 0)
    return into, outof


def layout(lengths_row, row_span):
    seg_ends = jnp.cumsum(lengths_row)
    seg_starts = seg_ends - lengths_row
    places = jnp.arange(row_span, dtype=jnp.int32)
    segment = jnp.sum((places[:, None] >= seg_ends[None, :]).astype(jnp.int32), 1)
    numbers = jnp.arange(lengths_row.shape[0], dtype=jnp.int32)
    return jnp.sum(jnp.where(segment[:, None] == numbers[None, :], seg_starts[None, :], 0), 1)


def rope_tables(places):
    half_rot = ROT // 2
    lane = jnp.arange(2 * HD, dtype=jnp.int32) % HD
    exponent = (lane % half_rot).astype(jnp.float32)
    frequency = 10000.0 ** (-2.0 * exponent / ROT)
    angles = places.astype(jnp.float32)[:, None] * frequency[None, :]
    turned = (lane < ROT)[None, :]
    cosine = jnp.where(turned, jnp.cos(angles), 1.0)
    sine = jnp.where(turned, jnp.sin(angles), 0.0)
    return cosine, sine


def body(
    tokens,
    cotangent,
    lengths,
    in_weight,
    out_weight,
    vectors,
    in_first,
    in_second,
    out_first,
    out_second,
    vec_first,
    vec_second,
):
    local_rows, model_width = tokens.shape
    slice_width = in_weight.shape[2]
    context_count = lax.axis_size("context")
    context_index = lax.axis_index("context")
    tensor_count = lax.axis_size("tensor")
    tensor_index = lax.axis_index("tensor")
    row_span = local_rows * context_count
    first_row = context_index * local_rows
    begin_all = layout(lengths[0], row_span)
    begin = lax.dynamic_slice_in_dim(begin_all, first_row, local_rows, 0)
    places = first_row + jnp.arange(local_rows, dtype=jnp.int32) - begin
    tables = rope_tables(places)

    inputs = tokens.astype(jnp.float32)
    centered = inputs - jnp.mean(inputs, 1, keepdims=True)
    inv_dev = lax.rsqrt(jnp.mean(centered * centered, 1, keepdims=True) + norm_eps)
    unit_rows = centered * inv_dev
    norm_gain = vectors[NIN + 1]
    column = tensor_index * slice_width
    in_bias = lax.dynamic_slice_in_dim(vectors[:NIN], column, slice_width, 1)
    steps = slice_width // LANES
    hid_bias = in_bias[3:].reshape(steps, 2, HID)
    att_bias = in_bias[:3].reshape(3, steps, LANES).transpose(1, 0, 2).reshape(steps, ATT)
    bias = jnp.stack(
        [
            jnp.pad(hid_bias[:, 0], ((0, 0), (0, WIDE - HID))),
            jnp.pad(att_bias, ((0, 0), (0, WIDE - ATT))),
            jnp.pad(hid_bias[:, 1], ((0, 0), (0, WIDE - HID))),
        ],
        1,
    ).reshape(3 * steps, 1, WIDE)
    own = pack_weights(in_weight, out_weight)
    full, saved, total_packed, _, _ = run_block(
        own, tokens, cotangent, bias, vectors[NIN + 1 : NIN + 3], tables[0], tables[1], begin[None]
    )
    total_in, total_out = unpack_columns(total_packed, (own.shape[1],))
    grad_projected, mixed = unpack_columns(saved, (local_rows,))

    units = full.shape[0]
    splits = [ATT if u % 3 == 1 else HID for u in range(units)]
    partial_out = sum(
        lax.dot_general(
            saved[u][:, splits[u] :], full[u].reshape(model_width, WIDE)[:, splits[u] :], NT,
            preferred_element_type=jnp.float32,
        )
        for u in range(units)
    )
    norm_partial = sum(
        lax.dot_general(
            saved[u][:, : splits[u]], full[u].reshape(model_width, WIDE)[:, : splits[u]], NT,
            preferred_element_type=jnp.float32,
        )
        for u in range(units)
    )
    branch = lax.psum_scatter(
        partial_out.astype(jnp.bfloat16), "tensor", scatter_dimension=1, tiled=True
    ).astype(jnp.float32)
    out_width = branch.shape[1]
    out_column = tensor_index * out_width
    residual = lax.dynamic_slice_in_dim(inputs, out_column, out_width, 1)
    out_bias = lax.dynamic_slice_in_dim(vectors[NIN], out_column, out_width, 0)
    result = (residual + (branch + out_bias[None])).astype(jnp.bfloat16)

    unit_partial = norm_partial * norm_gain
    row_sums = lax.psum(
        jnp.stack([jnp.sum(unit_partial, 1), jnp.sum(unit_partial * unit_rows, 1)], 0), "tensor"
    ) / model_width
    grad_normed = lax.psum_scatter(
        norm_partial.astype(jnp.bfloat16), "tensor", scatter_dimension=1, tiled=True
    ).astype(jnp.float32)
    unit_slice = lax.dynamic_slice_in_dim(unit_rows, out_column, out_width, 1)
    gain_slice = lax.dynamic_slice_in_dim(norm_gain, out_column, out_width, 0)
    cot_slice = lax.dynamic_slice_in_dim(cotangent, out_column, out_width, 1).astype(jnp.float32)
    token_grad = (
        inv_dev * (grad_normed * gain_slice - row_sums[0][:, None] - unit_slice * row_sums[1][:, None])
        + cot_slice
    )

    vector_slice = jnp.stack(
        [jnp.sum(grad_projected[g].astype(jnp.float32), 0) for g in range(NIN)]
        + [
            jnp.sum(cot_slice, 0),
            jnp.sum(grad_normed * unit_slice, 0),
            jnp.sum(grad_normed, 0),
        ],
        0,
    )
    vector_rows = lax.dynamic_update_slice_in_dim(
        jnp.zeros((NIN + 3, model_width), jnp.float32), vector_slice, column, 1
    )
    vector_grad = lax.psum(vector_rows, ("dp", "context", "tensor"))
    new_vectors, new_vec_first, new_vec_second = adamw(
        vectors, vector_grad, vec_first, vec_second, rate_vector, 0.0
    )
    new_in, new_in_first, new_in_second = adamw(
        in_weight, jnp.transpose(total_in, (1, 0, 2)), in_first, in_second, rate_matrix, weight_decay
    )
    new_out, new_out_first, new_out_second = adamw(
        out_weight, jnp.transpose(total_out, (0, 2, 1)), out_first, out_second, rate_matrix, weight_decay
    )
    return (
        result,
        token_grad,
        new_in,
        new_in_first,
        new_in_second,
        new_out,
        new_out_first,
        new_out_second,
        new_vectors,
        new_vec_first,
        new_vec_second,
    )


def solution(mesh):
    return jax.shard_map(
        body,
        mesh=mesh,
        in_specs=(
            P(("dp", "context"), None),
            P(("dp", "context"), None),
            P("dp", None),
            P("dp", None, "tensor"),
            P(None, "tensor", "dp"),
            P(),
            P("dp", None, "tensor"),
            P("dp", None, "tensor"),
            P(None, "tensor", "dp"),
            P(None, "tensor", "dp"),
            P(),
            P(),
        ),
        out_specs=(
            P(("dp", "context"), "tensor"),
            P(("dp", "context"), "tensor"),
            P("dp", None, "tensor"),
            P("dp", None, "tensor"),
            P("dp", None, "tensor"),
            P(None, "tensor", "dp"),
            P(None, "tensor", "dp"),
            P(None, "tensor", "dp"),
            P(),
            P(),
            P(),
        ),
        check_vma=False,
    )
```

```python
import functools

import jax
import jax.numpy as jnp
from jax import lax
from jax.experimental import pallas as pl
from jax.experimental.pallas import tpu as pltpu
from jax.sharding import PartitionSpec as P

HD = 64
ROT = 32
STEP = 10
NIN = 7
MESH = pl.DeviceIdType.MESH
VMEM_LIMIT = 60 * 2**20

norm_eps = 1e-05
beta_one = 0.9
beta_two = 0.95
adam_eps = 1e-08
weight_decay = 0.1
rate_matrix = 0.02
rate_vector = 0.4


def adamw(master, gradient, moment_one, moment_two, step_rate, decay_rate):
    first_new = beta_one * moment_one + (1.0 - beta_one) * gradient
    second_new = beta_two * moment_two + (1.0 - beta_two) * gradient * gradient
    first_hat = first_new / (1.0 - beta_one**STEP)
    second_hat = second_new / (1.0 - beta_two**STEP)
    updated = master - step_rate * (
        first_hat / (jnp.sqrt(second_hat) + adam_eps) + decay_rate * master
    )
    return (updated, first_new, second_new)


LANES = 2 * HD
WIDE = 4 * LANES
HID = WIDE // 2
ATT = 3 * LANES
LAG = 2

NT = (((1,), (1,)), ((), ()))
NN = (((1,), (0,)), ((), ()))
TN = (((0,), (0,)), ((), ()))


def dot(x, y, dims=NN):
    return lax.dot_general(x, y, dims, preferred_element_type=jnp.float32)


def greet(n, peers):
    z = lax.axis_index("dp")
    k = lax.axis_index("context")
    t = lax.axis_index("tensor")
    barrier = pltpu.get_barrier_semaphore()
    pl.semaphore_signal(barrier, inc=1, device_id={"context": 1 - k}, device_id_type=MESH)
    for i in range(1, n):
        pl.semaphore_signal(barrier, inc=1, device_id={"dp": lax.rem(z + i, n)}, device_id_type=MESH)
    for i in range(1, peers):
        pl.semaphore_signal(
            barrier, inc=1, device_id={"tensor": lax.rem(t + i, peers)}, device_id_type=MESH
        )
    pl.semaphore_wait(barrier, n + peers - 1)


def gelu_both(v):
    rate = 0.7978845608028654
    t = jnp.tanh(rate * (v + 0.044715 * (v * v * v)))
    value = 0.5 * v * (1.0 + t)
    slope = 0.5 * (1.0 + t) + 0.5 * v * (1.0 - t * t) * (rate * (1.0 + 3.0 * 0.044715 * (v * v)))
    return value, slope


def block_kernel(
    n, steps, peers,
    in_w, out_w, tokens, cot_hbm, bias_ref, vec_ref, cos_ref, sin_ref, begin_ref,
    full, saved, total, swap, dkv_other, arrived, result, token_grad, vec_grad,
    kv, held, line, outbox, stats, vec, vec_core, vec_line, vec_all, sums, sums_in,
    send_sem, recv_sem, psend_sem, precv_sem,
    xsend_sem, xrecv_sem, lsend_sem, lrecv_sem, keep_sem, fsend_sem, frecv_sem,
    kvsend_sem, kvrecv_sem, dsend_sem, drecv_sem, load_sem, save_sem, weight_sem, pack_sem,
    tsend_sem, trecv_sem, ssend_sem, srecv_sem, vsend_sem, vrecv_sem, tile_sem, out_sem,
):
    units = 3 * steps
    size, cols_all = in_w.shape[1], in_w.shape[2]
    half = size // 2
    rows_all, width = tokens.shape
    tensor = lax.axis_index("tensor")
    columns = pl.ds(pl.multiple_of(tensor * size, size), size)
    last = n - 1
    z = lax.axis_index("dp")
    k = lax.axis_index("context")
    mine = pl.ds(pl.multiple_of(k * half, half), half)
    theirs = pl.ds(pl.multiple_of((1 - k) * half, half), half)
    other_core = {"context": 1 - k}
    greet(n, peers)


    def hop(way, g, h, shard):
        return pltpu.make_async_remote_copy(
            src_ref=full.at[g, shard, mine],
            dst_ref=full.at[g, shard, mine],
            send_sem=send_sem.at[way, g, h],
            recv_sem=recv_sem.at[way, g, h],
            device_id={"dp": z + 1 - 2 * way},
            device_id_type=MESH,
        )

    def across(way, g, h, shard, rows):
        return pltpu.make_async_remote_copy(
            src_ref=full.at[g, shard, rows],
            dst_ref=full.at[g, shard, rows],
            send_sem=psend_sem.at[way, g, h],
            recv_sem=precv_sem.at[way, g, h],
            device_id=other_core,
            device_id_type=MESH,
        )

    def send_own(g):
        @pl.when(z < last)
        def _():
            hop(0, g, 0, z).start()

        @pl.when(z > 0)
        def _():
            hop(1, g, 0, z).start()

    def gather_tick(m):
        @pl.when(m < units * last)
        def _():
            g, s = m // last, m % last + 1

            @pl.when((s == 1) & (g < units - 1))
            def _():
                send_own(g + 1)

            @pl.when(z >= s)
            def _():
                hop(0, g, s - 1, z - s).wait_recv()

                @pl.when(z < last)
                def _():
                    hop(0, g, s, z - s).start()

                across(0, g, s - 1, z - s, mine).start()

            @pl.when(z + s <= last)
            def _():
                hop(1, g, s - 1, z + s).wait_recv()

                @pl.when(z > 0)
                def _():
                    hop(1, g, s, z + s).start()

                across(1, g, s - 1, z + s, mine).start()

    def need(u):
        def one(i, carry):
            s = i + 1

            @pl.when(z >= s)
            def _():
                across(0, u, s - 1, z - s, theirs).wait_recv()

            @pl.when(z + s <= last)
            def _():
                across(1, u, s - 1, z + s, theirs).wait_recv()

            return carry

        lax.fori_loop(0, last, one, 0)

    def send_kv(s):
        rows = pl.ds(pl.multiple_of(k * rows_all, rows_all), rows_all)
        return pltpu.make_async_remote_copy(
            src_ref=kv.at[s, :, rows],
            dst_ref=kv.at[s, :, rows],
            send_sem=kvsend_sem.at[s],
            recv_sem=kvrecv_sem.at[s],
            device_id=other_core,
            device_id_type=MESH,
        )


    def exchange_from(outgoing, g):
        return pltpu.make_async_remote_copy(
            src_ref=outgoing,
            dst_ref=swap.at[g],
            send_sem=xsend_sem.at[g],
            recv_sem=xrecv_sem.at[g],
            device_id=other_core,
            device_id_type=MESH,
        )

    def slot_of(way, i):
        return i if way == 0 else n - i

    def pass_on(way, g, i):
        slot = slot_of(way, i)
        return pltpu.make_async_remote_copy(
            src_ref=line.at[g, slot],
            dst_ref=line.at[g, slot],
            send_sem=lsend_sem.at[way, g, i],
            recv_sem=lrecv_sem.at[way, g, i],
            device_id={"dp": z + 1 - 2 * way},
            device_id_type=MESH,
        )

    def keep(g):
        return pltpu.make_async_copy(outbox.at[g % (LAG + 3)], total.at[g, mine], keep_sem.at[g])

    def share(g, rows):
        return pltpu.make_async_remote_copy(
            src_ref=outbox.at[g % (LAG + 3)],
            dst_ref=total.at[g, rows],
            send_sem=fsend_sem.at[g],
            recv_sem=frecv_sem.at[g],
            device_id=other_core,
            device_id_type=MESH,
        )

    def prepare(g, swap_in):
        exchange_from(swap_in, g).wait_recv()
        pltpu.make_async_copy(swap.at[g], swap_in, load_sem).start()
        pltpu.make_async_copy(swap.at[g], swap_in, load_sem).wait()
        box = g % (LAG + 3)

        @pl.when(g >= LAG + 3)
        def _():
            keep(g - (LAG + 3)).wait()
            share(g - (LAG + 3), mine).wait_send()

        def one(j, carry):
            held[g % 3, j] += swap_in[j].astype(jnp.float32)
            return carry

        lax.fori_loop(0, n, one, 0)
        outbox[box] = held[g % 3, z]

    def scatter_step(way, m, distance):
        @pl.when((m >= 0) & (m < units * last))
        def _():
            g, i = m // last, m % last
            shard = n - 1 - i if way == 0 else i
            slot = slot_of(way, i)

            @pl.when(distance == 0)
            def _():
                line[g, slot] = held[g % 3, shard].astype(jnp.bfloat16)
                pass_on(way, g, i).start()

            @pl.when((distance > 0) & (distance <= last - i))
            def _():
                pass_on(way, g, i).wait_recv()

                @pl.when(distance < last - i)
                def _():
                    line[g, slot] = (line[g, slot].astype(jnp.float32) + held[g % 3, shard]).astype(
                        jnp.bfloat16
                    )
                    pass_on(way, g, i).start()

    def finish(g):
        box = g % (LAG + 3)

        @pl.when(z > 0)
        def _():
            outbox[box] += line[g, slot_of(0, n - 1 - z)].astype(jnp.float32)

        @pl.when(z < last)
        def _():
            outbox[box] += line[g, slot_of(1, z)].astype(jnp.float32)

        keep(g).start()
        share(g, mine).start()

    def scatter_tick(t, swap_in):
        @pl.when((t >= 0) & (t % last == 0) & (t < units * last))
        def _():
            prepare(t // last, swap_in)

        scatter_step(0, t - LAG * z, z)
        scatter_step(1, t - LAG * (last - z), last - z)
        done = t - last * (LAG + 1)

        @pl.when((done >= 0) & (done % last == 0))
        def _():
            finish(done // last)

    def run_ticks(swap_in, gather_from, gather_count, scatter_from, scatter_count):
        def one_gather(i, carry):
            gather_tick(gather_from + i)
            return carry

        def one_scatter(i, carry):
            scatter_tick(scatter_from + i, swap_in)
            return carry

        lax.fori_loop(0, gather_count, one_gather, 0)
        lax.fori_loop(0, scatter_count, one_scatter, 0)

    def forward_backward(
        normed, cot, stage, raw_in, raw_out, packed, wbuf, x, q_s, g_s, dkv, dkv_tmp, mask, outgoing, swap_in
    ):

        def exchange(g):
            return exchange_from(outgoing.at[g % 2], g)

        def ticks(gather_from, gather_count, scatter_from, scatter_count):
            run_ticks(swap_in, gather_from, gather_count, scatter_from, scatter_count)

        def normalize(i):
            part = stage.shape[0]
            rows = pl.ds(pl.multiple_of(i * part, part), part)
            copy = pltpu.make_async_copy(tokens.at[rows], stage, load_sem)
            copy.start()
            copy.wait()

            def few(r, c):
                sub = pl.ds(pl.multiple_of(r * 64, 64), 64)
                there = pl.ds(pl.multiple_of(i * part + r * 64, 64), 64)
                inputs = stage[sub, :].astype(jnp.float32)
                centered = inputs - jnp.mean(inputs, 1, keepdims=True)
                inv_dev = lax.rsqrt(jnp.mean(centered * centered, 1, keepdims=True) + norm_eps)
                normed[there, :] = (
                    centered * inv_dev * vec_ref[NIN + 1 : NIN + 2, :] + vec_ref[NIN + 2 : NIN + 3, :]
                ).astype(jnp.bfloat16)
                lane = lax.broadcasted_iota(jnp.int32, (64, LANES), 1)
                stats[there, :] = jnp.where(lane == 0, jnp.mean(inputs, 1, keepdims=True), inv_dev)
                return c

            lax.fori_loop(0, part // 64, few, 0)

        def hidden_place(i):
            return i * HID // cols_all, pl.multiple_of(i * HID % cols_all, HID)

        def pack(u):
            s = u // 3

            def fetch(copies):
                for copy in copies:
                    copy.start()
                for copy in copies:
                    copy.wait()

            @pl.when(u % 3 == 1)
            def _():
                cols = pl.ds(pl.multiple_of(s * LANES, LANES), LANES)
                fetch(
                    [
                        pltpu.make_async_copy(
                            in_w.at[g, :, cols], raw_in.at[:, pl.ds(g * LANES, LANES)], pack_sem.at[g]
                        )
                        for g in range(3)
                    ]
                    + [pltpu.make_async_copy(out_w.at[0, cols], raw_out.at[pl.ds(0, LANES)], pack_sem.at[3])]
                )
                packed[:, :ATT] = raw_in[...].astype(jnp.bfloat16)
                packed[:, ATT:] = raw_out[:LANES, :].astype(jnp.bfloat16).T

            @pl.when(u % 3 != 1)
            def _():
                group, first = hidden_place(2 * s + (u % 3) // 2)
                cols = pl.ds(first, HID)
                fetch(
                    [
                        pltpu.make_async_copy(
                            in_w.at[3 + group, :, cols], raw_in.at[:, pl.ds(0, HID)], pack_sem.at[0]
                        ),
                        pltpu.make_async_copy(out_w.at[1 + group, cols], raw_out, pack_sem.at[1]),
                    ]
                )
                packed[:, :HID] = raw_in[:, :HID].astype(jnp.bfloat16)
                packed[:, HID:] = raw_out[...].astype(jnp.bfloat16).T

            copy = pltpu.make_async_copy(packed, full.at[u, z], load_sem)
            copy.start()
            copy.wait()

        def fetch_weights(u):
            return pltpu.make_async_copy(full.at[u], wbuf, weight_sem)

        def next_weights(u):
            @pl.when(u < units)
            def _():
                need(u)
                fetch_weights(u).start()

        def column_sums(split):
            ones = jnp.ones((8, rows_all), jnp.bfloat16)
            return dot(ones, x[:, :split])[0:1, :]

        def save(u):
            return pltpu.make_async_copy(x, saved.at[u], save_sem)

        def wait_saved(u):
            @pl.when(u > 0)
            def _():
                save(u - 1).wait()

        def gradients(u, split):
            @pl.when(u >= 2)
            def _():
                exchange(u - 2).wait_send()

            def one(j, carry):
                for core, place in ((k, None), (1 - k, outgoing)):
                    cols = pl.ds(pl.multiple_of(j * size + core * half, half), half)
                    into = dot(normed[:, cols], x[:, :split], TN)
                    outof = dot(cot[:, cols], x[:, split:], TN)
                    if place is None:
                        held[u % 3, j, :, :split] = into
                        held[u % 3, j, :, split:] = outof
                    else:
                        place[u % 2, j, :, :split] = into.astype(jnp.bfloat16)
                        place[u % 2, j, :, split:] = outof.astype(jnp.bfloat16)
                return carry

            lax.fori_loop(0, n, one, 0)
            exchange(u).start()

        block = min(512, rows_all)

        def hidden_unit(u, i_hidden, gather_from, gather_count):
            fetch_weights(u).wait()
            wait_saved(u)

            def one(i, carry):
                rows = pl.ds(pl.multiple_of(i * block, block), block)
                pre = dot(normed[rows, :], wbuf[:, :, :HID].reshape(width, HID)) + bias_ref[u][:, :HID]
                value, slope = gelu_both(pre)
                x[rows, HID:] = value.astype(jnp.bfloat16)
                grad = dot(cot[rows, :], wbuf[:, :, HID:].reshape(width, HID))
                x[rows, :HID] = (grad * slope).astype(jnp.bfloat16)
                return carry

            lax.fori_loop(0, rows_all // block, one, 0)
            save(u).start()
            scatter_from = (u - 1) * last
            ticks(gather_from, gather_count, scatter_from, last // 2)
            next_weights(u + 1)
            group, first = hidden_place(i_hidden)
            vec[pl.ds(3 + group, 1), pl.ds(first, HID)] = column_sums(HID)
            gradients(u, HID)
            ticks(0, 0, scatter_from + last // 2, last - last // 2)

        qblock = mask.shape[1]
        window = mask.shape[0]
        qblocks = rows_all // qblock

        def rope(v, rows, sign):
            half_rot = ROT // 2
            lane = lax.broadcasted_iota(jnp.int32, v.shape, 1) % HD
            ahead = pltpu.roll(v, LANES - half_rot, 1)
            behind = pltpu.roll(v, half_rot, 1)
            other = jnp.where(lane < half_rot, -ahead, behind)
            return v * cos_ref[rows, :] + other * (sign * sin_ref[rows, :])

        def recv_kv(s):
            rows = pl.ds(pl.multiple_of((1 - k) * rows_all, rows_all), rows_all)
            return pltpu.make_async_remote_copy(
                src_ref=kv.at[s, :, rows],
                dst_ref=kv.at[s, :, rows],
                send_sem=kvsend_sem.at[s],
                recv_sem=kvrecv_sem.at[s],
                device_id=other_core,
                device_id_type=MESH,
            )

        def send_dkv(s):
            return pltpu.make_async_remote_copy(
                src_ref=dkv.at[:, pl.ds(0, rows_all)],
                dst_ref=dkv_other.at[s],
                send_sem=dsend_sem.at[s],
                recv_sem=drecv_sem.at[s],
                device_id=other_core,
                device_id_type=MESH,
            )

        def attention_unit(u, s, gather_from, gather_count):
            fetch_weights(u).wait()
            wait_saved(u)

            @pl.when((s > 0) & (k == 1))
            def _():
                send_dkv(s - 1).wait_send()

            def project(i, carry):
                rows = pl.ds(pl.multiple_of(i * block, block), block)
                there = pl.ds(pl.multiple_of(k * rows_all + i * block, block), block)
                pre = dot(normed[rows, :], wbuf[:, :, :ATT].reshape(width, ATT)) + bias_ref[u][:, :ATT]
                grad = dot(cot[rows, :], wbuf[:, :, ATT:].reshape(width, LANES))
                g_s[rows, :] = grad.astype(jnp.bfloat16)
                query = rope(pre[:, :LANES], rows, 1.0).astype(jnp.bfloat16)
                q_s[rows, :] = query * jnp.bfloat16(HD**-0.5)
                kv[s, 0, there, :] = rope(pre[:, LANES : 2 * LANES], rows, 1.0).astype(jnp.bfloat16)
                kv[s, 1, there, :] = pre[:, 2 * LANES :].astype(jnp.bfloat16)
                return carry

            lax.fori_loop(0, rows_all // block, project, 0)
            send_kv(s).start()
            dkv[...] = jnp.zeros_like(dkv)
            scatter_from = (u - 1) * last
            per_block = gather_count // qblocks
            early = gather_count - per_block * qblocks
            ticks(gather_from, early, scatter_from, 0)
            recv_kv(s).wait_recv()

            def queries(b, carry):
                first_query = k * rows_all + b * qblock
                first_key = pl.multiple_of(jnp.maximum(first_query + qblock - window, 0), qblock)
                rows = pl.ds(pl.multiple_of(b * qblock, qblock), qblock)
                keys = pl.ds(first_key, window)
                key_at = first_key + lax.broadcasted_iota(jnp.int32, (window, qblock), 0)
                query_at = first_query + lax.broadcasted_iota(jnp.int32, (window, qblock), 1)
                begin = begin_ref[0:1, rows]
                mask[...] = jnp.where((key_at >= begin) & (key_at <= query_at), 0.0, -1e30)
                lane = lax.broadcasted_iota(jnp.int32, (qblock, LANES), 1)
                att = jnp.zeros((qblock, LANES), jnp.float32)
                dq = jnp.zeros((qblock, LANES), jnp.float32)
                for head in range(2):
                    inside = (lane >= head * HD) & (lane < (head + 1) * HD)
                    q_own = jnp.where(inside, q_s[rows, :], jnp.zeros((qblock, LANES), jnp.bfloat16))
                    g_own = jnp.where(inside, g_s[rows, :], jnp.zeros((qblock, LANES), jnp.bfloat16))
                    scores = dot(kv[s, 0, keys, :], q_own, NT) + mask[...]
                    weights = jnp.exp(scores - jnp.max(scores, 0, keepdims=True))
                    probs = weights * (1.0 / jnp.sum(weights, 0, keepdims=True))
                    probs_low = probs.astype(jnp.bfloat16)
                    grad_probs = dot(kv[s, 1, keys, :], g_own, NT)
                    inner = jnp.sum(probs * grad_probs, 0, keepdims=True)
                    grad_scores = (probs * (grad_probs - inner)).astype(jnp.bfloat16)
                    att = jnp.where(inside, dot(probs_low, kv[s, 1, keys, :], TN), att)
                    dq = jnp.where(inside, dot(grad_scores, kv[s, 0, keys, :], TN), dq)
                    dkv[1, keys, :] += dot(probs_low, g_own)
                    dkv[0, keys, :] += dot(grad_scores, q_own)
                x[rows, ATT:] = att.astype(jnp.bfloat16)
                x[rows, :LANES] = rope(dq * HD**-0.5, rows, -1.0).astype(jnp.bfloat16)
                low, high = b * last // qblocks, (b + 1) * last // qblocks
                ticks(gather_from + early + b * per_block, per_block, scatter_from + low, high - low)
                return carry

            lax.fori_loop(0, qblocks, queries, 0)

            @pl.when(k == 1)
            def _():
                send_dkv(s).start()

            @pl.when(k == 0)
            def _():
                send_dkv(s).wait_recv()
                copy = pltpu.make_async_copy(dkv_other.at[s], dkv_tmp, load_sem)
                copy.start()
                copy.wait()

            @pl.when(k == 1)
            def _():
                dkv_tmp[...] = jnp.zeros_like(dkv_tmp)

            def turn(i, carry):
                rows = pl.ds(pl.multiple_of(i * qblock, qblock), qblock)
                there = pl.ds(pl.multiple_of(k * rows_all + i * qblock, qblock), qblock)
                x[rows, LANES : 2 * LANES] = rope(
                    dkv[0, there, :] + dkv_tmp[0, rows, :], rows, -1.0
                ).astype(jnp.bfloat16)
                x[rows, 2 * LANES : ATT] = (dkv[1, there, :] + dkv_tmp[1, rows, :]).astype(jnp.bfloat16)
                return carry

            lax.fori_loop(0, qblocks, turn, 0)
            save(u).start()
            next_weights(u + 1)
            bias_grad = column_sums(ATT)
            for g in range(3):
                vec[g : g + 1, pl.ds(pl.multiple_of(s * LANES, LANES), LANES)] = bias_grad[
                    :, g * LANES : (g + 1) * LANES
                ]
            gradients(u, ATT)


        cot_copy = pltpu.make_async_copy(cot_hbm, cot, save_sem)
        cot_copy.start()
        per_step = 3 * last
        in_hidden = 2 * per_step // 9
        in_attention = per_step - 2 * in_hidden
        lead = max(last, 2 * last - in_hidden)
        norm_blocks = rows_all // stage.shape[0]
        pack(0)
        send_own(0)
        pack(1)

        def begin_step(i, carry):
            @pl.when(i + 2 < units)
            def _():
                pack(i + 2)

            @pl.when(i < norm_blocks)
            def _():
                normalize(i)

            @pl.when(i < lead)
            def _():
                gather_tick(i)

            return carry

        lax.fori_loop(0, max(units - 2, norm_blocks, lead), begin_step, 0)
        cot_copy.wait()
        next_weights(0)
        vec[...] = jnp.zeros_like(vec)
        vec[NIN : NIN + 1, :] = dot(jnp.ones((8, rows_all), jnp.bfloat16), cot[:, columns])[0:1, :]

        def super_step(s, carry):
            base = s * per_step + lead
            hidden_unit(3 * s, 2 * s, base, in_hidden)
            attention_unit(3 * s + 1, s, base + in_hidden, in_attention)
            hidden_unit(3 * s + 2, 2 * s + 1, base + in_hidden + in_attention, in_hidden)
            return carry

        lax.fori_loop(0, steps, super_step, 0)

        save(units - 1).wait()
        exchange(units - 2).wait_send()
        exchange(units - 1).wait_send()

        @pl.when(k == 1)
        def _():
            send_dkv(steps - 1).wait_send()


    def tensor_copy(what, i, source):
        return pltpu.make_async_remote_copy(
            src_ref=source,
            dst_ref=arrived.at[what, i],
            send_sem=tsend_sem.at[what, i],
            recv_sem=trecv_sem.at[what, i],
            device_id={"tensor": lax.rem(tensor + 1 + i, peers)},
            device_id_type=MESH,
        )

    def sums_copy(i):
        return pltpu.make_async_remote_copy(
            src_ref=sums,
            dst_ref=sums_in.at[i],
            send_sem=ssend_sem.at[i],
            recv_sem=srecv_sem.at[i],
            device_id={"tensor": lax.rem(tensor + 1 + i, peers)},
            device_id_type=MESH,
        )

    def finals(xs, tile, blocks, swap_in):
        part = size // 2
        tiles = 2 * peers

        def fetch_tile(q):
            shard = lax.rem(tensor + 1 + q // 2, peers)
            rows = pl.ds(pl.multiple_of(q % 2 * part, part), part)
            return pltpu.make_async_copy(full.at[:, shard, rows], tile.at[q % 2], tile_sem.at[q % 2])

        fetch_xs = pltpu.make_async_copy(saved, xs.at[pl.ds(0, units)], load_sem)
        fetch_xs.start()
        fetch_tile(0).start()
        fetch_xs.wait()
        block = min(512, rows_all)

        def products(q, store):
            @pl.when(q + 1 < tiles)
            def _():
                fetch_tile(q + 1).start()

            fetch_tile(q).wait()

            def one(r, carry):
                rows = pl.ds(pl.multiple_of(r * block, block), block)
                grads, branch = None, None
                for u in range(units):
                    split = ATT if u % 3 == 1 else HID
                    left = dot(xs[u, rows, :split], tile[q % 2, u, :, :split], NT)
                    right = dot(xs[u, rows, split:], tile[q % 2, u, :, split:], NT)
                    grads = left if grads is None else grads + left
                    branch = right if branch is None else branch + right
                store(r, 0, grads)
                store(r, 1, branch)
                return carry

            lax.fori_loop(0, rows_all // block, one, 0)

        scatter_from = (units - 1) * last
        scatter_count = last * (LAG + 1) + 1
        remote = 2 * (peers - 1)

        def remote_tile(q, carry):
            i, h = q // 2, q % 2

            def store(r, what, value):
                rows = pl.ds(pl.multiple_of(r * block, block), block)
                cols = pl.ds(pl.multiple_of(h * part, part), part)
                blocks[what, i, rows, cols] = value.astype(jnp.bfloat16)

            products(q, store)

            @pl.when(h == 1)
            def _():
                tensor_copy(0, i, blocks.at[0, i]).start()

            low, high = q * scatter_count // remote, (q + 1) * scatter_count // remote
            run_ticks(swap_in, 0, 0, scatter_from + low, high - low)
            return carry

        lax.fori_loop(0, remote, remote_tile, 0)

        def start_branch(i, carry):
            tensor_copy(1, i, blocks.at[1, i]).start()
            return carry

        lax.fori_loop(0, peers - 1, start_branch, 0)

        for h in range(2):

            def store(r, what, value):
                for a in range(block // half):
                    held[what, r * (block // half) + a, :, h * part : (h + 1) * part] = value[
                        a * half : (a + 1) * half
                    ]

            products(remote + h, store)

        tok_at, cot_at, out_at = 2 * (peers - 1), 2 * (peers - 1) + 1, 2 * (peers - 1) + 2
        bring = [
            pltpu.make_async_copy(tokens.at[:, columns], xs.at[tok_at, :, pl.ds(0, size)], tile_sem.at[0]),
            pltpu.make_async_copy(cot_hbm.at[:, columns], xs.at[cot_at, :, pl.ds(0, size)], tile_sem.at[1]),
        ]
        for copy in bring:
            copy.start()
        for copy in bring:
            copy.wait()

        def collect(what):
            def one(i, carry):
                tensor_copy(what, i, blocks.at[what, i]).wait_recv()
                copy = pltpu.make_async_copy(
                    arrived.at[what, i], xs.at[what * (peers - 1) + i, :, pl.ds(0, size)], load_sem
                )
                copy.start()
                copy.wait()
                return carry

            lax.fori_loop(0, peers - 1, one, 0)

        def summed(what, r, rows):
            value = held[what, r, :, :size]
            for i in range(peers - 1):
                value += xs[what * (peers - 1) + i, rows, :size].astype(jnp.float32)
            return value

        gain = vec_ref[NIN + 1 : NIN + 2, columns]
        ones = jnp.ones((8, size), jnp.float32)

        def unit_of(rows):
            token = xs[tok_at, rows, :size].astype(jnp.float32)
            return (token - stats[rows, 0:1]) * stats[rows, 1:2]

        collect(0)

        def first_pass(r, carry):
            rows = pl.ds(pl.multiple_of(r * half, half), half)
            grad = summed(0, r, rows)
            held[0, r, :, :size] = grad
            unit = unit_of(rows)
            scaled = grad * gain
            sums[0:8, rows] = lax.dot_general(
                ones, scaled, NT, precision=lax.Precision.HIGHEST, preferred_element_type=jnp.float32
            )
            sums[8:16, rows] = lax.dot_general(
                ones, scaled * unit, NT, precision=lax.Precision.HIGHEST, preferred_element_type=jnp.float32
            )
            vec[NIN + 1 : NIN + 2, :] += jnp.sum(grad * unit, 0, keepdims=True)
            vec[NIN + 2 : NIN + 3, :] += jnp.sum(grad, 0, keepdims=True)
            return carry

        lax.fori_loop(0, rows_all // half, first_pass, 0)
        for i in range(peers - 1):
            sums_copy(i).start()
        to_core = pltpu.make_async_remote_copy(
            src_ref=vec, dst_ref=vec_core, send_sem=vsend_sem.at[0], recv_sem=vrecv_sem.at[0],
            device_id=other_core, device_id_type=MESH,
        )
        to_core.start()
        for i in range(peers - 1):
            sums_copy(i).wait_recv()
        inv_width = 1.0 / width

        def second_pass(r, carry):
            rows = pl.ds(pl.multiple_of(r * half, half), half)
            means = sums[:, rows]
            for i in range(peers - 1):
                means += sums_in[i, :, rows]
            means = (means * inv_width).T
            unit = unit_of(rows)
            held[0, r, :, :size] = stats[rows, 1:2] * (
                held[0, r, :, :size] * gain - means[:, 0:1] - unit * means[:, 8:9]
            ) + xs[cot_at, rows, :size].astype(jnp.float32)
            return carry

        lax.fori_loop(0, rows_all // half, second_pass, 0)
        put_grad = pltpu.make_async_copy(held.at[0, :, :, pl.ds(0, size)], token_grad, out_sem.at[0])
        put_grad.start()

        to_core.wait_recv()
        vec_line[z] = vec[...] + vec_core[...]

        def along_dp(i):
            return pltpu.make_async_remote_copy(
                src_ref=vec_line.at[z], dst_ref=vec_line.at[z],
                send_sem=vsend_sem.at[1 + i], recv_sem=vrecv_sem.at[1 + i],
                device_id={"dp": lax.rem(z + 1 + i, n)}, device_id_type=MESH,
            )

        def from_dp(i):
            there = lax.rem(z + n - 1 - i, n)
            return pltpu.make_async_remote_copy(
                src_ref=vec_line.at[there], dst_ref=vec_line.at[there],
                send_sem=vsend_sem.at[1 + i], recv_sem=vrecv_sem.at[1 + i],
                device_id={"dp": lax.rem(z + 1 + i, n)}, device_id_type=MESH,
            )

        for i in range(n - 1):
            along_dp(i).start()
        for i in range(n - 1):
            from_dp(i).wait_recv()
        vec_sum = vec_line[0]
        for i in range(1, n):
            vec_sum += vec_line[i]
        vec_all[tensor] = vec_sum

        def along_tensor(i):
            return pltpu.make_async_remote_copy(
                src_ref=vec_all.at[tensor], dst_ref=vec_all.at[tensor],
                send_sem=vsend_sem.at[n + i], recv_sem=vrecv_sem.at[n + i],
                device_id={"tensor": lax.rem(tensor + 1 + i, peers)}, device_id_type=MESH,
            )

        def from_tensor(i):
            there = lax.rem(tensor + peers - 1 - i, peers)
            return pltpu.make_async_remote_copy(
                src_ref=vec_all.at[there], dst_ref=vec_all.at[there],
                send_sem=vsend_sem.at[n + i], recv_sem=vrecv_sem.at[n + i],
                device_id={"tensor": lax.rem(tensor + 1 + i, peers)}, device_id_type=MESH,
            )

        for i in range(peers - 1):
            along_tensor(i).start()

        collect(1)
        out_bias = vec_ref[NIN : NIN + 1, columns]

        def third_pass(r, carry):
            rows = pl.ds(pl.multiple_of(r * half, half), half)
            value = xs[tok_at, rows, :size].astype(jnp.float32) + (summed(1, r, rows) + out_bias)
            xs[out_at, rows, :size] = value.astype(jnp.bfloat16)
            return carry

        lax.fori_loop(0, rows_all // half, third_pass, 0)
        put_result = pltpu.make_async_copy(xs.at[out_at, :, pl.ds(0, size)], result, out_sem.at[1])
        put_result.start()

        for i in range(peers - 1):
            from_tensor(i).wait_recv()
        vec_grad[...] = vec_all[...]
        put_grad.wait()
        put_result.wait()
        to_core.wait_send()
        for i in range(n - 1):
            along_dp(i).wait_send()
        for i in range(peers - 1):
            along_tensor(i).wait_send()
            sums_copy(i).wait_send()
            tensor_copy(0, i, blocks.at[0, i]).wait_send()
            tensor_copy(1, i, blocks.at[1, i]).wait_send()

    low, wide = jnp.bfloat16, jnp.float32
    window, qblock = rows_all + min(256, rows_all), min(256, rows_all)
    pl.run_scoped(
        forward_backward,
        pltpu.VMEM((rows_all, width), low),
        pltpu.VMEM((rows_all, width), low),
        pltpu.VMEM((rows_all // 4, width), low),
        pltpu.VMEM((size, ATT), wide),
        pltpu.VMEM((HID, size), wide),
        pltpu.VMEM((size, WIDE), low),
        pltpu.VMEM((n, size, WIDE), low),
        pltpu.VMEM((rows_all, WIDE), low),
        pltpu.VMEM((rows_all, LANES), low),
        pltpu.VMEM((rows_all, LANES), low),
        pltpu.VMEM((2, 2 * rows_all, LANES), wide),
        pltpu.VMEM((2, rows_all, LANES), wide),
        pltpu.VMEM((window, qblock), wide),
        pltpu.VMEM((2, n, half, WIDE), low),
        pltpu.VMEM((n, half, WIDE), low),
    )
    pl.run_scoped(
        finals,
        pltpu.VMEM((max(units, 2 * peers + 1), rows_all, WIDE), low),
        pltpu.VMEM((2, units, size // 2, WIDE), low),
        pltpu.VMEM((2, peers - 1, rows_all, size), low),
        pltpu.VMEM((n, half, WIDE), low),
    )


    def drain_kv(s, carry):
        send_kv(s).wait_send()
        return carry

    lax.fori_loop(0, steps, drain_kv, 0)

    def drain(m, carry):
        g, s = m // last, m % last + 1

        @pl.when(s == 1)
        def _():
            @pl.when(z < last)
            def _():
                hop(0, g, 0, z).wait_send()

            @pl.when(z > 0)
            def _():
                hop(1, g, 0, z).wait_send()

            @pl.when(g >= units - (LAG + 3))
            def _():
                keep(g).wait()
                share(g, mine).wait_send()

            share(g, theirs).wait_recv()

        @pl.when(z >= s)
        def _():
            @pl.when(z < last)
            def _():
                hop(0, g, s, z - s).wait_send()

            across(0, g, s - 1, z - s, mine).wait_send()

        @pl.when(z + s <= last)
        def _():
            @pl.when(z > 0)
            def _():
                hop(1, g, s, z + s).wait_send()

            across(1, g, s - 1, z + s, mine).wait_send()

        for way in range(2):
            distance = z if way == 0 else last - z

            @pl.when(distance < last - (s - 1))
            def _():
                pass_on(way, g, s - 1).wait_send()

        return carry

    lax.fori_loop(0, units * last, drain, 0)


def run_block(in_weight, out_weight, tokens, cotangent, bias, vectors, cosine, sine, begin):
    n, peers = lax.axis_size("dp"), lax.axis_size("tensor")
    size, cols_all = in_weight.shape[1:]
    steps = cols_all // LANES
    units = 3 * steps
    half = size // 2
    rows, width = tokens.shape
    assert width == n * size == peers * cols_all and size == cols_all and rows == n * half
    low, wide = jnp.bfloat16, jnp.float32
    anywhere = pl.BlockSpec(memory_space=pl.ANY)
    vm = pl.BlockSpec(memory_space=pltpu.VMEM)
    dma = pltpu.SemaphoreType.DMA
    return pl.pallas_call(
        functools.partial(block_kernel, n, steps, peers),
        out_shape=(
            jax.ShapeDtypeStruct((units, n, size, WIDE), low),
            jax.ShapeDtypeStruct((units, rows, WIDE), low),
            jax.ShapeDtypeStruct((units, size, WIDE), wide),
            jax.ShapeDtypeStruct((units, n, half, WIDE), low),
            jax.ShapeDtypeStruct((steps, 2, rows, LANES), wide),
            jax.ShapeDtypeStruct((2, peers - 1, rows, size), low),
            jax.ShapeDtypeStruct((rows, size), low),
            jax.ShapeDtypeStruct((n, half, size), wide),
            jax.ShapeDtypeStruct((peers, 16, size), wide),
        ),
        in_specs=[anywhere] * 4 + [vm] * 5,
        out_specs=[anywhere] * 8 + [vm],
        scratch_shapes=[
            pltpu.VMEM((steps, 2, 2 * rows, LANES), low),
            pltpu.VMEM((3, n, half, WIDE), wide),
            pltpu.VMEM((units, n + 1, half, WIDE), low),
            pltpu.VMEM((LAG + 3, half, WIDE), wide),
            pltpu.VMEM((rows, LANES), wide),
            pltpu.VMEM((16, size), wide),
            pltpu.VMEM((16, size), wide),
            pltpu.VMEM((n, 16, size), wide),
            pltpu.VMEM((peers, 16, size), wide),
            pltpu.VMEM((16, rows), wide),
            pltpu.VMEM((peers - 1, 16, rows), wide),
            dma((2, units, n)),
            dma((2, units, n)),
            dma((2, units, n)),
            dma((2, units, n)),
            dma((units,)),
            dma((units,)),
            dma((2, units, n - 1)),
            dma((2, units, n - 1)),
            dma((units,)),
            dma((units,)),
            dma((units,)),
            dma((steps,)),
            dma((steps,)),
            dma((steps,)),
            dma((steps,)),
            dma,
            dma,
            dma,
            dma((4,)),
            dma((2, peers - 1)),
            dma((2, peers - 1)),
            dma((peers - 1,)),
            dma((peers - 1,)),
            dma((n + peers - 1,)),
            dma((n + peers - 1,)),
            dma((2,)),
            dma((2,)),
        ],
        compiler_params=pltpu.CompilerParams(
            collective_id=1, has_side_effects=True, vmem_limit_bytes=VMEM_LIMIT
        ),
        name="parallel_block",
    )(in_weight, out_weight, tokens, cotangent, bias, vectors, cosine, sine, begin)


def adam_kernel(turned, total, w, m, v, new_w, new_m, new_v):
    gradient = total[0].T if turned else total[0]
    new_w[0], new_m[0], new_v[0] = adamw(w[0], gradient, m[0], v[0], rate_matrix, weight_decay)


def adam_weights(turned, total, weight, first, second):
    groups, cols_all = weight.shape[0], weight.shape[1 if turned else 2]
    size = total.shape[1]
    lead = 1 if turned else 3

    def place(g, c):
        i = ((g - lead) * cols_all + c * LANES) // HID
        unit = jnp.where(g < lead, 3 * c + 1, 3 * (i // 2) + 2 * (i % 2))
        lane = jnp.where(g < lead, 3 if turned else g, c % 2 + (2 if turned else 0))
        return unit, 0, lane

    if turned:
        spec = pl.BlockSpec((1, LANES, size), lambda g, c: (g, c, 0))
    else:
        spec = pl.BlockSpec((1, size, LANES), lambda g, c: (g, 0, c))
    return pl.pallas_call(
        functools.partial(adam_kernel, turned),
        grid=(groups, cols_all // LANES),
        out_shape=tuple(jax.ShapeDtypeStruct(weight.shape, jnp.float32) for _ in range(3)),
        in_specs=[pl.BlockSpec((1, size, LANES), place)] + [spec] * 3,
        out_specs=[spec] * 3,
        compiler_params=pltpu.CompilerParams(vmem_limit_bytes=VMEM_LIMIT),
        name="adam_out" if turned else "adam_in",
    )(total, weight, first, second)


def layout(lengths_row, row_span):
    seg_ends = jnp.cumsum(lengths_row)
    seg_starts = seg_ends - lengths_row
    places = jnp.arange(row_span, dtype=jnp.int32)
    segment = jnp.sum((places[:, None] >= seg_ends[None, :]).astype(jnp.int32), 1)
    numbers = jnp.arange(lengths_row.shape[0], dtype=jnp.int32)
    return jnp.sum(jnp.where(segment[:, None] == numbers[None, :], seg_starts[None, :], 0), 1)


def rope_tables(places):
    half_rot = ROT // 2
    lane = jnp.arange(2 * HD, dtype=jnp.int32) % HD
    exponent = (lane % half_rot).astype(jnp.float32)
    frequency = 10000.0 ** (-2.0 * exponent / ROT)
    angles = places.astype(jnp.float32)[:, None] * frequency[None, :]
    turned = (lane < ROT)[None, :]
    cosine = jnp.where(turned, jnp.cos(angles), 1.0)
    sine = jnp.where(turned, jnp.sin(angles), 0.0)
    return cosine, sine


def body(
    tokens,
    cotangent,
    lengths,
    in_weight,
    out_weight,
    vectors,
    in_first,
    in_second,
    out_first,
    out_second,
    vec_first,
    vec_second,
):
    local_rows, model_width = tokens.shape
    slice_width = in_weight.shape[2]
    context_count = lax.axis_size("context")
    context_index = lax.axis_index("context")
    tensor_index = lax.axis_index("tensor")
    row_span = local_rows * context_count
    first_row = context_index * local_rows
    begin_all = layout(lengths[0], row_span)
    begin = lax.dynamic_slice_in_dim(begin_all, first_row, local_rows, 0)
    places = first_row + jnp.arange(local_rows, dtype=jnp.int32) - begin
    tables = rope_tables(places)

    column = tensor_index * slice_width
    in_bias = lax.dynamic_slice_in_dim(vectors[:NIN], column, slice_width, 1)
    steps = slice_width // LANES
    hid_bias = in_bias[3:].reshape(steps, 2, HID)
    att_bias = in_bias[:3].reshape(3, steps, LANES).transpose(1, 0, 2).reshape(steps, ATT)
    bias = jnp.stack(
        [
            jnp.pad(hid_bias[:, 0], ((0, 0), (0, WIDE - HID))),
            jnp.pad(att_bias, ((0, 0), (0, WIDE - ATT))),
            jnp.pad(hid_bias[:, 1], ((0, 0), (0, WIDE - HID))),
        ],
        1,
    ).reshape(3 * steps, 1, WIDE)
    by_group = jnp.transpose(in_weight, (1, 0, 2))
    _, _, total, _, _, _, result, token_grad, vec_grad = run_block(
        by_group, out_weight, tokens, cotangent, bias, vectors, tables[0], tables[1], begin[None]
    )
    token_grad = token_grad.reshape(local_rows, slice_width)
    vector_grad = jnp.transpose(vec_grad, (1, 0, 2)).reshape(-1, model_width)[: NIN + 3]
    new_vectors, new_vec_first, new_vec_second = adamw(
        vectors, vector_grad, vec_first, vec_second, rate_vector, 0.0
    )
    new_in, new_in_first, new_in_second = (
        jnp.transpose(v, (1, 0, 2))
        for v in adam_weights(
            False, total, by_group, jnp.transpose(in_first, (1, 0, 2)), jnp.transpose(in_second, (1, 0, 2))
        )
    )
    new_out, new_out_first, new_out_second = adam_weights(
        True, total, out_weight, out_first, out_second
    )
    return (
        result,
        token_grad,
        new_in,
        new_in_first,
        new_in_second,
        new_out,
        new_out_first,
        new_out_second,
        new_vectors,
        new_vec_first,
        new_vec_second,
    )


def solution(mesh):
    return jax.shard_map(
        body,
        mesh=mesh,
        in_specs=(
            P(("dp", "context"), None),
            P(("dp", "context"), None),
            P("dp", None),
            P("dp", None, "tensor"),
            P(None, "tensor", "dp"),
            P(),
            P("dp", None, "tensor"),
            P("dp", None, "tensor"),
            P(None, "tensor", "dp"),
            P(None, "tensor", "dp"),
            P(),
            P(),
        ),
        out_specs=(
            P(("dp", "context"), "tensor"),
            P(("dp", "context"), "tensor"),
            P("dp", None, "tensor"),
            P("dp", None, "tensor"),
            P("dp", None, "tensor"),
            P(None, "tensor", "dp"),
            P(None, "tensor", "dp"),
            P(None, "tensor", "dp"),
            P(),
            P(),
            P(),
        ),
        check_vma=False,
    )
```

```python
import functools

import jax
import jax.numpy as jnp
from jax import lax
from jax.experimental import pallas as pl
from jax.experimental.pallas import tpu as pltpu
from jax.sharding import PartitionSpec as P

HD = 64
ROT = 32
STEP = 10
NIN = 7
MESH = pl.DeviceIdType.MESH
VMEM_LIMIT = 60 * 2**20

norm_eps = 1e-05
beta_one = 0.9
beta_two = 0.95
adam_eps = 1e-08
weight_decay = 0.1
rate_matrix = 0.02
rate_vector = 0.4


def adamw(master, gradient, moment_one, moment_two, step_rate, decay_rate):
    first_new = beta_one * moment_one + (1.0 - beta_one) * gradient
    second_new = beta_two * moment_two + (1.0 - beta_two) * gradient * gradient
    first_hat = first_new / (1.0 - beta_one**STEP)
    second_hat = second_new / (1.0 - beta_two**STEP)
    updated = master - step_rate * (
        first_hat / (jnp.sqrt(second_hat) + adam_eps) + decay_rate * master
    )
    return (updated, first_new, second_new)


LANES = 2 * HD
WIDE = 4 * LANES
HID = WIDE // 2
ATT = 3 * LANES
LAG = 3

NT = (((1,), (1,)), ((), ()))
NN = (((1,), (0,)), ((), ()))
TN = (((0,), (0,)), ((), ()))


def dot(x, y, dims=NN):
    return lax.dot_general(x, y, dims, preferred_element_type=jnp.float32)


def greet(n, peers):
    z = lax.axis_index("dp")
    k = lax.axis_index("context")
    t = lax.axis_index("tensor")
    barrier = pltpu.get_barrier_semaphore()
    pl.semaphore_signal(barrier, inc=1, device_id={"context": 1 - k}, device_id_type=MESH)
    for i in range(1, n):
        pl.semaphore_signal(barrier, inc=1, device_id={"dp": lax.rem(z + i, n)}, device_id_type=MESH)
    for i in range(1, peers):
        pl.semaphore_signal(
            barrier, inc=1, device_id={"tensor": lax.rem(t + i, peers)}, device_id_type=MESH
        )
    pl.semaphore_wait(barrier, n + peers - 1)


def gelu_both(v):
    rate = 0.7978845608028654
    t = jnp.tanh(rate * (v + 0.044715 * (v * v * v)))
    value = 0.5 * v * (1.0 + t)
    slope = 0.5 * (1.0 + t) + 0.5 * v * (1.0 - t * t) * (rate * (1.0 + 3.0 * 0.044715 * (v * v)))
    return value, slope


def schedule(n):
    last = n - 1
    per_step = 3 * last
    in_hidden = 2 * per_step // 9
    in_attention = per_step - 2 * in_hidden
    done = (in_hidden, in_hidden + in_attention, per_step)
    lead = max([last * (n + i) - done[i] for i in range(3)] + [last * (n - 1)])
    behind = max(done[i] - last * i for i in range(3))
    depth = 3
    while any(done[i] - behind < last * (i - depth) + LAG * (n - 2) + 1 for i in range(3)):
        depth += 1
    return per_step, in_hidden, in_attention, lead, behind, depth


def block_kernel(
    n, steps, peers,
    in_w, out_w, tokens, cot_hbm, bias_ref, vec_ref, cos_ref, sin_ref, begin_ref,
    full, saved, total, swap, dkv_other, arrived, result, token_grad, vec_grad,
    kv, held, line, outbox, stats, vec, vec_core, vec_line, vec_all, sums, sums_in,
    send_sem, recv_sem, psend_sem, precv_sem,
    xsend_sem, xrecv_sem, lsend_sem, lrecv_sem, keep_sem, fsend_sem, frecv_sem,
    kvsend_sem, kvrecv_sem, dsend_sem, drecv_sem, load_sem, save_sem, weight_sem, pack_sem, put_sem, rows_sem, swap_sem,
    tsend_sem, trecv_sem, ssend_sem, srecv_sem, vsend_sem, vrecv_sem, tile_sem, out_sem,
):
    units = 3 * steps
    last = n - 1
    per_step, in_hidden, in_attention, lead, behind, depth = schedule(n)
    size, cols_all = in_w.shape[1], in_w.shape[2]
    half = size // 2
    rows_all, width = tokens.shape
    tensor = lax.axis_index("tensor")
    columns = pl.ds(pl.multiple_of(tensor * size, size), size)
    z = lax.axis_index("dp")
    k = lax.axis_index("context")
    mine = pl.ds(pl.multiple_of(k * half, half), half)
    theirs = pl.ds(pl.multiple_of((1 - k) * half, half), half)
    other_core = {"context": 1 - k}
    greet(n, peers)


    def hop(way, g, h, shard):
        return pltpu.make_async_remote_copy(
            src_ref=full.at[g, shard, mine],
            dst_ref=full.at[g, shard, mine],
            send_sem=send_sem.at[way, g, h],
            recv_sem=recv_sem.at[way, g, h],
            device_id={"dp": z + 1 - 2 * way},
            device_id_type=MESH,
        )

    def across(way, g, h, shard, rows):
        return pltpu.make_async_remote_copy(
            src_ref=full.at[g, shard, rows],
            dst_ref=full.at[g, shard, rows],
            send_sem=psend_sem.at[way, g, h],
            recv_sem=precv_sem.at[way, g, h],
            device_id=other_core,
            device_id_type=MESH,
        )

    def send_own(g):
        @pl.when(z < last)
        def _():
            hop(0, g, 0, z).start()

        @pl.when(z > 0)
        def _():
            hop(1, g, 0, z).start()

    def gather_tick(m):
        s = m % last + 1
        g = m // last - (s - 1)

        @pl.when((s == 1) & (g < units - 1))
        def _():
            send_own(g + 1)

        @pl.when((g >= 0) & (g < units))
        def _():
            @pl.when(z >= s)
            def _():
                hop(0, g, s - 1, z - s).wait_recv()

                @pl.when(z < last)
                def _():
                    hop(0, g, s, z - s).start()

                across(0, g, s - 1, z - s, mine).start()

            @pl.when(z + s <= last)
            def _():
                hop(1, g, s - 1, z + s).wait_recv()

                @pl.when(z > 0)
                def _():
                    hop(1, g, s, z + s).start()

                across(1, g, s - 1, z + s, mine).start()

    def need(u):
        def one(i, carry):
            s = i + 1

            @pl.when(z >= s)
            def _():
                across(0, u, s - 1, z - s, theirs).wait_recv()

            @pl.when(z + s <= last)
            def _():
                across(1, u, s - 1, z + s, theirs).wait_recv()

            return carry

        lax.fori_loop(0, last, one, 0)

    def send_kv(s):
        rows = pl.ds(pl.multiple_of(k * rows_all, rows_all), rows_all)
        return pltpu.make_async_remote_copy(
            src_ref=kv.at[s, :, rows],
            dst_ref=kv.at[s, :, rows],
            send_sem=kvsend_sem.at[s],
            recv_sem=kvrecv_sem.at[s],
            device_id=other_core,
            device_id_type=MESH,
        )


    def exchange_from(outgoing, g):
        return pltpu.make_async_remote_copy(
            src_ref=outgoing,
            dst_ref=swap.at[g],
            send_sem=xsend_sem.at[g],
            recv_sem=xrecv_sem.at[g],
            device_id=other_core,
            device_id_type=MESH,
        )

    def slot_of(way, i):
        return i if way == 0 else n - i

    def pass_on(way, g, i):
        slot = slot_of(way, i)
        return pltpu.make_async_remote_copy(
            src_ref=line.at[g, slot],
            dst_ref=line.at[g, slot],
            send_sem=lsend_sem.at[way, g, i],
            recv_sem=lrecv_sem.at[way, g, i],
            device_id={"dp": z + 1 - 2 * way},
            device_id_type=MESH,
        )

    def keep(g):
        return pltpu.make_async_copy(outbox.at[g % (LAG + 2)], total.at[g, mine], keep_sem.at[g])

    def share(g, rows):
        return pltpu.make_async_remote_copy(
            src_ref=outbox.at[g % (LAG + 2)],
            dst_ref=total.at[g, rows],
            send_sem=fsend_sem.at[g],
            recv_sem=frecv_sem.at[g],
            device_id=other_core,
            device_id_type=MESH,
        )

    def fetch_swapped(g, swap_in):
        @pl.when(g >= 0)
        def _():
            exchange_from(swap_in, g).wait_recv()
            pltpu.make_async_copy(swap.at[g], swap_in, swap_sem).start()

    def prepare(g, swap_in):
        pltpu.make_async_copy(swap.at[g], swap_in, swap_sem).wait()
        box = g % (LAG + 2)

        @pl.when(g >= LAG + 2)
        def _():
            keep(g - (LAG + 2)).wait()
            share(g - (LAG + 2), mine).wait_send()

        def one(j, carry):
            held[g % depth, j] += swap_in[j].astype(jnp.float32)
            return carry

        lax.fori_loop(0, n, one, 0)
        outbox[box] = held[g % depth, z]

    def scatter_step(way, m, distance):
        @pl.when((m >= 0) & (m < units * last))
        def _():
            g, i = m // last, m % last
            shard = n - 1 - i if way == 0 else i
            slot = slot_of(way, i)

            @pl.when(distance == 0)
            def _():
                line[g, slot] = held[g % depth, shard].astype(jnp.bfloat16)
                pass_on(way, g, i).start()

            @pl.when((distance > 0) & (distance <= last - i))
            def _():
                pass_on(way, g, i).wait_recv()

                @pl.when(distance < last - i)
                def _():
                    line[g, slot] = (line[g, slot].astype(jnp.float32) + held[g % depth, shard]).astype(
                        jnp.bfloat16
                    )
                    pass_on(way, g, i).start()

    def finish(g):
        box = g % (LAG + 2)

        @pl.when(z > 0)
        def _():
            outbox[box] += line[g, slot_of(0, n - 1 - z)].astype(jnp.float32)

        @pl.when(z < last)
        def _():
            outbox[box] += line[g, slot_of(1, z)].astype(jnp.float32)

        keep(g).start()
        share(g, mine).start()

    def scatter_tick(t, swap_in):
        @pl.when((t >= 0) & (t % last == 0) & (t < units * last))
        def _():
            prepare(t // last, swap_in)

        scatter_step(0, t - LAG * z, z)
        scatter_step(1, t - LAG * (last - z), last - z)
        done = t - last * LAG

        @pl.when((done >= 0) & (done % last == 0))
        def _():
            finish(done // last)

    def run_ticks(swap_in, gather_from, gather_count, scatter_from, scatter_count):
        def one_gather(i, carry):
            gather_tick(gather_from + i)
            return carry

        def one_scatter(i, carry):
            scatter_tick(scatter_from + i, swap_in)
            return carry

        lax.fori_loop(0, gather_count, one_gather, 0)
        lax.fori_loop(0, scatter_count, one_scatter, 0)

    def forward_backward(
        normed, cot, stage, raw_in, raw_out, packed, wbuf, x, q_s, g_s, dkv, dkv_tmp, mask, outgoing, swap_in
    ):

        def exchange(g):
            return exchange_from(outgoing.at[g % 2], g)

        def ticks(gather_from, gather_count, scatter_from, scatter_count):
            run_ticks(swap_in, gather_from, gather_count, scatter_from, scatter_count)

        part = stage.shape[1]
        norm_blocks = rows_all // part

        def fetch_rows(i):
            rows = pl.ds(pl.multiple_of(i * part, part), part)
            return pltpu.make_async_copy(tokens.at[rows], stage.at[i % 2], rows_sem.at[i % 2])

        def normalize(i):
            @pl.when(i + 1 < norm_blocks)
            def _():
                fetch_rows(i + 1).start()

            fetch_rows(i).wait()

            def few(r, c):
                sub = pl.ds(pl.multiple_of(r * 64, 64), 64)
                there = pl.ds(pl.multiple_of(i * part + r * 64, 64), 64)
                inputs = stage[i % 2, sub, :].astype(jnp.float32)
                centered = inputs - jnp.mean(inputs, 1, keepdims=True)
                inv_dev = lax.rsqrt(jnp.mean(centered * centered, 1, keepdims=True) + norm_eps)
                normed[there, :] = (
                    centered * inv_dev * vec_ref[NIN + 1 : NIN + 2, :] + vec_ref[NIN + 2 : NIN + 3, :]
                ).astype(jnp.bfloat16)
                lane = lax.broadcasted_iota(jnp.int32, (64, LANES), 1)
                stats[there, :] = jnp.where(lane == 0, jnp.mean(inputs, 1, keepdims=True), inv_dev)
                return c

            lax.fori_loop(0, part // 64, few, 0)

        def hidden_place(i):
            return i * HID // cols_all, pl.multiple_of(i * HID % cols_all, HID)

        def fetch_raw(u, start):
            s, slot = u // 3, u % 2

            def each(copies):
                for copy in copies:
                    copy.start() if start else copy.wait()

            @pl.when(u % 3 == 1)
            def _():
                cols = pl.ds(pl.multiple_of(s * LANES, LANES), LANES)
                each(
                    [
                        pltpu.make_async_copy(
                            in_w.at[g, :, cols],
                            raw_in.at[slot, :, pl.ds(g * LANES, LANES)],
                            pack_sem.at[slot, g],
                        )
                        for g in range(3)
                    ]
                    + [
                        pltpu.make_async_copy(
                            out_w.at[0, cols], raw_out.at[slot, pl.ds(0, LANES)], pack_sem.at[slot, 3]
                        )
                    ]
                )

            @pl.when(u % 3 != 1)
            def _():
                group, first = hidden_place(2 * s + (u % 3) // 2)
                cols = pl.ds(first, HID)
                each(
                    [
                        pltpu.make_async_copy(
                            in_w.at[3 + group, :, cols],
                            raw_in.at[slot, :, pl.ds(0, HID)],
                            pack_sem.at[slot, 0],
                        ),
                        pltpu.make_async_copy(out_w.at[1 + group, cols], raw_out.at[slot], pack_sem.at[slot, 1]),
                    ]
                )

        def put_packed(u):
            return pltpu.make_async_copy(packed.at[u % 2], full.at[u, z], put_sem.at[u % 2])

        def pack(u):
            slot = u % 2
            fetch_raw(u, False)

            @pl.when(u % 3 == 1)
            def _():
                packed[slot, :, :ATT] = raw_in[slot].astype(jnp.bfloat16)
                packed[slot, :, ATT:] = raw_out[slot, :LANES, :].astype(jnp.bfloat16).T

            @pl.when(u % 3 != 1)
            def _():
                packed[slot, :, :HID] = raw_in[slot, :, :HID].astype(jnp.bfloat16)
                packed[slot, :, HID:] = raw_out[slot].astype(jnp.bfloat16).T

            put_packed(u).start()

        def fetch_weights(u):
            return pltpu.make_async_copy(full.at[u], wbuf, weight_sem)

        def next_weights(u):
            @pl.when(u < units)
            def _():
                need(u)
                fetch_weights(u).start()

        def column_sums(split):
            ones = jnp.ones((8, rows_all), jnp.bfloat16)
            return dot(ones, x[:, :split])[0:1, :]

        def save(u):
            return pltpu.make_async_copy(x, saved.at[u], save_sem)

        def wait_saved(u):
            @pl.when(u > 0)
            def _():
                save(u - 1).wait()

        def gradients(u, split):
            @pl.when(u >= 2)
            def _():
                exchange(u - 2).wait_send()

            def one(j, carry):
                for core, place in ((k, None), (1 - k, outgoing)):
                    cols = pl.ds(pl.multiple_of(j * size + core * half, half), half)
                    into = dot(normed[:, cols], x[:, :split], TN)
                    outof = dot(cot[:, cols], x[:, split:], TN)
                    if place is None:
                        held[u % depth, j, :, :split] = into
                        held[u % depth, j, :, split:] = outof
                    else:
                        place[u % 2, j, :, :split] = into.astype(jnp.bfloat16)
                        place[u % 2, j, :, split:] = outof.astype(jnp.bfloat16)
                return carry

            lax.fori_loop(0, n, one, 0)
            exchange(u).start()

        block = min(512, rows_all)

        def hidden_unit(u, i_hidden, at):
            fetch_weights(u).wait()
            wait_saved(u)

            def one(i, carry):
                rows = pl.ds(pl.multiple_of(i * block, block), block)
                pre = dot(normed[rows, :], wbuf[:, :, :HID].reshape(width, HID)) + bias_ref[u][:, :HID]
                value, slope = gelu_both(pre)
                x[rows, HID:] = value.astype(jnp.bfloat16)
                grad = dot(cot[rows, :], wbuf[:, :, HID:].reshape(width, HID))
                x[rows, :HID] = (grad * slope).astype(jnp.bfloat16)
                return carry

            lax.fori_loop(0, rows_all // block, one, 0)
            save(u).start()
            fetch_swapped(u - 1, swap_in)
            ticks(at + lead, in_hidden, at - behind, in_hidden)
            next_weights(u + 1)
            group, first = hidden_place(i_hidden)
            vec[pl.ds(3 + group, 1), pl.ds(first, HID)] = column_sums(HID)
            gradients(u, HID)

        qblock = mask.shape[1]
        window = mask.shape[0]
        qblocks = rows_all // qblock

        def rope(v, rows, sign):
            half_rot = ROT // 2
            lane = lax.broadcasted_iota(jnp.int32, v.shape, 1) % HD
            ahead = pltpu.roll(v, LANES - half_rot, 1)
            behind = pltpu.roll(v, half_rot, 1)
            other = jnp.where(lane < half_rot, -ahead, behind)
            return v * cos_ref[rows, :] + other * (sign * sin_ref[rows, :])

        def recv_kv(s):
            rows = pl.ds(pl.multiple_of((1 - k) * rows_all, rows_all), rows_all)
            return pltpu.make_async_remote_copy(
                src_ref=kv.at[s, :, rows],
                dst_ref=kv.at[s, :, rows],
                send_sem=kvsend_sem.at[s],
                recv_sem=kvrecv_sem.at[s],
                device_id=other_core,
                device_id_type=MESH,
            )

        def send_dkv(s):
            return pltpu.make_async_remote_copy(
                src_ref=dkv.at[:, pl.ds(0, rows_all)],
                dst_ref=dkv_other.at[s],
                send_sem=dsend_sem.at[s],
                recv_sem=drecv_sem.at[s],
                device_id=other_core,
                device_id_type=MESH,
            )

        def attention_unit(u, s, at):
            fetch_weights(u).wait()
            wait_saved(u)

            @pl.when((s > 0) & (k == 1))
            def _():
                send_dkv(s - 1).wait_send()

            def project(i, carry):
                rows = pl.ds(pl.multiple_of(i * block, block), block)
                there = pl.ds(pl.multiple_of(k * rows_all + i * block, block), block)
                pre = dot(normed[rows, :], wbuf[:, :, :ATT].reshape(width, ATT)) + bias_ref[u][:, :ATT]
                grad = dot(cot[rows, :], wbuf[:, :, ATT:].reshape(width, LANES))
                g_s[rows, :] = grad.astype(jnp.bfloat16)
                query = rope(pre[:, :LANES], rows, 1.0).astype(jnp.bfloat16)
                q_s[rows, :] = query * jnp.bfloat16(HD**-0.5)
                kv[s, 0, there, :] = rope(pre[:, LANES : 2 * LANES], rows, 1.0).astype(jnp.bfloat16)
                kv[s, 1, there, :] = pre[:, 2 * LANES :].astype(jnp.bfloat16)
                return carry

            lax.fori_loop(0, rows_all // block, project, 0)
            send_kv(s).start()
            dkv[...] = jnp.zeros_like(dkv)
            per_block = in_attention // qblocks
            early = in_attention - per_block * qblocks
            fetch_swapped(u - 1, swap_in)
            ticks(at + lead, early, at - behind, early)
            recv_kv(s).wait_recv()

            def queries(b, carry):
                first_query = k * rows_all + b * qblock
                first_key = pl.multiple_of(jnp.maximum(first_query + qblock - window, 0), qblock)
                rows = pl.ds(pl.multiple_of(b * qblock, qblock), qblock)
                keys = pl.ds(first_key, window)
                key_at = first_key + lax.broadcasted_iota(jnp.int32, (window, qblock), 0)
                query_at = first_query + lax.broadcasted_iota(jnp.int32, (window, qblock), 1)
                begin = begin_ref[0:1, rows]
                mask[...] = jnp.where((key_at >= begin) & (key_at <= query_at), 0.0, -1e30)
                lane = lax.broadcasted_iota(jnp.int32, (qblock, LANES), 1)
                att = jnp.zeros((qblock, LANES), jnp.float32)
                dq = jnp.zeros((qblock, LANES), jnp.float32)
                for head in range(2):
                    inside = (lane >= head * HD) & (lane < (head + 1) * HD)
                    q_own = jnp.where(inside, q_s[rows, :], jnp.zeros((qblock, LANES), jnp.bfloat16))
                    g_own = jnp.where(inside, g_s[rows, :], jnp.zeros((qblock, LANES), jnp.bfloat16))
                    scores = dot(kv[s, 0, keys, :], q_own, NT) + mask[...]
                    weights = jnp.exp(scores - jnp.max(scores, 0, keepdims=True))
                    probs = weights * (1.0 / jnp.sum(weights, 0, keepdims=True))
                    probs_low = probs.astype(jnp.bfloat16)
                    grad_probs = dot(kv[s, 1, keys, :], g_own, NT)
                    inner = jnp.sum(probs * grad_probs, 0, keepdims=True)
                    grad_scores = (probs * (grad_probs - inner)).astype(jnp.bfloat16)
                    att = jnp.where(inside, dot(probs_low, kv[s, 1, keys, :], TN), att)
                    dq = jnp.where(inside, dot(grad_scores, kv[s, 0, keys, :], TN), dq)
                    dkv[1, keys, :] += dot(probs_low, g_own)
                    dkv[0, keys, :] += dot(grad_scores, q_own)
                x[rows, ATT:] = att.astype(jnp.bfloat16)
                x[rows, :LANES] = rope(dq * HD**-0.5, rows, -1.0).astype(jnp.bfloat16)
                there = at + early + b * per_block
                ticks(there + lead, per_block, there - behind, per_block)
                return carry

            lax.fori_loop(0, qblocks, queries, 0)

            @pl.when(k == 1)
            def _():
                send_dkv(s).start()

            @pl.when(k == 0)
            def _():
                send_dkv(s).wait_recv()
                copy = pltpu.make_async_copy(dkv_other.at[s], dkv_tmp, load_sem)
                copy.start()
                copy.wait()

            @pl.when(k == 1)
            def _():
                dkv_tmp[...] = jnp.zeros_like(dkv_tmp)

            def turn(i, carry):
                rows = pl.ds(pl.multiple_of(i * qblock, qblock), qblock)
                there = pl.ds(pl.multiple_of(k * rows_all + i * qblock, qblock), qblock)
                x[rows, LANES : 2 * LANES] = rope(
                    dkv[0, there, :] + dkv_tmp[0, rows, :], rows, -1.0
                ).astype(jnp.bfloat16)
                x[rows, 2 * LANES : ATT] = (dkv[1, there, :] + dkv_tmp[1, rows, :]).astype(jnp.bfloat16)
                return carry

            lax.fori_loop(0, qblocks, turn, 0)
            save(u).start()
            next_weights(u + 1)
            bias_grad = column_sums(ATT)
            for g in range(3):
                vec[g : g + 1, pl.ds(pl.multiple_of(s * LANES, LANES), LANES)] = bias_grad[
                    :, g * LANES : (g + 1) * LANES
                ]
            gradients(u, ATT)


        cot_copy = pltpu.make_async_copy(cot_hbm, cot, save_sem)
        cot_copy.start()
        fetch_rows(0).start()
        fetch_raw(0, True)
        fetch_raw(1, True)
        for u in range(2):
            pack(u)
            put_packed(u).wait()
            if u == 0:
                send_own(0)
            fetch_raw(u + 2, True)

        def begin_step(i, carry):
            @pl.when(i + 2 < units)
            def _():
                pack(i + 2)

            @pl.when(i < norm_blocks)
            def _():
                normalize(i)

            @pl.when(i + 2 < units)
            def _():
                put_packed(i + 2).wait()

            @pl.when(i + 4 < units)
            def _():
                fetch_raw(i + 4, True)

            @pl.when(i < lead)
            def _():
                gather_tick(i)

            return carry

        lax.fori_loop(0, max(units - 2, norm_blocks, lead), begin_step, 0)
        cot_copy.wait()
        next_weights(0)
        vec[...] = jnp.zeros_like(vec)
        vec[NIN : NIN + 1, :] = dot(jnp.ones((8, rows_all), jnp.bfloat16), cot[:, columns])[0:1, :]

        def super_step(s, carry):
            at = s * per_step
            hidden_unit(3 * s, 2 * s, at)
            attention_unit(3 * s + 1, s, at + in_hidden)
            hidden_unit(3 * s + 2, 2 * s + 1, at + in_hidden + in_attention)
            return carry

        lax.fori_loop(0, steps, super_step, 0)

        save(units - 1).wait()
        exchange(units - 2).wait_send()
        exchange(units - 1).wait_send()

        @pl.when(k == 1)
        def _():
            send_dkv(steps - 1).wait_send()


    square = peers == 4
    upper, lower = pl.ds(0, rows_all // 2), pl.ds(rows_all // 2, rows_all // 2)

    def beside(axis):
        return tensor + 1 - 2 * (tensor % 2) if axis == 0 else tensor + 2 - 4 * (tensor // 2)

    def block_at(i):
        if not square:
            return lax.rem(tensor + 1 + i, peers)
        return jnp.where(
            i == 0, 3 - tensor, jnp.where(i == 1, beside(0), jnp.where(i == 2, beside(1), tensor))
        )

    def tensor_copy(blocks, what, message):
        if square:
            slot, rows, axis = ((0, upper, 0), (0, lower, 1), (1, upper, 0), (2, lower, 1), (1, lower, 0), (2, upper, 1))[
                message
            ]
            source, there = blocks.at[what, slot, rows], arrived.at[what, slot, rows]
            target = beside(axis)
        else:
            source, there = blocks.at[what, message], arrived.at[what, message]
            target = block_at(message)
        return pltpu.make_async_remote_copy(
            src_ref=source,
            dst_ref=there,
            send_sem=tsend_sem.at[what, message],
            recv_sem=trecv_sem.at[what, message],
            device_id={"tensor": target},
            device_id_type=MESH,
        )

    def sums_copy(i):
        return pltpu.make_async_remote_copy(
            src_ref=sums,
            dst_ref=sums_in.at[i],
            send_sem=ssend_sem.at[i],
            recv_sem=srecv_sem.at[i],
            device_id={"tensor": lax.rem(tensor + 1 + i, peers)},
            device_id_type=MESH,
        )

    def finals(xs, tile, blocks, swap_in, passing):
        part = size // 2
        tiles = 2 * peers

        def fetch_tile(q):
            shard = block_at(q // 2)
            rows = pl.ds(pl.multiple_of(q % 2 * part, part), part)
            return pltpu.make_async_copy(full.at[:, shard, rows], tile.at[q % 2], tile_sem.at[q % 2])

        fetch_xs = pltpu.make_async_copy(saved, xs.at[pl.ds(0, units)], load_sem)
        fetch_xs.start()
        fetch_tile(0).start()
        fetch_swapped(units - 1, swap_in)
        fetch_xs.wait()
        block = min(512, rows_all)

        def products(q, store):
            @pl.when(q + 1 < tiles)
            def _():
                fetch_tile(q + 1).start()

            fetch_tile(q).wait()

            def one(r, carry):
                rows = pl.ds(pl.multiple_of(r * block, block), block)
                grads, branch = None, None
                for u in range(units):
                    split = ATT if u % 3 == 1 else HID
                    left = dot(xs[u, rows, :split], tile[q % 2, u, :, :split], NT)
                    right = dot(xs[u, rows, split:], tile[q % 2, u, :, split:], NT)
                    grads = left if grads is None else grads + left
                    branch = right if branch is None else branch + right
                store(r, 0, grads)
                store(r, 1, branch)
                return carry

            lax.fori_loop(0, rows_all // block, one, 0)

        scatter_from = units * last - behind
        scatter_count = last * (LAG - 1) + 1 + behind
        remote = 2 * (peers - 1)

        def remote_tile(i):
            def one(h, carry):
                def store(r, what, value):
                    rows = pl.ds(pl.multiple_of(r * block, block), block)
                    cols = pl.ds(pl.multiple_of(h * part, part), part)
                    blocks[what, i, rows, cols] = value.astype(jnp.bfloat16)

                q = 2 * i + h
                products(q, store)
                low, high = q * scatter_count // remote, (q + 1) * scatter_count // remote
                run_ticks(swap_in, 0, 0, scatter_from + low, high - low)
                return carry

            lax.fori_loop(0, 2, one, 0)

        def send(what, *messages):
            for message in messages:
                tensor_copy(blocks, what, message).start()

        def add_half(what, slot, rows, message, onward):
            tensor_copy(blocks, what, message).wait_recv()
            copy = pltpu.make_async_copy(
                arrived.at[what, 0, rows], passing, load_sem
            )
            copy.start()
            copy.wait()
            blocks[what, slot, rows, :] = (
                blocks[what, slot, rows, :].astype(jnp.float32) + passing[...].astype(jnp.float32)
            ).astype(jnp.bfloat16)
            send(what, onward)

        if square:
            remote_tile(0)
            send(0, 0, 1)
            remote_tile(1)
            send(0, 2)
            remote_tile(2)
            send(0, 3)
            add_half(0, 1, lower, 1, 4)
            add_half(0, 2, upper, 0, 5)
            send(1, 0, 1, 2, 3)
        else:

            def one_block(i, carry):
                remote_tile(i)
                send(0, i)
                return carry

            def one_branch(i, carry):
                send(1, i)
                return carry

            lax.fori_loop(0, peers - 1, one_block, 0)
            lax.fori_loop(0, peers - 1, one_branch, 0)

        for h in range(2):

            def store(r, what, value):
                for a in range(block // half):
                    held[what, r * (block // half) + a, :, h * part : (h + 1) * part] = value[
                        a * half : (a + 1) * half
                    ]

            products(remote + h, store)

        if square:
            add_half(1, 1, lower, 1, 4)
            add_half(1, 2, upper, 0, 5)

        tok_at, cot_at, out_at = 2 * (peers - 1), 2 * (peers - 1) + 1, 2 * (peers - 1) + 2
        bring = [
            pltpu.make_async_copy(tokens.at[:, columns], xs.at[tok_at, :, pl.ds(0, size)], tile_sem.at[0]),
            pltpu.make_async_copy(cot_hbm.at[:, columns], xs.at[cot_at, :, pl.ds(0, size)], tile_sem.at[1]),
        ]
        for copy in bring:
            copy.start()
        for copy in bring:
            copy.wait()

        first = 1 if square else 0
        count = peers - 1 - first

        def collect(what):
            for message in range(2, 6) if square else ():
                tensor_copy(blocks, what, message).wait_recv()

            def one(i, carry):
                if not square:
                    tensor_copy(blocks, what, i).wait_recv()
                copy = pltpu.make_async_copy(
                    arrived.at[what, first + i], xs.at[what * count + i, :, pl.ds(0, size)], load_sem
                )
                copy.start()
                copy.wait()
                return carry

            lax.fori_loop(0, count, one, 0)

        def summed(what, r, rows):
            value = held[what, r, :, :size]
            for i in range(count):
                value += xs[what * count + i, rows, :size].astype(jnp.float32)
            return value

        gain = vec_ref[NIN + 1 : NIN + 2, columns]
        ones = jnp.ones((8, size), jnp.float32)

        def unit_of(rows):
            token = xs[tok_at, rows, :size].astype(jnp.float32)
            return (token - stats[rows, 0:1]) * stats[rows, 1:2]

        collect(0)

        def first_pass(r, carry):
            rows = pl.ds(pl.multiple_of(r * half, half), half)
            grad = summed(0, r, rows)
            held[0, r, :, :size] = grad
            unit = unit_of(rows)
            scaled = grad * gain
            sums[0:8, rows] = lax.dot_general(
                ones, scaled, NT, precision=lax.Precision.HIGHEST, preferred_element_type=jnp.float32
            )
            sums[8:16, rows] = lax.dot_general(
                ones, scaled * unit, NT, precision=lax.Precision.HIGHEST, preferred_element_type=jnp.float32
            )
            vec[NIN + 1 : NIN + 2, :] += jnp.sum(grad * unit, 0, keepdims=True)
            vec[NIN + 2 : NIN + 3, :] += jnp.sum(grad, 0, keepdims=True)
            return carry

        lax.fori_loop(0, rows_all // half, first_pass, 0)
        for i in range(peers - 1):
            sums_copy(i).start()
        to_core = pltpu.make_async_remote_copy(
            src_ref=vec, dst_ref=vec_core, send_sem=vsend_sem.at[0], recv_sem=vrecv_sem.at[0],
            device_id=other_core, device_id_type=MESH,
        )
        to_core.start()
        for i in range(peers - 1):
            sums_copy(i).wait_recv()
        inv_width = 1.0 / width

        def second_pass(r, carry):
            rows = pl.ds(pl.multiple_of(r * half, half), half)
            means = sums[:, rows]
            for i in range(peers - 1):
                means += sums_in[i, :, rows]
            means = (means * inv_width).T
            unit = unit_of(rows)
            held[0, r, :, :size] = stats[rows, 1:2] * (
                held[0, r, :, :size] * gain - means[:, 0:1] - unit * means[:, 8:9]
            ) + xs[cot_at, rows, :size].astype(jnp.float32)
            return carry

        lax.fori_loop(0, rows_all // half, second_pass, 0)
        put_grad = pltpu.make_async_copy(held.at[0, :, :, pl.ds(0, size)], token_grad, out_sem.at[0])
        put_grad.start()

        to_core.wait_recv()
        vec_line[z] = vec[...] + vec_core[...]

        def along_dp(i):
            return pltpu.make_async_remote_copy(
                src_ref=vec_line.at[z], dst_ref=vec_line.at[z],
                send_sem=vsend_sem.at[1 + i], recv_sem=vrecv_sem.at[1 + i],
                device_id={"dp": lax.rem(z + 1 + i, n)}, device_id_type=MESH,
            )

        def from_dp(i):
            there = lax.rem(z + n - 1 - i, n)
            return pltpu.make_async_remote_copy(
                src_ref=vec_line.at[there], dst_ref=vec_line.at[there],
                send_sem=vsend_sem.at[1 + i], recv_sem=vrecv_sem.at[1 + i],
                device_id={"dp": lax.rem(z + 1 + i, n)}, device_id_type=MESH,
            )

        for i in range(n - 1):
            along_dp(i).start()
        for i in range(n - 1):
            from_dp(i).wait_recv()
        vec_sum = vec_line[0]
        for i in range(1, n):
            vec_sum += vec_line[i]
        vec_all[tensor] = vec_sum

        def along_tensor(i):
            return pltpu.make_async_remote_copy(
                src_ref=vec_all.at[tensor], dst_ref=vec_all.at[tensor],
                send_sem=vsend_sem.at[n + i], recv_sem=vrecv_sem.at[n + i],
                device_id={"tensor": lax.rem(tensor + 1 + i, peers)}, device_id_type=MESH,
            )

        def from_tensor(i):
            there = lax.rem(tensor + peers - 1 - i, peers)
            return pltpu.make_async_remote_copy(
                src_ref=vec_all.at[there], dst_ref=vec_all.at[there],
                send_sem=vsend_sem.at[n + i], recv_sem=vrecv_sem.at[n + i],
                device_id={"tensor": lax.rem(tensor + 1 + i, peers)}, device_id_type=MESH,
            )

        for i in range(peers - 1):
            along_tensor(i).start()

        collect(1)
        out_bias = vec_ref[NIN : NIN + 1, columns]

        def third_pass(r, carry):
            rows = pl.ds(pl.multiple_of(r * half, half), half)
            value = xs[tok_at, rows, :size].astype(jnp.float32) + (summed(1, r, rows) + out_bias)
            xs[out_at, rows, :size] = value.astype(jnp.bfloat16)
            return carry

        lax.fori_loop(0, rows_all // half, third_pass, 0)
        put_result = pltpu.make_async_copy(xs.at[out_at, :, pl.ds(0, size)], result, out_sem.at[1])
        put_result.start()

        for i in range(peers - 1):
            from_tensor(i).wait_recv()
        vec_grad[...] = vec_all[...]
        put_grad.wait()
        put_result.wait()
        to_core.wait_send()
        for i in range(n - 1):
            along_dp(i).wait_send()
        for i in range(peers - 1):
            along_tensor(i).wait_send()
            sums_copy(i).wait_send()
        for i in range(6 if square else peers - 1):
            tensor_copy(blocks, 0, i).wait_send()
            tensor_copy(blocks, 1, i).wait_send()

    low, wide = jnp.bfloat16, jnp.float32
    window, qblock = rows_all + min(256, rows_all), min(256, rows_all)
    pl.run_scoped(
        forward_backward,
        pltpu.VMEM((rows_all, width), low),
        pltpu.VMEM((rows_all, width), low),
        pltpu.VMEM((2, rows_all // 8, width), low),
        pltpu.VMEM((2, size, ATT), wide),
        pltpu.VMEM((2, HID, size), wide),
        pltpu.VMEM((2, size, WIDE), low),
        pltpu.VMEM((n, size, WIDE), low),
        pltpu.VMEM((rows_all, WIDE), low),
        pltpu.VMEM((rows_all, LANES), low),
        pltpu.VMEM((rows_all, LANES), low),
        pltpu.VMEM((2, 2 * rows_all, LANES), wide),
        pltpu.VMEM((2, rows_all, LANES), wide),
        pltpu.VMEM((window, qblock), wide),
        pltpu.VMEM((2, n, half, WIDE), low),
        pltpu.VMEM((n, half, WIDE), low),
    )
    pl.run_scoped(
        finals,
        pltpu.VMEM((max(units, 2 * peers + 1), rows_all, WIDE), low),
        pltpu.VMEM((2, units, size // 2, WIDE), low),
        pltpu.VMEM((2, peers - 1, rows_all, size), low),
        pltpu.VMEM((n, half, WIDE), low),
        pltpu.VMEM((rows_all // 2, size), low),
    )


    def drain_kv(s, carry):
        send_kv(s).wait_send()
        return carry

    lax.fori_loop(0, steps, drain_kv, 0)

    def drain(m, carry):
        g, s = m // last, m % last + 1

        @pl.when(s == 1)
        def _():
            @pl.when(z < last)
            def _():
                hop(0, g, 0, z).wait_send()

            @pl.when(z > 0)
            def _():
                hop(1, g, 0, z).wait_send()

            @pl.when(g >= units - (LAG + 2))
            def _():
                keep(g).wait()
                share(g, mine).wait_send()

            share(g, theirs).wait_recv()

        @pl.when(z >= s)
        def _():
            @pl.when(z < last)
            def _():
                hop(0, g, s, z - s).wait_send()

            across(0, g, s - 1, z - s, mine).wait_send()

        @pl.when(z + s <= last)
        def _():
            @pl.when(z > 0)
            def _():
                hop(1, g, s, z + s).wait_send()

            across(1, g, s - 1, z + s, mine).wait_send()

        for way in range(2):
            distance = z if way == 0 else last - z

            @pl.when(distance < last - (s - 1))
            def _():
                pass_on(way, g, s - 1).wait_send()

        return carry

    lax.fori_loop(0, units * last, drain, 0)


def run_block(in_weight, out_weight, tokens, cotangent, bias, vectors, cosine, sine, begin):
    n, peers = lax.axis_size("dp"), lax.axis_size("tensor")
    size, cols_all = in_weight.shape[1:]
    steps = cols_all // LANES
    units = 3 * steps
    half = size // 2
    rows, width = tokens.shape
    assert width == n * size == peers * cols_all and size == cols_all and rows == n * half
    low, wide = jnp.bfloat16, jnp.float32
    anywhere = pl.BlockSpec(memory_space=pl.ANY)
    vm = pl.BlockSpec(memory_space=pltpu.VMEM)
    dma = pltpu.SemaphoreType.DMA
    return pl.pallas_call(
        functools.partial(block_kernel, n, steps, peers),
        out_shape=(
            jax.ShapeDtypeStruct((units, n, size, WIDE), low),
            jax.ShapeDtypeStruct((units, rows, WIDE), low),
            jax.ShapeDtypeStruct((units, size, WIDE), wide),
            jax.ShapeDtypeStruct((units, n, half, WIDE), low),
            jax.ShapeDtypeStruct((steps, 2, rows, LANES), wide),
            jax.ShapeDtypeStruct((2, peers - 1, rows, size), low),
            jax.ShapeDtypeStruct((rows, size), low),
            jax.ShapeDtypeStruct((n, half, size), wide),
            jax.ShapeDtypeStruct((peers, 16, size), wide),
        ),
        in_specs=[anywhere] * 4 + [vm] * 5,
        out_specs=[anywhere] * 8 + [vm],
        scratch_shapes=[
            pltpu.VMEM((steps, 2, 2 * rows, LANES), low),
            pltpu.VMEM((schedule(n)[-1], n, half, WIDE), wide),
            pltpu.VMEM((units, n + 1, half, WIDE), low),
            pltpu.VMEM((LAG + 2, half, WIDE), wide),
            pltpu.VMEM((rows, LANES), wide),
            pltpu.VMEM((16, size), wide),
            pltpu.VMEM((16, size), wide),
            pltpu.VMEM((n, 16, size), wide),
            pltpu.VMEM((peers, 16, size), wide),
            pltpu.VMEM((16, rows), wide),
            pltpu.VMEM((peers - 1, 16, rows), wide),
            dma((2, units, n)),
            dma((2, units, n)),
            dma((2, units, n)),
            dma((2, units, n)),
            dma((units,)),
            dma((units,)),
            dma((2, units, n - 1)),
            dma((2, units, n - 1)),
            dma((units,)),
            dma((units,)),
            dma((units,)),
            dma((steps,)),
            dma((steps,)),
            dma((steps,)),
            dma((steps,)),
            dma,
            dma,
            dma,
            dma((2, 4)),
            dma((2,)),
            dma((2,)),
            dma,
            dma((2, 6 if peers == 4 else peers - 1)),
            dma((2, 6 if peers == 4 else peers - 1)),
            dma((peers - 1,)),
            dma((peers - 1,)),
            dma((n + peers - 1,)),
            dma((n + peers - 1,)),
            dma((2,)),
            dma((2,)),
        ],
        compiler_params=pltpu.CompilerParams(
            collective_id=1, has_side_effects=True, vmem_limit_bytes=VMEM_LIMIT
        ),
        name="parallel_block",
    )(in_weight, out_weight, tokens, cotangent, bias, vectors, cosine, sine, begin)


def adam_kernel(into, chunks, *refs):
    pieces, refs = refs[:chunks], refs[chunks:]
    g = pl.program_id(0)

    def update(weights, turned):
        w, m, v, new_w, new_m, new_v = weights
        for c, piece in enumerate(pieces):
            part = slice(c * LANES, (c + 1) * LANES)
            at = (0, part) if turned else (0, slice(None), part)
            gradient = piece[0].T if turned else piece[0]
            new_w[at], new_m[at], new_v[at] = adamw(
                w[at], gradient, m[at], v[at], rate_matrix, weight_decay
            )

    @pl.when(g < into)
    def _():
        update(refs[:3] + refs[6:9], False)

    @pl.when(g >= into)
    def _():
        update(refs[3:6] + refs[9:], True)


def adam_weights(total, in_arrays, out_arrays):
    into, size, cols_all = in_arrays[0].shape
    outof = out_arrays[0].shape[0]
    chunks = cols_all // LANES

    def place(c, g):
        is_in = g < into
        group = jnp.where(is_in, g, g - into)
        lead = jnp.where(is_in, 3, 1)
        i = jnp.maximum((group - lead) * cols_all + c * LANES, 0) // HID
        unit = jnp.where(group < lead, 3 * c + 1, 3 * (i // 2) + 2 * (i % 2))
        lane = jnp.where(
            group < lead, jnp.where(is_in, group, 3), c % 2 + jnp.where(is_in, 0, 2)
        )
        return unit, 0, lane

    in_spec = pl.BlockSpec((1, size, cols_all), lambda g: (jnp.minimum(g, into - 1), 0, 0))
    out_spec = pl.BlockSpec((1, cols_all, size), lambda g: (jnp.maximum(g - into, 0), 0, 0))
    results = pl.pallas_call(
        functools.partial(adam_kernel, into, chunks),
        grid=(into + outof,),
        out_shape=tuple(jax.ShapeDtypeStruct(v.shape, jnp.float32) for v in in_arrays + out_arrays),
        in_specs=[pl.BlockSpec((1, size, LANES), functools.partial(place, c)) for c in range(chunks)]
        + [in_spec] * 3
        + [out_spec] * 3,
        out_specs=[in_spec] * 3 + [out_spec] * 3,
        compiler_params=pltpu.CompilerParams(vmem_limit_bytes=VMEM_LIMIT),
        name="adam_weights",
    )(*[total] * chunks, *in_arrays, *out_arrays)
    return results[:3], results[3:]


def layout(lengths_row, row_span):
    seg_ends = jnp.cumsum(lengths_row)
    seg_starts = seg_ends - lengths_row
    places = jnp.arange(row_span, dtype=jnp.int32)
    segment = jnp.sum((places[:, None] >= seg_ends[None, :]).astype(jnp.int32), 1)
    numbers = jnp.arange(lengths_row.shape[0], dtype=jnp.int32)
    return jnp.sum(jnp.where(segment[:, None] == numbers[None, :], seg_starts[None, :], 0), 1)


def rope_tables(places):
    half_rot = ROT // 2
    lane = jnp.arange(2 * HD, dtype=jnp.int32) % HD
    exponent = (lane % half_rot).astype(jnp.float32)
    frequency = 10000.0 ** (-2.0 * exponent / ROT)
    angles = places.astype(jnp.float32)[:, None] * frequency[None, :]
    turned = (lane < ROT)[None, :]
    cosine = jnp.where(turned, jnp.cos(angles), 1.0)
    sine = jnp.where(turned, jnp.sin(angles), 0.0)
    return cosine, sine


def body(
    tokens,
    cotangent,
    lengths,
    in_weight,
    out_weight,
    vectors,
    in_first,
    in_second,
    out_first,
    out_second,
    vec_first,
    vec_second,
):
    local_rows, model_width = tokens.shape
    slice_width = in_weight.shape[2]
    context_count = lax.axis_size("context")
    context_index = lax.axis_index("context")
    tensor_index = lax.axis_index("tensor")
    row_span = local_rows * context_count
    first_row = context_index * local_rows
    begin_all = layout(lengths[0], row_span)
    begin = lax.dynamic_slice_in_dim(begin_all, first_row, local_rows, 0)
    places = first_row + jnp.arange(local_rows, dtype=jnp.int32) - begin
    tables = rope_tables(places)

    column = tensor_index * slice_width
    in_bias = lax.dynamic_slice_in_dim(vectors[:NIN], column, slice_width, 1)
    steps = slice_width // LANES
    hid_bias = in_bias[3:].reshape(steps, 2, HID)
    att_bias = in_bias[:3].reshape(3, steps, LANES).transpose(1, 0, 2).reshape(steps, ATT)
    bias = jnp.stack(
        [
            jnp.pad(hid_bias[:, 0], ((0, 0), (0, WIDE - HID))),
            jnp.pad(att_bias, ((0, 0), (0, WIDE - ATT))),
            jnp.pad(hid_bias[:, 1], ((0, 0), (0, WIDE - HID))),
        ],
        1,
    ).reshape(3 * steps, 1, WIDE)
    by_group = jnp.transpose(in_weight, (1, 0, 2))
    _, _, total, _, _, _, result, token_grad, vec_grad = run_block(
        by_group, out_weight, tokens, cotangent, bias, vectors, tables[0], tables[1], begin[None]
    )
    token_grad = token_grad.reshape(local_rows, slice_width)
    vector_grad = jnp.transpose(vec_grad, (1, 0, 2)).reshape(-1, model_width)[: NIN + 3]
    new_vectors, new_vec_first, new_vec_second = adamw(
        vectors, vector_grad, vec_first, vec_second, rate_vector, 0.0
    )
    by_group_moments = [jnp.transpose(v, (1, 0, 2)) for v in (in_first, in_second)]
    new_by_group, (new_out, new_out_first, new_out_second) = adam_weights(
        total, [by_group] + by_group_moments, [out_weight, out_first, out_second]
    )
    new_in, new_in_first, new_in_second = (jnp.transpose(v, (1, 0, 2)) for v in new_by_group)
    return (
        result,
        token_grad,
        new_in,
        new_in_first,
        new_in_second,
        new_out,
        new_out_first,
        new_out_second,
        new_vectors,
        new_vec_first,
        new_vec_second,
    )


def solution(mesh):
    return jax.shard_map(
        body,
        mesh=mesh,
        in_specs=(
            P(("dp", "context"), None),
            P(("dp", "context"), None),
            P("dp", None),
            P("dp", None, "tensor"),
            P(None, "tensor", "dp"),
            P(),
            P("dp", None, "tensor"),
            P("dp", None, "tensor"),
            P(None, "tensor", "dp"),
            P(None, "tensor", "dp"),
            P(),
            P(),
        ),
        out_specs=(
            P(("dp", "context"), "tensor"),
            P(("dp", "context"), "tensor"),
            P("dp", None, "tensor"),
            P("dp", None, "tensor"),
            P("dp", None, "tensor"),
            P(None, "tensor", "dp"),
            P(None, "tensor", "dp"),
            P(None, "tensor", "dp"),
            P(),
            P(),
            P(),
        ),
        check_vma=False,
    )
```

```python
import functools

import jax
import jax.numpy as jnp
from jax import lax
from jax.experimental import pallas as pl
from jax.experimental.pallas import tpu as pltpu
from jax.sharding import PartitionSpec as P

HD = 64
ROT = 32
STEP = 10
NIN = 7
MESH = pl.DeviceIdType.MESH
VMEM_LIMIT = 60 * 2**20

norm_eps = 1e-05
beta_one = 0.9
beta_two = 0.95
adam_eps = 1e-08
weight_decay = 0.1
rate_matrix = 0.02
rate_vector = 0.4


def adamw(master, gradient, moment_one, moment_two, step_rate, decay_rate):
    first_new = beta_one * moment_one + (1.0 - beta_one) * gradient
    second_new = beta_two * moment_two + (1.0 - beta_two) * gradient * gradient
    first_hat = first_new / (1.0 - beta_one**STEP)
    second_hat = second_new / (1.0 - beta_two**STEP)
    updated = master - step_rate * (
        first_hat / (jnp.sqrt(second_hat) + adam_eps) + decay_rate * master
    )
    return (updated, first_new, second_new)


LANES = 2 * HD
WIDE = 4 * LANES
HID = WIDE // 2
ATT = 3 * LANES
LAG = 8

NT = (((1,), (1,)), ((), ()))
NN = (((1,), (0,)), ((), ()))
TN = (((0,), (0,)), ((), ()))


def dot(x, y, dims=NN):
    return lax.dot_general(x, y, dims, preferred_element_type=jnp.float32)


def greet(n, peers):
    z = lax.axis_index("dp")
    k = lax.axis_index("context")
    t = lax.axis_index("tensor")
    barrier = pltpu.get_barrier_semaphore()
    pl.semaphore_signal(barrier, inc=1, device_id={"context": 1 - k}, device_id_type=MESH)
    for i in range(1, n):
        pl.semaphore_signal(barrier, inc=1, device_id={"dp": lax.rem(z + i, n)}, device_id_type=MESH)
    for i in range(1, peers):
        pl.semaphore_signal(
            barrier, inc=1, device_id={"tensor": lax.rem(t + i, peers)}, device_id_type=MESH
        )
    pl.semaphore_wait(barrier, n + peers - 1)


def gelu_both(v):
    rate = 0.7978845608028654
    t = jnp.tanh(rate * (v + 0.044715 * (v * v * v)))
    value = 0.5 * v * (1.0 + t)
    slope = 0.5 * (1.0 + t) + 0.5 * v * (1.0 - t * t) * (rate * (1.0 + 3.0 * 0.044715 * (v * v)))
    return value, slope


def schedule(n):
    last = n - 1
    per_step = 3 * last
    in_hidden = 2 * per_step // 9
    in_attention = per_step - 2 * in_hidden
    done = (in_hidden, in_hidden + in_attention, per_step)
    lead = max([last * (n + i) - done[i] for i in range(3)] + [last * (n - 1)])
    out_hidden, out_attention = in_hidden // 2, in_attention
    behind = max(out_hidden + last, out_hidden + out_attention, 2 * out_hidden + out_attention - last)
    return per_step, in_hidden, in_attention, lead, out_hidden, out_attention, behind


def block_kernel(
    n, steps, peers,
    in_w, out_w, tokens, cot_hbm, bias_ref, vec_ref, cos_ref, sin_ref, begin_ref,
    full, saved, total, swap, kept, dkv_other, arrived, result, token_grad, vec_grad,
    kv, moved, returned, extra, held, pieces, line, outbox, stats, vec, vec_core, vec_line, vec_all, sums, sums_in,
    send_sem, recv_sem, psend_sem, precv_sem,
    xsend_sem, xrecv_sem, lsend_sem, lrecv_sem, keep_sem, fsend_sem, frecv_sem,
    kvsend_sem, kvrecv_sem, dsend_sem, drecv_sem, msend_sem, mrecv_sem, bsend_sem, brecv_sem, esend_sem, erecv_sem, load_sem, save_sem, weight_sem, pack_sem, put_sem, rows_sem, swap_sem, held_sem, piece_sem, box_sem,
    tsend_sem, trecv_sem, ssend_sem, srecv_sem, vsend_sem, vrecv_sem, tile_sem, out_sem,
):
    units = 3 * steps
    last = n - 1
    per_step, in_hidden, in_attention, lead, out_hidden, out_attention, behind = schedule(n)
    depth, boxes = 2, 3
    size, cols_all = in_w.shape[1], in_w.shape[2]
    half = size // 2
    rows_all, width = tokens.shape
    tensor = lax.axis_index("tensor")
    columns = pl.ds(pl.multiple_of(tensor * size, size), size)
    z = lax.axis_index("dp")
    k = lax.axis_index("context")
    mine = pl.ds(pl.multiple_of(k * half, half), half)
    theirs = pl.ds(pl.multiple_of((1 - k) * half, half), half)
    other_core = {"context": 1 - k}
    greet(n, peers)


    def hop(way, g, h, shard):
        return pltpu.make_async_remote_copy(
            src_ref=full.at[g, shard, mine],
            dst_ref=full.at[g, shard, mine],
            send_sem=send_sem.at[way, g, h],
            recv_sem=recv_sem.at[way, g, h],
            device_id={"dp": z + 1 - 2 * way},
            device_id_type=MESH,
        )

    def across(way, g, h, shard, rows):
        return pltpu.make_async_remote_copy(
            src_ref=full.at[g, shard, rows],
            dst_ref=full.at[g, shard, rows],
            send_sem=psend_sem.at[way, g, h],
            recv_sem=precv_sem.at[way, g, h],
            device_id=other_core,
            device_id_type=MESH,
        )

    def send_own(g):
        @pl.when(z < last)
        def _():
            hop(0, g, 0, z).start()

        @pl.when(z > 0)
        def _():
            hop(1, g, 0, z).start()

    def gather_tick(m):
        s = m % last + 1
        g = m // last - (s - 1)

        @pl.when((s == 1) & (g < units - 1))
        def _():
            send_own(g + 1)

        @pl.when((g >= 0) & (g < units))
        def _():
            @pl.when(z >= s)
            def _():
                hop(0, g, s - 1, z - s).wait_recv()

                @pl.when(z < last)
                def _():
                    hop(0, g, s, z - s).start()

                across(0, g, s - 1, z - s, mine).start()

            @pl.when(z + s <= last)
            def _():
                hop(1, g, s - 1, z + s).wait_recv()

                @pl.when(z > 0)
                def _():
                    hop(1, g, s, z + s).start()

                across(1, g, s - 1, z + s, mine).start()

    def need(u):
        def one(i, carry):
            s = i + 1

            @pl.when(z >= s)
            def _():
                across(0, u, s - 1, z - s, theirs).wait_recv()

            @pl.when(z + s <= last)
            def _():
                across(1, u, s - 1, z + s, theirs).wait_recv()

            return carry

        lax.fori_loop(0, last, one, 0)

    def send_kv(s):
        rows = pl.ds(pl.multiple_of(k * rows_all, rows_all), rows_all)
        return pltpu.make_async_remote_copy(
            src_ref=kv.at[s, :, rows],
            dst_ref=kv.at[s, :, rows],
            send_sem=kvsend_sem.at[s],
            recv_sem=kvrecv_sem.at[s],
            device_id=other_core,
            device_id_type=MESH,
        )


    def exchange_from(outgoing, g):
        return pltpu.make_async_remote_copy(
            src_ref=outgoing,
            dst_ref=swap.at[g],
            send_sem=xsend_sem.at[g],
            recv_sem=xrecv_sem.at[g],
            device_id=other_core,
            device_id_type=MESH,
        )

    def slot_of(way, i):
        return i if way == 0 else n - i

    def pass_on(way, g, i):
        slot = slot_of(way, i)
        return pltpu.make_async_remote_copy(
            src_ref=line.at[g, slot],
            dst_ref=line.at[g, slot],
            send_sem=lsend_sem.at[way, g, i],
            recv_sem=lrecv_sem.at[way, g, i],
            device_id={"dp": z + 1 - 2 * way},
            device_id_type=MESH,
        )

    my_part = pl.ds(pl.multiple_of(k * HID, HID), HID)
    their_part = pl.ds(pl.multiple_of((1 - k) * HID, HID), HID)

    def keep(g):
        return pltpu.make_async_copy(outbox.at[g % boxes], total.at[g, my_part], keep_sem.at[g])

    def share(g, rows):
        return pltpu.make_async_remote_copy(
            src_ref=outbox.at[g % boxes],
            dst_ref=total.at[g, rows],
            send_sem=fsend_sem.at[g],
            recv_sem=frecv_sem.at[g],
            device_id=other_core,
            device_id_type=MESH,
        )

    def fetch_swapped(g, swap_in):
        @pl.when(g >= 0)
        def _():
            exchange_from(swap_in, g).wait_recv()
            pltpu.make_async_copy(swap.at[g], swap_in, swap_sem).start()

    def put_held(g):
        return pltpu.make_async_copy(held.at[g % depth], kept.at[g], held_sem.at[g % depth])

    def prepare(g, swap_in):
        @pl.when(g >= 0)
        def _():
            pltpu.make_async_copy(swap.at[g], swap_in, swap_sem).wait()

            def one(j, carry):
                held[g % depth, j] += swap_in[j].astype(jnp.float32)
                return carry

            lax.fori_loop(0, n, one, 0)
            put_held(g).start()

    def wait_put(g):
        @pl.when(g >= 0)
        def _():
            put_held(g).wait()

    def piece_copy(way, g, i, slot):
        shard = n - 1 - i if way == 0 else i
        return pltpu.make_async_copy(kept.at[g, shard], pieces.at[way, slot], piece_sem.at[way, slot])

    def box_copy(g):
        return pltpu.make_async_copy(kept.at[g, z], outbox.at[g % boxes], box_sem.at[g % boxes])

    def needs(way, t):
        distance = z if way == 0 else last - z
        m = t - LAG * distance
        g, i = m // last, m % last
        return g, i, (m >= 0) & (m < units * last) & (distance < last - i)

    def fetch_pieces(t):
        for way in range(2):
            g, i, needed = needs(way, t)

            @pl.when(needed)
            def _():
                piece_copy(way, g, i, t % 2).start()

        done = t - last * LAG

        @pl.when((done >= 0) & (done % last == 0))
        def _():
            g = done // last

            @pl.when(g >= boxes)
            def _():
                keep(g - boxes).wait()
                share(g - boxes, my_part).wait_send()

            box_copy(g).start()

    def scatter_step(way, t):
        distance = z if way == 0 else last - z
        m = t - LAG * distance
        g, i, needed = needs(way, t)
        slot = slot_of(way, i)

        @pl.when(needed)
        def _():
            piece_copy(way, g, i, t % 2).wait()

        @pl.when((m >= 0) & (m < units * last) & (distance > 0) & (distance <= last - i))
        def _():
            pass_on(way, g, i).wait_recv()

        @pl.when(needed)
        def _():
            @pl.when(distance == 0)
            def _():
                line[g, slot] = pieces[way, t % 2].astype(jnp.bfloat16)

            @pl.when(distance > 0)
            def _():
                line[g, slot] = (line[g, slot].astype(jnp.float32) + pieces[way, t % 2]).astype(jnp.bfloat16)

            pass_on(way, g, i).start()

    def finish(g):
        box = g % boxes
        box_copy(g).wait()

        @pl.when(z > 0)
        def _():
            outbox[box] += line[g, slot_of(0, n - 1 - z)].astype(jnp.float32)

        @pl.when(z < last)
        def _():
            outbox[box] += line[g, slot_of(1, z)].astype(jnp.float32)

        keep(g).start()
        share(g, my_part).start()

    def scatter_tick(t):
        scatter_step(0, t)
        scatter_step(1, t)
        done = t - last * LAG

        @pl.when((done >= 0) & (done % last == 0))
        def _():
            finish(done // last)

    def run_ticks(gather_from, gather_count, scatter_from, scatter_count):
        def one_gather(i, carry):
            gather_tick(gather_from + i)
            return carry

        def one_scatter(i, carry):
            @pl.when(i + 1 < scatter_count)
            def _():
                fetch_pieces(scatter_from + i + 1)

            scatter_tick(scatter_from + i)
            return carry

        if not isinstance(scatter_count, int):
            pl.when(scatter_count > 0)(lambda: fetch_pieces(scatter_from))
        elif scatter_count:
            fetch_pieces(scatter_from)
        lax.fori_loop(0, gather_count, one_gather, 0)
        lax.fori_loop(0, scatter_count, one_scatter, 0)

    def forward_backward(
        normed, cot, stage, raw_in, raw_out, packed, wbuf, x, qg, dkv, back, dkv_tmp, mask, outgoing, swap_in
    ):

        def exchange(g):
            return exchange_from(outgoing.at[g % 2], g)

        ticks = run_ticks

        part = stage.shape[1]
        norm_blocks = rows_all // part

        def fetch_rows(i):
            rows = pl.ds(pl.multiple_of(i * part, part), part)
            return pltpu.make_async_copy(tokens.at[rows], stage.at[i % 2], rows_sem.at[i % 2])

        def normalize(i):
            @pl.when(i + 1 < norm_blocks)
            def _():
                fetch_rows(i + 1).start()

            fetch_rows(i).wait()

            def few(r, c):
                sub = pl.ds(pl.multiple_of(r * 64, 64), 64)
                there = pl.ds(pl.multiple_of(i * part + r * 64, 64), 64)
                inputs = stage[i % 2, sub, :].astype(jnp.float32)
                centered = inputs - jnp.mean(inputs, 1, keepdims=True)
                inv_dev = lax.rsqrt(jnp.mean(centered * centered, 1, keepdims=True) + norm_eps)
                normed[there, :] = (
                    centered * inv_dev * vec_ref[NIN + 1 : NIN + 2, :] + vec_ref[NIN + 2 : NIN + 3, :]
                ).astype(jnp.bfloat16)
                lane = lax.broadcasted_iota(jnp.int32, (64, LANES), 1)
                stats[there, :] = jnp.where(lane == 0, jnp.mean(inputs, 1, keepdims=True), inv_dev)
                return c

            lax.fori_loop(0, part // 64, few, 0)

        def hidden_place(i):
            return i * HID // cols_all, pl.multiple_of(i * HID % cols_all, HID)

        def fetch_raw(u, start):
            s, slot = u // 3, u % 2

            def each(copies):
                for copy in copies:
                    copy.start() if start else copy.wait()

            @pl.when(u % 3 == 1)
            def _():
                cols = pl.ds(pl.multiple_of(s * LANES, LANES), LANES)
                each(
                    [
                        pltpu.make_async_copy(
                            in_w.at[g, :, cols],
                            raw_in.at[slot, :, pl.ds(g * LANES, LANES)],
                            pack_sem.at[slot, g],
                        )
                        for g in range(3)
                    ]
                    + [
                        pltpu.make_async_copy(
                            out_w.at[0, cols], raw_out.at[slot, pl.ds(0, LANES)], pack_sem.at[slot, 3]
                        )
                    ]
                )

            @pl.when(u % 3 != 1)
            def _():
                group, first = hidden_place(2 * s + (u % 3) // 2)
                cols = pl.ds(first, HID)
                each(
                    [
                        pltpu.make_async_copy(
                            in_w.at[3 + group, :, cols],
                            raw_in.at[slot, :, pl.ds(0, HID)],
                            pack_sem.at[slot, 0],
                        ),
                        pltpu.make_async_copy(out_w.at[1 + group, cols], raw_out.at[slot], pack_sem.at[slot, 1]),
                    ]
                )

        def put_packed(u):
            return pltpu.make_async_copy(packed.at[u % 2], full.at[u, z], put_sem.at[u % 2])

        def pack(u):
            slot = u % 2
            fetch_raw(u, False)

            @pl.when(u % 3 == 1)
            def _():
                packed[slot, :, :ATT] = raw_in[slot].astype(jnp.bfloat16)
                packed[slot, :, ATT:] = raw_out[slot, :LANES, :].astype(jnp.bfloat16).T

            @pl.when(u % 3 != 1)
            def _():
                packed[slot, :, :HID] = raw_in[slot, :, :HID].astype(jnp.bfloat16)
                packed[slot, :, HID:] = raw_out[slot].astype(jnp.bfloat16).T

            put_packed(u).start()

        def fetch_weights(u):
            return pltpu.make_async_copy(full.at[u], wbuf, weight_sem)

        def next_weights(u):
            @pl.when(u < units)
            def _():
                need(u)
                fetch_weights(u).start()

        def column_sums(split):
            ones = jnp.ones((8, rows_all), jnp.bfloat16)
            return dot(ones, x[:, :split])[0:1, :]

        def save(u):
            return pltpu.make_async_copy(x, saved.at[u], save_sem)

        def wait_saved(u):
            @pl.when(u > 0)
            def _():
                save(u - 1).wait()

        def gradients(u, split):
            @pl.when(u >= 2)
            def _():
                exchange(u - 2).wait_send()

            def part(first, end, j):
                turns = [(first, min(end, split), normed), (max(first, split), end, cot)]
                return [
                    (low, high, dot(x[:, low:high], rows[:, pl.ds(pl.multiple_of(j * size, size), size)], TN))
                    for low, high, rows in turns
                    if low < high
                ]

            for core in range(2):

                @pl.when(k == core)
                def _():
                    def one(j, carry):
                        for low, high, value in part(core * HID, (core + 1) * HID, j):
                            held[u % depth, j, low - core * HID : high - core * HID] = value
                        for low, high, value in part((1 - core) * HID, (2 - core) * HID, j):
                            outgoing[u % 2, j, low - (1 - core) * HID : high - (1 - core) * HID] = value.astype(
                                jnp.bfloat16
                            )
                        return carry

                    lax.fori_loop(0, n, one, 0)

            exchange(u).start()

        block = min(512, rows_all)

        def other_first_ticks():
            def one(m, carry):
                @pl.when((m // last != m % last) & (m != last))
                def _():
                    gather_tick(m)

                return carry

            lax.fori_loop(0, lead, one, 0)

        def hidden_unit(u, i_hidden, at, out_at, opens):
            fetch_weights(u).wait()
            wait_saved(u)
            wait_put(u - 2)

            def one(i, carry):
                rows = pl.ds(pl.multiple_of(i * block, block), block)
                pre = dot(normed[rows, :], wbuf[:, :, :HID].reshape(width, HID)) + bias_ref[u][:, :HID]
                value, slope = gelu_both(pre)
                x[rows, HID:] = value.astype(jnp.bfloat16)
                grad = dot(cot[rows, :], wbuf[:, :, HID:].reshape(width, HID))
                x[rows, :HID] = (grad * slope).astype(jnp.bfloat16)
                return carry

            lax.fori_loop(0, rows_all // block, one, 0)
            save(u).start()
            fetch_swapped(u - 1, swap_in)

            def gather():
                ticks(at + lead, in_hidden, 0, 0)
                next_weights(u + 1)

            if opens:
                pl.when(u > 0)(gather)
            else:
                gather()
            ticks(0, 0, out_at - behind, out_hidden)
            prepare(u - 1, swap_in)
            group, first = hidden_place(i_hidden)
            vec[pl.ds(3 + group, 1), pl.ds(first, HID)] = column_sums(HID)
            gradients(u, HID)
            if opens:

                @pl.when(u == 0)
                def _():
                    other_first_ticks()
                    gather()


        qblock = mask.shape[1]
        window = mask.shape[0]
        qblocks = rows_all // qblock

        def rope(v, rows, sign):
            half_rot = ROT // 2
            lane = lax.broadcasted_iota(jnp.int32, v.shape, 1) % HD
            ahead = pltpu.roll(v, LANES - half_rot, 1)
            behind = pltpu.roll(v, half_rot, 1)
            other = jnp.where(lane < half_rot, -ahead, behind)
            return v * cos_ref[rows, :] + other * (sign * sin_ref[rows, :])

        def recv_kv(s):
            rows = pl.ds(pl.multiple_of((1 - k) * rows_all, rows_all), rows_all)
            return pltpu.make_async_remote_copy(
                src_ref=kv.at[s, :, rows],
                dst_ref=kv.at[s, :, rows],
                send_sem=kvsend_sem.at[s],
                recv_sem=kvrecv_sem.at[s],
                device_id=other_core,
                device_id_type=MESH,
            )

        def send_dkv(s):
            return pltpu.make_async_remote_copy(
                src_ref=dkv.at[:, pl.ds(0, rows_all)],
                dst_ref=dkv_other.at[s],
                send_sem=dsend_sem.at[s],
                recv_sem=drecv_sem.at[s],
                device_id=other_core,
                device_id_type=MESH,
            )

        def send_first(s):
            return pltpu.make_async_remote_copy(
                src_ref=qg.at[:, pl.ds(0, qblock)],
                dst_ref=moved.at[s],
                send_sem=msend_sem.at[s],
                recv_sem=mrecv_sem.at[s],
                device_id=other_core,
                device_id_type=MESH,
            )

        def send_back(s):
            return pltpu.make_async_remote_copy(
                src_ref=back,
                dst_ref=returned.at[s],
                send_sem=bsend_sem.at[s],
                recv_sem=brecv_sem.at[s],
                device_id=other_core,
                device_id_type=MESH,
            )

        def send_extra(s):
            return pltpu.make_async_remote_copy(
                src_ref=dkv.at[:, pl.ds(rows_all, qblock)],
                dst_ref=extra.at[s],
                send_sem=esend_sem.at[s],
                recv_sem=erecv_sem.at[s],
                device_id=other_core,
                device_id_type=MESH,
            )

        def sent(s):
            @pl.when(k == 1)
            def _():
                send_dkv(s).wait_send()
                send_first(s).wait_send()

            @pl.when(k == 0)
            def _():
                send_back(s).wait_send()
                send_extra(s).wait_send()

        def attend(s, q_low, g_low, first_query, first_key, span):
            keys = pl.ds(first_key, span)
            key_at = first_key + lax.broadcasted_iota(jnp.int32, (span, qblock), 0)
            query_at = first_query + lax.broadcasted_iota(jnp.int32, (span, qblock), 1)
            begin = begin_ref[0:1, pl.ds(pl.multiple_of(first_query, qblock), qblock)]
            mask[:span] = jnp.where((key_at >= begin) & (key_at <= query_at), 0.0, -1e30)
            lane = lax.broadcasted_iota(jnp.int32, (qblock, LANES), 1)
            att = jnp.zeros((qblock, LANES), jnp.float32)
            dq = jnp.zeros((qblock, LANES), jnp.float32)
            for head in range(2):
                inside = (lane >= head * HD) & (lane < (head + 1) * HD)
                q_own = jnp.where(inside, q_low, jnp.zeros((qblock, LANES), jnp.bfloat16))
                g_own = jnp.where(inside, g_low, jnp.zeros((qblock, LANES), jnp.bfloat16))
                scores = dot(kv[s, 0, keys, :], q_own, NT) + mask[:span]
                weights = jnp.exp(scores - jnp.max(scores, 0, keepdims=True))
                probs = weights * (1.0 / jnp.sum(weights, 0, keepdims=True))
                probs_low = probs.astype(jnp.bfloat16)
                grad_probs = dot(kv[s, 1, keys, :], g_own, NT)
                inner = jnp.sum(probs * grad_probs, 0, keepdims=True)
                grad_scores = (probs * (grad_probs - inner)).astype(jnp.bfloat16)
                att = jnp.where(inside, dot(probs_low, kv[s, 1, keys, :], TN), att)
                dq = jnp.where(inside, dot(grad_scores, kv[s, 0, keys, :], TN), dq)
                dkv[1, keys, :] += dot(probs_low, g_own)
                dkv[0, keys, :] += dot(grad_scores, q_own)
            return att, dq * HD**-0.5

        def attend_own(s, b, first_key, span):
            rows = pl.ds(pl.multiple_of(b * qblock, qblock), qblock)
            att, dq = attend(s, qg[0, rows, :], qg[1, rows, :], k * rows_all + b * qblock, first_key, span)
            x[rows, ATT:] = att.astype(jnp.bfloat16)
            x[rows, :LANES] = rope(dq, rows, -1.0).astype(jnp.bfloat16)

        def attention_unit(u, s, at, out_at):
            fetch_weights(u).wait()
            wait_saved(u)
            wait_put(u - 2)

            @pl.when(s > 0)
            def _():
                sent(s - 1)

            def project(i, carry):
                rows = pl.ds(pl.multiple_of(i * block, block), block)
                there = pl.ds(pl.multiple_of(k * rows_all + i * block, block), block)
                pre = dot(normed[rows, :], wbuf[:, :, :ATT].reshape(width, ATT)) + bias_ref[u][:, :ATT]
                query = rope(pre[:, :LANES], rows, 1.0).astype(jnp.bfloat16)
                qg[0, rows, :] = query * jnp.bfloat16(HD**-0.5)
                kv[s, 0, there, :] = rope(pre[:, LANES : 2 * LANES], rows, 1.0).astype(jnp.bfloat16)
                kv[s, 1, there, :] = pre[:, 2 * LANES :].astype(jnp.bfloat16)
                return carry

            lax.fori_loop(0, rows_all // block, project, 0)
            send_kv(s).start()

            def project_grad(i, carry):
                rows = pl.ds(pl.multiple_of(i * block, block), block)
                grad = dot(cot[rows, :], wbuf[:, :, ATT:].reshape(width, LANES))
                qg[1, rows, :] = grad.astype(jnp.bfloat16)
                return carry

            lax.fori_loop(0, rows_all // block, project_grad, 0)

            @pl.when(k == 1)
            def _():
                send_first(s).start()

            dkv[...] = jnp.zeros_like(dkv)
            per_block = in_attention // qblocks
            early = in_attention - per_block * qblocks
            out_block = out_attention // qblocks
            out_early = out_attention - out_block * qblocks
            fetch_swapped(u - 1, swap_in)
            ticks(at + lead, early, out_at - behind, out_early)
            prepare(u - 1, swap_in)
            recv_kv(s).wait_recv()

            def turn_of(b, carry):
                @pl.when((k == 1) & (b < qblocks - 1))
                def _():
                    first_key = pl.multiple_of(rows_all + (b + 2) * qblock - window, qblock)
                    attend_own(s, b + 1, first_key, window)

                @pl.when((k == 1) & (b == qblocks - 2))
                def _():
                    send_dkv(s).start()

                for own in range(qblocks):

                    @pl.when((k == 0) & (b == (own if own > 1 else 0)))
                    def _():
                        attend_own(s, own, 0, (own + 1) * qblock)

                @pl.when((k == 0) & (b == 1))
                def _():
                    send_first(s).wait_recv()
                    att, dq = attend(s, moved[s, 0], moved[s, 1], rows_all, 0, window)
                    back[0], back[1] = att, dq
                    send_back(s).start()
                    send_extra(s).start()

                ticks(
                    at + early + b * per_block + lead,
                    per_block,
                    out_at + out_early + b * out_block - behind,
                    out_block,
                )
                return carry

            lax.fori_loop(0, qblocks, turn_of, 0)
            first_rows, own_rows = pl.ds(0, qblock), pl.ds(0, rows_all)

            @pl.when(k == 1)
            def _():
                send_back(s).wait_recv()
                send_extra(s).wait_recv()
                x[first_rows, ATT:] = returned[s, 0].astype(jnp.bfloat16)
                x[first_rows, :LANES] = rope(returned[s, 1], first_rows, -1.0).astype(jnp.bfloat16)
                dkv[:, pl.ds(rows_all, qblock)] += extra[s]

            @pl.when(k == 0)
            def _():
                send_dkv(s).wait_recv()
                copy = pltpu.make_async_copy(dkv_other.at[s], dkv_tmp, load_sem)
                copy.start()
                copy.wait()
                dkv[:, own_rows] += dkv_tmp[...]

            def turn(i, carry):
                rows = pl.ds(pl.multiple_of(i * qblock, qblock), qblock)
                there = pl.ds(pl.multiple_of(k * rows_all + i * qblock, qblock), qblock)
                x[rows, LANES : 2 * LANES] = rope(dkv[0, there, :], rows, -1.0).astype(jnp.bfloat16)
                x[rows, 2 * LANES : ATT] = dkv[1, there, :].astype(jnp.bfloat16)
                return carry

            lax.fori_loop(0, qblocks, turn, 0)
            save(u).start()
            next_weights(u + 1)
            bias_grad = column_sums(ATT)
            for g in range(3):
                vec[g : g + 1, pl.ds(pl.multiple_of(s * LANES, LANES), LANES)] = bias_grad[
                    :, g * LANES : (g + 1) * LANES
                ]
            gradients(u, ATT)


        cot_copy = pltpu.make_async_copy(cot_hbm, cot, save_sem)
        cot_copy.start()
        fetch_rows(0).start()
        fetch_raw(0, True)
        fetch_raw(1, True)
        for u in range(2):
            pack(u)
            put_packed(u).wait()
            if u == 0:
                send_own(0)
            fetch_raw(u + 2, True)

        def begin_step(i, carry):
            @pl.when(i + 2 < units)
            def _():
                pack(i + 2)

            @pl.when(i < norm_blocks)
            def _():
                normalize(i)

            @pl.when(i + 2 < units)
            def _():
                put_packed(i + 2).wait()

            @pl.when(i + 4 < units)
            def _():
                fetch_raw(i + 4, True)

            @pl.when(i == 0)
            def _():
                gather_tick(0)

            @pl.when(i == 1)
            def _():
                gather_tick(last)

            @pl.when((i >= 2) & (i <= last))
            def _():
                gather_tick((i - 1) * last + i - 1)

            return carry

        lax.fori_loop(0, max(units - 2, norm_blocks, n), begin_step, 0)
        cot_copy.wait()
        next_weights(0)
        vec[...] = jnp.zeros_like(vec)
        vec[NIN : NIN + 1, :] = dot(jnp.ones((8, rows_all), jnp.bfloat16), cot[:, columns])[0:1, :]

        def super_step(s, carry):
            at = s * per_step
            out_at = s * (2 * out_hidden + out_attention)
            hidden_unit(3 * s, 2 * s, at, out_at, True)
            attention_unit(3 * s + 1, s, at + in_hidden, out_at + out_hidden)
            hidden_unit(
                3 * s + 2, 2 * s + 1, at + in_hidden + in_attention, out_at + out_hidden + out_attention, False
            )
            return carry

        lax.fori_loop(0, steps, super_step, 0)

        save(units - 1).wait()
        exchange(units - 2).wait_send()
        exchange(units - 1).wait_send()

        sent(steps - 1)


    square = peers == 4
    upper, lower = pl.ds(0, rows_all // 2), pl.ds(rows_all // 2, rows_all // 2)

    def beside(axis):
        return tensor + 1 - 2 * (tensor % 2) if axis == 0 else tensor + 2 - 4 * (tensor // 2)

    def block_at(i):
        if not square:
            return lax.rem(tensor + 1 + i, peers)
        return jnp.where(
            i == 0, 3 - tensor, jnp.where(i == 1, beside(0), jnp.where(i == 2, beside(1), tensor))
        )

    def tensor_copy(blocks, what, message):
        if square:
            slot, rows, axis = ((0, upper, 0), (0, lower, 1), (1, upper, 0), (2, lower, 1), (1, lower, 0), (2, upper, 1))[
                message
            ]
            source, there = blocks.at[what, slot, rows], arrived.at[what, slot, rows]
            target = beside(axis)
        else:
            source, there = blocks.at[what, message], arrived.at[what, message]
            target = block_at(message)
        return pltpu.make_async_remote_copy(
            src_ref=source,
            dst_ref=there,
            send_sem=tsend_sem.at[what, message],
            recv_sem=trecv_sem.at[what, message],
            device_id={"tensor": target},
            device_id_type=MESH,
        )

    def sums_copy(i):
        return pltpu.make_async_remote_copy(
            src_ref=sums,
            dst_ref=sums_in.at[i],
            send_sem=ssend_sem.at[i],
            recv_sem=srecv_sem.at[i],
            device_id={"tensor": lax.rem(tensor + 1 + i, peers)},
            device_id_type=MESH,
        )

    def finals(xs, tile, blocks, swap_in, passing):
        part = size // 2
        tiles = 2 * peers

        def fetch_tile(q):
            shard = block_at(q // 2)
            rows = pl.ds(pl.multiple_of(q % 2 * part, part), part)
            return pltpu.make_async_copy(full.at[:, shard, rows], tile.at[q % 2], tile_sem.at[q % 2])

        fetch_xs = pltpu.make_async_copy(saved, xs.at[pl.ds(0, units)], load_sem)
        fetch_xs.start()
        fetch_tile(0).start()
        fetch_swapped(units - 1, swap_in)
        prepare(units - 1, swap_in)
        wait_put(units - 2)
        wait_put(units - 1)
        fetch_xs.wait()
        block = min(512, rows_all)

        def products(q, store):
            @pl.when(q + 1 < tiles)
            def _():
                fetch_tile(q + 1).start()

            fetch_tile(q).wait()

            def one(r, carry):
                rows = pl.ds(pl.multiple_of(r * block, block), block)
                grads, branch = None, None
                for u in range(units):
                    split = ATT if u % 3 == 1 else HID
                    left = dot(xs[u, rows, :split], tile[q % 2, u, :, :split], NT)
                    right = dot(xs[u, rows, split:], tile[q % 2, u, :, split:], NT)
                    grads = left if grads is None else grads + left
                    branch = right if branch is None else branch + right
                store(r, 0, grads)
                store(r, 1, branch)
                return carry

            lax.fori_loop(0, rows_all // block, one, 0)

        scatter_at = steps * (2 * out_hidden + out_attention) - behind
        scatter_count = (units - 1) * last + last * LAG + 1 - scatter_at
        remote = 2 * (peers - 1)
        tile_count = scatter_count * 2 // 5 // remote
        rest_at, rest_count = scatter_at + tile_count * remote, scatter_count - tile_count * remote
        cuts = [rest_at + rest_count * share_of // 16 for share_of in (0, 2, 5, 8, 11, 13, 16)]

        def rest(i):
            run_ticks(0, 0, cuts[i], cuts[i + 1] - cuts[i])

        def remote_tile(i):
            def one(h, carry):
                def store(r, what, value):
                    rows = pl.ds(pl.multiple_of(r * block, block), block)
                    cols = pl.ds(pl.multiple_of(h * part, part), part)
                    blocks[what, i, rows, cols] = value.astype(jnp.bfloat16)

                q = 2 * i + h
                products(q, store)
                run_ticks(0, 0, scatter_at + q * tile_count, tile_count)
                return carry

            lax.fori_loop(0, 2, one, 0)

        def send(what, *messages):
            for message in messages:
                tensor_copy(blocks, what, message).start()

        def add_half(what, slot, rows, message, onward):
            tensor_copy(blocks, what, message).wait_recv()
            copy = pltpu.make_async_copy(
                arrived.at[what, 0, rows], passing, load_sem
            )
            copy.start()
            copy.wait()
            blocks[what, slot, rows, :] = (
                blocks[what, slot, rows, :].astype(jnp.float32) + passing[...].astype(jnp.float32)
            ).astype(jnp.bfloat16)
            send(what, onward)

        if square:
            remote_tile(0)
            send(0, 0, 1)
            remote_tile(1)
            send(0, 2)
            remote_tile(2)
            send(0, 3)
            add_half(0, 1, lower, 1, 4)
            add_half(0, 2, upper, 0, 5)
            send(1, 0, 1, 2, 3)
        else:

            def one_block(i, carry):
                remote_tile(i)
                send(0, i)
                return carry

            def one_branch(i, carry):
                send(1, i)
                return carry

            lax.fori_loop(0, peers - 1, one_block, 0)
            lax.fori_loop(0, peers - 1, one_branch, 0)

        for h in range(2):

            def store(r, what, value):
                for a in range(block // HID):
                    held[what, r * (block // HID) + a, :, h * part : (h + 1) * part] = value[
                        a * HID : (a + 1) * HID
                    ]

            products(remote + h, store)

        rest(0)
        if square:
            add_half(1, 1, lower, 1, 4)
            add_half(1, 2, upper, 0, 5)

        tok_at, cot_at, out_at = 2 * (peers - 1), 2 * (peers - 1) + 1, 2 * (peers - 1) + 2
        bring = [
            pltpu.make_async_copy(tokens.at[:, columns], xs.at[tok_at, :, pl.ds(0, size)], tile_sem.at[0]),
            pltpu.make_async_copy(cot_hbm.at[:, columns], xs.at[cot_at, :, pl.ds(0, size)], tile_sem.at[1]),
        ]
        for copy in bring:
            copy.start()
        for copy in bring:
            copy.wait()

        first = 1 if square else 0
        count = peers - 1 - first

        def collect(what):
            for message in range(2, 6) if square else ():
                tensor_copy(blocks, what, message).wait_recv()

            def one(i, carry):
                if not square:
                    tensor_copy(blocks, what, i).wait_recv()
                copy = pltpu.make_async_copy(
                    arrived.at[what, first + i], xs.at[what * count + i, :, pl.ds(0, size)], load_sem
                )
                copy.start()
                copy.wait()
                return carry

            lax.fori_loop(0, count, one, 0)

        def summed(what, r, rows):
            value = held[what, r]
            for i in range(count):
                value += xs[what * count + i, rows, :size].astype(jnp.float32)
            return value

        gain = vec_ref[NIN + 1 : NIN + 2, columns]
        ones = jnp.ones((8, size), jnp.float32)

        def unit_of(rows):
            token = xs[tok_at, rows, :size].astype(jnp.float32)
            return (token - stats[rows, 0:1]) * stats[rows, 1:2]

        rest(1)
        collect(0)

        def first_pass(r, carry):
            rows = pl.ds(pl.multiple_of(r * HID, HID), HID)
            grad = summed(0, r, rows)
            held[0, r] = grad
            unit = unit_of(rows)
            scaled = grad * gain
            sums[0:8, rows] = lax.dot_general(
                ones, scaled, NT, precision=lax.Precision.HIGHEST, preferred_element_type=jnp.float32
            )
            sums[8:16, rows] = lax.dot_general(
                ones, scaled * unit, NT, precision=lax.Precision.HIGHEST, preferred_element_type=jnp.float32
            )
            vec[NIN + 1 : NIN + 2, :] += jnp.sum(grad * unit, 0, keepdims=True)
            vec[NIN + 2 : NIN + 3, :] += jnp.sum(grad, 0, keepdims=True)
            return carry

        lax.fori_loop(0, rows_all // HID, first_pass, 0)
        for i in range(peers - 1):
            sums_copy(i).start()
        to_core = pltpu.make_async_remote_copy(
            src_ref=vec, dst_ref=vec_core, send_sem=vsend_sem.at[0], recv_sem=vrecv_sem.at[0],
            device_id=other_core, device_id_type=MESH,
        )
        to_core.start()
        rest(2)
        for i in range(peers - 1):
            sums_copy(i).wait_recv()
        inv_width = 1.0 / width

        def second_pass(r, carry):
            rows = pl.ds(pl.multiple_of(r * HID, HID), HID)
            means = sums[:, rows]
            for i in range(peers - 1):
                means += sums_in[i, :, rows]
            means = (means * inv_width).T
            unit = unit_of(rows)
            held[0, r] = stats[rows, 1:2] * (
                held[0, r] * gain - means[:, 0:1] - unit * means[:, 8:9]
            ) + xs[cot_at, rows, :size].astype(jnp.float32)
            return carry

        lax.fori_loop(0, rows_all // HID, second_pass, 0)
        put_grad = pltpu.make_async_copy(held.at[0, pl.ds(0, rows_all // HID)], token_grad, out_sem.at[0])
        put_grad.start()

        rest(3)
        to_core.wait_recv()
        vec_line[z] = vec[...] + vec_core[...]

        def along_dp(i):
            return pltpu.make_async_remote_copy(
                src_ref=vec_line.at[z], dst_ref=vec_line.at[z],
                send_sem=vsend_sem.at[1 + i], recv_sem=vrecv_sem.at[1 + i],
                device_id={"dp": lax.rem(z + 1 + i, n)}, device_id_type=MESH,
            )

        def from_dp(i):
            there = lax.rem(z + n - 1 - i, n)
            return pltpu.make_async_remote_copy(
                src_ref=vec_line.at[there], dst_ref=vec_line.at[there],
                send_sem=vsend_sem.at[1 + i], recv_sem=vrecv_sem.at[1 + i],
                device_id={"dp": lax.rem(z + 1 + i, n)}, device_id_type=MESH,
            )

        for i in range(n - 1):
            along_dp(i).start()
        for i in range(n - 1):
            from_dp(i).wait_recv()
        vec_sum = vec_line[0]
        for i in range(1, n):
            vec_sum += vec_line[i]
        vec_all[tensor] = vec_sum

        def along_tensor(i):
            return pltpu.make_async_remote_copy(
                src_ref=vec_all.at[tensor], dst_ref=vec_all.at[tensor],
                send_sem=vsend_sem.at[n + i], recv_sem=vrecv_sem.at[n + i],
                device_id={"tensor": lax.rem(tensor + 1 + i, peers)}, device_id_type=MESH,
            )

        def from_tensor(i):
            there = lax.rem(tensor + peers - 1 - i, peers)
            return pltpu.make_async_remote_copy(
                src_ref=vec_all.at[there], dst_ref=vec_all.at[there],
                send_sem=vsend_sem.at[n + i], recv_sem=vrecv_sem.at[n + i],
                device_id={"tensor": lax.rem(tensor + 1 + i, peers)}, device_id_type=MESH,
            )

        for i in range(peers - 1):
            along_tensor(i).start()

        rest(4)
        collect(1)
        out_bias = vec_ref[NIN : NIN + 1, columns]

        def third_pass(r, carry):
            rows = pl.ds(pl.multiple_of(r * HID, HID), HID)
            value = xs[tok_at, rows, :size].astype(jnp.float32) + (summed(1, r, rows) + out_bias)
            xs[out_at, rows, :size] = value.astype(jnp.bfloat16)
            return carry

        lax.fori_loop(0, rows_all // HID, third_pass, 0)
        put_result = pltpu.make_async_copy(xs.at[out_at, :, pl.ds(0, size)], result, out_sem.at[1])
        put_result.start()
        rest(5)

        for i in range(peers - 1):
            from_tensor(i).wait_recv()
        vec_grad[...] = vec_all[...]
        put_grad.wait()
        put_result.wait()
        to_core.wait_send()
        for i in range(n - 1):
            along_dp(i).wait_send()
        for i in range(peers - 1):
            along_tensor(i).wait_send()
            sums_copy(i).wait_send()
        for i in range(6 if square else peers - 1):
            tensor_copy(blocks, 0, i).wait_send()
            tensor_copy(blocks, 1, i).wait_send()

    low, wide = jnp.bfloat16, jnp.float32
    window, qblock = rows_all + 256, 256
    pl.run_scoped(
        forward_backward,
        pltpu.VMEM((rows_all, width), low),
        pltpu.VMEM((rows_all, width), low),
        pltpu.VMEM((2, rows_all // 8, width), low),
        pltpu.VMEM((2, size, ATT), wide),
        pltpu.VMEM((2, HID, size), wide),
        pltpu.VMEM((2, size, WIDE), low),
        pltpu.VMEM((n, size, WIDE), low),
        pltpu.VMEM((rows_all, WIDE), low),
        pltpu.VMEM((2, rows_all, LANES), low),
        pltpu.VMEM((2, 2 * rows_all, LANES), wide),
        pltpu.VMEM((2, 256, LANES), wide),
        pltpu.VMEM((2, rows_all, LANES), wide),
        pltpu.VMEM((window, qblock), wide),
        pltpu.VMEM((2, n, HID, size), low),
        pltpu.VMEM((n, HID, size), low),
    )
    pl.run_scoped(
        finals,
        pltpu.VMEM((max(units, 2 * peers + 1), rows_all, WIDE), low),
        pltpu.VMEM((2, units, size // 2, WIDE), low),
        pltpu.VMEM((2, peers - 1, rows_all, size), low),
        pltpu.VMEM((n, HID, size), low),
        pltpu.VMEM((rows_all // 2, size), low),
    )


    def drain_kv(s, carry):
        send_kv(s).wait_send()
        return carry

    lax.fori_loop(0, steps, drain_kv, 0)

    def drain(m, carry):
        g, s = m // last, m % last + 1

        @pl.when(s == 1)
        def _():
            @pl.when(z < last)
            def _():
                hop(0, g, 0, z).wait_send()

            @pl.when(z > 0)
            def _():
                hop(1, g, 0, z).wait_send()

            @pl.when(g >= units - boxes)
            def _():
                keep(g).wait()
                share(g, my_part).wait_send()

            share(g, their_part).wait_recv()

        @pl.when(z >= s)
        def _():
            @pl.when(z < last)
            def _():
                hop(0, g, s, z - s).wait_send()

            across(0, g, s - 1, z - s, mine).wait_send()

        @pl.when(z + s <= last)
        def _():
            @pl.when(z > 0)
            def _():
                hop(1, g, s, z + s).wait_send()

            across(1, g, s - 1, z + s, mine).wait_send()

        for way in range(2):
            distance = z if way == 0 else last - z

            @pl.when(distance < last - (s - 1))
            def _():
                pass_on(way, g, s - 1).wait_send()

        return carry

    lax.fori_loop(0, units * last, drain, 0)


def run_block(in_weight, out_weight, tokens, cotangent, bias, vectors, cosine, sine, begin):
    n, peers = lax.axis_size("dp"), lax.axis_size("tensor")
    size, cols_all = in_weight.shape[1:]
    steps = cols_all // LANES
    units = 3 * steps
    rows, width = tokens.shape
    assert width == n * size == peers * cols_all and size == cols_all and rows <= n * HID
    low, wide = jnp.bfloat16, jnp.float32
    anywhere = pl.BlockSpec(memory_space=pl.ANY)
    vm = pl.BlockSpec(memory_space=pltpu.VMEM)
    dma = pltpu.SemaphoreType.DMA
    return pl.pallas_call(
        functools.partial(block_kernel, n, steps, peers),
        out_shape=(
            jax.ShapeDtypeStruct((units, n, size, WIDE), low),
            jax.ShapeDtypeStruct((units, rows, WIDE), low),
            jax.ShapeDtypeStruct((units, WIDE, size), wide),
            jax.ShapeDtypeStruct((units, n, HID, size), low),
            jax.ShapeDtypeStruct((units, n, HID, size), wide),
            jax.ShapeDtypeStruct((steps, 2, rows, LANES), wide),
            jax.ShapeDtypeStruct((2, peers - 1, rows, size), low),
            jax.ShapeDtypeStruct((rows, size), low),
            jax.ShapeDtypeStruct((rows // HID, HID, size), wide),
            jax.ShapeDtypeStruct((peers, 16, size), wide),
        ),
        in_specs=[anywhere] * 4 + [vm] * 5,
        out_specs=[anywhere] * 9 + [vm],
        scratch_shapes=[
            pltpu.VMEM((steps, 2, 2 * rows, LANES), low),
            pltpu.VMEM((steps, 2, 256, LANES), low),
            pltpu.VMEM((steps, 2, 256, LANES), wide),
            pltpu.VMEM((steps, 2, 256, LANES), wide),
            pltpu.VMEM((2, n, HID, size), wide),
            pltpu.VMEM((2, 2, HID, size), wide),
            pltpu.VMEM((units, n + 1, HID, size), low),
            pltpu.VMEM((3, HID, size), wide),
            pltpu.VMEM((rows, LANES), wide),
            pltpu.VMEM((16, size), wide),
            pltpu.VMEM((16, size), wide),
            pltpu.VMEM((n, 16, size), wide),
            pltpu.VMEM((peers, 16, size), wide),
            pltpu.VMEM((16, rows), wide),
            pltpu.VMEM((peers - 1, 16, rows), wide),
            dma((2, units, n)),
            dma((2, units, n)),
            dma((2, units, n)),
            dma((2, units, n)),
            dma((units,)),
            dma((units,)),
            dma((2, units, n - 1)),
            dma((2, units, n - 1)),
            dma((units,)),
            dma((units,)),
            dma((units,)),
            dma((steps,)),
            dma((steps,)),
            dma((steps,)),
            dma((steps,)),
            dma((steps,)),
            dma((steps,)),
            dma((steps,)),
            dma((steps,)),
            dma((steps,)),
            dma((steps,)),
            dma,
            dma,
            dma,
            dma((2, 4)),
            dma((2,)),
            dma((2,)),
            dma,
            dma((2,)),
            dma((2, 2)),
            dma((3,)),
            dma((2, 6 if peers == 4 else peers - 1)),
            dma((2, 6 if peers == 4 else peers - 1)),
            dma((peers - 1,)),
            dma((peers - 1,)),
            dma((n + peers - 1,)),
            dma((n + peers - 1,)),
            dma((2,)),
            dma((2,)),
        ],
        compiler_params=pltpu.CompilerParams(
            collective_id=1, has_side_effects=True, vmem_limit_bytes=VMEM_LIMIT
        ),
        name="parallel_block",
    )(in_weight, out_weight, tokens, cotangent, bias, vectors, cosine, sine, begin)


def adam_kernel(into, chunks, *refs):
    pieces, refs = refs[:chunks], refs[chunks:]
    g = pl.program_id(0)

    def update(weights, turned):
        w, m, v, new_w, new_m, new_v = weights
        for c, piece in enumerate(pieces):
            part = slice(c * LANES, (c + 1) * LANES)
            at = (0, part) if turned else (0, slice(None), part)
            gradient = piece[0] if turned else piece[0].T
            new_w[at], new_m[at], new_v[at] = adamw(
                w[at], gradient, m[at], v[at], rate_matrix, weight_decay
            )

    @pl.when(g < into)
    def _():
        update(refs[:3] + refs[6:9], False)

    @pl.when(g >= into)
    def _():
        update(refs[3:6] + refs[9:], True)


def adam_weights(total, in_arrays, out_arrays):
    into, size, cols_all = in_arrays[0].shape
    outof = out_arrays[0].shape[0]
    chunks = cols_all // LANES

    def place(c, g):
        is_in = g < into
        group = jnp.where(is_in, g, g - into)
        lead = jnp.where(is_in, 3, 1)
        i = jnp.maximum((group - lead) * cols_all + c * LANES, 0) // HID
        unit = jnp.where(group < lead, 3 * c + 1, 3 * (i // 2) + 2 * (i % 2))
        lane = jnp.where(
            group < lead, jnp.where(is_in, group, 3), c % 2 + jnp.where(is_in, 0, 2)
        )
        return unit, lane, 0

    in_spec = pl.BlockSpec((1, size, cols_all), lambda g: (jnp.minimum(g, into - 1), 0, 0))
    out_spec = pl.BlockSpec((1, cols_all, size), lambda g: (jnp.maximum(g - into, 0), 0, 0))
    results = pl.pallas_call(
        functools.partial(adam_kernel, into, chunks),
        grid=(into + outof,),
        out_shape=tuple(jax.ShapeDtypeStruct(v.shape, jnp.float32) for v in in_arrays + out_arrays),
        in_specs=[pl.BlockSpec((1, LANES, size), functools.partial(place, c)) for c in range(chunks)]
        + [in_spec] * 3
        + [out_spec] * 3,
        out_specs=[in_spec] * 3 + [out_spec] * 3,
        compiler_params=pltpu.CompilerParams(vmem_limit_bytes=VMEM_LIMIT),
        name="adam_weights",
    )(*[total] * chunks, *in_arrays, *out_arrays)
    return results[:3], results[3:]


def layout(lengths_row, row_span):
    seg_ends = jnp.cumsum(lengths_row)
    seg_starts = seg_ends - lengths_row
    places = jnp.arange(row_span, dtype=jnp.int32)
    segment = jnp.sum((places[:, None] >= seg_ends[None, :]).astype(jnp.int32), 1)
    numbers = jnp.arange(lengths_row.shape[0], dtype=jnp.int32)
    return jnp.sum(jnp.where(segment[:, None] == numbers[None, :], seg_starts[None, :], 0), 1)


def rope_tables(places):
    half_rot = ROT // 2
    lane = jnp.arange(2 * HD, dtype=jnp.int32) % HD
    exponent = (lane % half_rot).astype(jnp.float32)
    frequency = 10000.0 ** (-2.0 * exponent / ROT)
    angles = places.astype(jnp.float32)[:, None] * frequency[None, :]
    turned = (lane < ROT)[None, :]
    cosine = jnp.where(turned, jnp.cos(angles), 1.0)
    sine = jnp.where(turned, jnp.sin(angles), 0.0)
    return cosine, sine


def body(
    tokens,
    cotangent,
    lengths,
    in_weight,
    out_weight,
    vectors,
    in_first,
    in_second,
    out_first,
    out_second,
    vec_first,
    vec_second,
):
    local_rows, model_width = tokens.shape
    slice_width = in_weight.shape[2]
    context_count = lax.axis_size("context")
    context_index = lax.axis_index("context")
    tensor_index = lax.axis_index("tensor")
    row_span = local_rows * context_count
    first_row = context_index * local_rows
    begin_all = layout(lengths[0], row_span)
    begin = lax.dynamic_slice_in_dim(begin_all, first_row, local_rows, 0)
    places = first_row + jnp.arange(local_rows, dtype=jnp.int32) - begin
    tables = rope_tables(places)

    column = tensor_index * slice_width
    in_bias = lax.dynamic_slice_in_dim(vectors[:NIN], column, slice_width, 1)
    steps = slice_width // LANES
    hid_bias = in_bias[3:].reshape(steps, 2, HID)
    att_bias = in_bias[:3].reshape(3, steps, LANES).transpose(1, 0, 2).reshape(steps, ATT)
    bias = jnp.stack(
        [
            jnp.pad(hid_bias[:, 0], ((0, 0), (0, WIDE - HID))),
            jnp.pad(att_bias, ((0, 0), (0, WIDE - ATT))),
            jnp.pad(hid_bias[:, 1], ((0, 0), (0, WIDE - HID))),
        ],
        1,
    ).reshape(3 * steps, 1, WIDE)
    by_group = jnp.transpose(in_weight, (1, 0, 2))
    _, _, total, _, _, _, _, result, token_grad, vec_grad = run_block(
        by_group, out_weight, tokens, cotangent, bias, vectors, tables[0], tables[1], begin_all[None]
    )
    token_grad = token_grad.reshape(local_rows, slice_width)
    vector_grad = jnp.transpose(vec_grad, (1, 0, 2)).reshape(-1, model_width)[: NIN + 3]
    new_vectors, new_vec_first, new_vec_second = adamw(
        vectors, vector_grad, vec_first, vec_second, rate_vector, 0.0
    )
    by_group_moments = [jnp.transpose(v, (1, 0, 2)) for v in (in_first, in_second)]
    new_by_group, (new_out, new_out_first, new_out_second) = adam_weights(
        total, [by_group] + by_group_moments, [out_weight, out_first, out_second]
    )
    new_in, new_in_first, new_in_second = (jnp.transpose(v, (1, 0, 2)) for v in new_by_group)
    return (
        result,
        token_grad,
        new_in,
        new_in_first,
        new_in_second,
        new_out,
        new_out_first,
        new_out_second,
        new_vectors,
        new_vec_first,
        new_vec_second,
    )


def solution(mesh):
    return jax.shard_map(
        body,
        mesh=mesh,
        in_specs=(
            P(("dp", "context"), None),
            P(("dp", "context"), None),
            P("dp", None),
            P("dp", None, "tensor"),
            P(None, "tensor", "dp"),
            P(),
            P("dp", None, "tensor"),
            P("dp", None, "tensor"),
            P(None, "tensor", "dp"),
            P(None, "tensor", "dp"),
            P(),
            P(),
        ),
        out_specs=(
            P(("dp", "context"), "tensor"),
            P(("dp", "context"), "tensor"),
            P("dp", None, "tensor"),
            P("dp", None, "tensor"),
            P("dp", None, "tensor"),
            P(None, "tensor", "dp"),
            P(None, "tensor", "dp"),
            P(None, "tensor", "dp"),
            P(),
            P(),
            P(),
        ),
        check_vma=False,
    )
```

```python
import functools

import jax
import jax.numpy as jnp
from jax import lax
from jax.experimental import pallas as pl
from jax.experimental.pallas import tpu as pltpu
from jax.sharding import PartitionSpec as P

HD = 64
ROT = 32
STEP = 10
NIN = 7
MESH = pl.DeviceIdType.MESH
VMEM_LIMIT = 60 * 2**20

norm_eps = 1e-05
beta_one = 0.9
beta_two = 0.95
adam_eps = 1e-08
weight_decay = 0.1
rate_matrix = 0.02
rate_vector = 0.4


def adamw(master, gradient, moment_one, moment_two, step_rate, decay_rate):
    first_new = beta_one * moment_one + (1.0 - beta_one) * gradient
    second_new = beta_two * moment_two + (1.0 - beta_two) * gradient * gradient
    first_hat = first_new * (1.0 / (1.0 - beta_one**STEP))
    second_hat = second_new * (1.0 / (1.0 - beta_two**STEP))
    updated = master - step_rate * (
        first_hat / (jnp.sqrt(second_hat) + adam_eps) + decay_rate * master
    )
    return (updated, first_new, second_new)


LANES = 2 * HD
WIDE = 4 * LANES
HID = WIDE // 2
ATT = 3 * LANES
LAG = 5

NT = (((1,), (1,)), ((), ()))
NN = (((1,), (0,)), ((), ()))
TN = (((0,), (0,)), ((), ()))


def dot(x, y, dims=NN):
    return lax.dot_general(x, y, dims, preferred_element_type=jnp.float32)


def greet(n, peers):
    z = lax.axis_index("dp")
    k = lax.axis_index("context")
    t = lax.axis_index("tensor")
    barrier = pltpu.get_barrier_semaphore()
    pl.semaphore_signal(barrier, inc=1, device_id={"context": 1 - k}, device_id_type=MESH)
    for i in range(1, n):
        pl.semaphore_signal(barrier, inc=1, device_id={"dp": lax.rem(z + i, n)}, device_id_type=MESH)
    for i in range(1, peers):
        pl.semaphore_signal(
            barrier, inc=1, device_id={"tensor": lax.rem(t + i, peers)}, device_id_type=MESH
        )
    pl.semaphore_wait(barrier, n + peers - 1)


def gelu_both(v):
    rate = 0.7978845608028654
    t = jnp.tanh(rate * (v + 0.044715 * (v * v * v)))
    value = 0.5 * v * (1.0 + t)
    slope = 0.5 * (1.0 + t) + 0.5 * v * (1.0 - t * t) * (rate * (1.0 + 3.0 * 0.044715 * (v * v)))
    return value, slope


def schedule(n):
    last = n - 1
    per_step = 3 * last
    in_hidden = 2 * per_step // 9
    in_attention = per_step - 2 * in_hidden
    done = (in_hidden, in_hidden + in_attention, per_step)
    lead = max([last * (n + i) - done[i] for i in range(3)] + [last * (n - 1)])
    out_hidden, out_attention = in_hidden, in_attention
    behind = 1 + max(out_hidden + last, out_hidden + out_attention, 2 * out_hidden + out_attention - last)
    return per_step, in_hidden, in_attention, lead, out_hidden, out_attention, behind


def block_kernel(
    n, steps, peers,
    in_w, out_w, tokens, cot_hbm, bias_ref, vec_ref, cos_ref, sin_ref, begin_ref,
    full, saved, total, swap, kept, dkv_other, arrived, result, token_grad, vec_grad,
    kv, moved, returned, extra, held, pieces, line, outbox, stats, vec, vec_core, vec_line, vec_all, sums, sums_in,
    send_sem, recv_sem, psend_sem, precv_sem,
    xsend_sem, xrecv_sem, lsend_sem, lrecv_sem, keep_sem, fsend_sem, frecv_sem,
    kvsend_sem, kvrecv_sem, dsend_sem, drecv_sem, msend_sem, mrecv_sem, bsend_sem, brecv_sem, esend_sem, erecv_sem, load_sem, save_sem, weight_sem, pack_sem, put_sem, rows_sem, swap_sem, held_sem, piece_sem, box_sem,
    tsend_sem, trecv_sem, ssend_sem, srecv_sem, vsend_sem, vrecv_sem, tile_sem, out_sem,
):
    units = 3 * steps
    last = n - 1
    per_step, in_hidden, in_attention, lead, out_hidden, out_attention, behind = schedule(n)
    depth, boxes = 2, 3
    size, cols_all = in_w.shape[1], in_w.shape[2]
    half = size // 2
    rows_all, width = tokens.shape
    tensor = lax.axis_index("tensor")
    columns = pl.ds(pl.multiple_of(tensor * size, size), size)
    z = lax.axis_index("dp")
    k = lax.axis_index("context")
    mine = pl.ds(pl.multiple_of(k * half, half), half)
    theirs = pl.ds(pl.multiple_of((1 - k) * half, half), half)
    other_core = {"context": 1 - k}
    greet(n, peers)


    def hop(way, g, h, shard):
        return pltpu.make_async_remote_copy(
            src_ref=full.at[g, shard, mine],
            dst_ref=full.at[g, shard, mine],
            send_sem=send_sem.at[way, g, h],
            recv_sem=recv_sem.at[way, g, h],
            device_id={"dp": z + 1 - 2 * way},
            device_id_type=MESH,
        )

    def across(way, g, h, shard, rows):
        return pltpu.make_async_remote_copy(
            src_ref=full.at[g, shard, rows],
            dst_ref=full.at[g, shard, rows],
            send_sem=psend_sem.at[way, g, h],
            recv_sem=precv_sem.at[way, g, h],
            device_id=other_core,
            device_id_type=MESH,
        )

    def send_own(g):
        @pl.when(z < last)
        def _():
            hop(0, g, 0, z).start()

        @pl.when(z > 0)
        def _():
            hop(1, g, 0, z).start()

    def gather_tick(m):
        s = m % last + 1
        g = m // last - (s - 1)

        @pl.when((s == 1) & (g < units - 1))
        def _():
            send_own(g + 1)

        @pl.when((g >= 0) & (g < units))
        def _():
            @pl.when(z >= s)
            def _():
                hop(0, g, s - 1, z - s).wait_recv()

                @pl.when(z < last)
                def _():
                    hop(0, g, s, z - s).start()

                across(0, g, s - 1, z - s, mine).start()

            @pl.when(z + s <= last)
            def _():
                hop(1, g, s - 1, z + s).wait_recv()

                @pl.when(z > 0)
                def _():
                    hop(1, g, s, z + s).start()

                across(1, g, s - 1, z + s, mine).start()

    def need(u):
        def one(i, carry):
            s = i + 1

            @pl.when(z >= s)
            def _():
                across(0, u, s - 1, z - s, theirs).wait_recv()

            @pl.when(z + s <= last)
            def _():
                across(1, u, s - 1, z + s, theirs).wait_recv()

            return carry

        lax.fori_loop(0, last, one, 0)

    def send_kv(s):
        rows = pl.ds(pl.multiple_of(k * rows_all, rows_all), rows_all)
        return pltpu.make_async_remote_copy(
            src_ref=kv.at[s, :, rows],
            dst_ref=kv.at[s, :, rows],
            send_sem=kvsend_sem.at[s],
            recv_sem=kvrecv_sem.at[s],
            device_id=other_core,
            device_id_type=MESH,
        )


    def exchange_from(outgoing, g):
        return pltpu.make_async_remote_copy(
            src_ref=outgoing,
            dst_ref=swap.at[g],
            send_sem=xsend_sem.at[g],
            recv_sem=xrecv_sem.at[g],
            device_id=other_core,
            device_id_type=MESH,
        )

    def slot_of(way, i):
        return i if way == 0 else n - i

    def pass_on(way, g, i):
        slot = slot_of(way, i)
        return pltpu.make_async_remote_copy(
            src_ref=line.at[g, slot],
            dst_ref=line.at[g, slot],
            send_sem=lsend_sem.at[way, g, i],
            recv_sem=lrecv_sem.at[way, g, i],
            device_id={"dp": z + 1 - 2 * way},
            device_id_type=MESH,
        )

    my_part = pl.ds(pl.multiple_of(k * HID, HID), HID)
    their_part = pl.ds(pl.multiple_of((1 - k) * HID, HID), HID)

    def keep(g):
        return pltpu.make_async_copy(outbox.at[g % boxes], total.at[g, my_part], keep_sem.at[g])

    def share(g, rows):
        return pltpu.make_async_remote_copy(
            src_ref=outbox.at[g % boxes],
            dst_ref=total.at[g, rows],
            send_sem=fsend_sem.at[g],
            recv_sem=frecv_sem.at[g],
            device_id=other_core,
            device_id_type=MESH,
        )

    def fetch_swapped(g, swap_in):
        @pl.when(g >= 0)
        def _():
            exchange_from(swap_in, g).wait_recv()
            pltpu.make_async_copy(swap.at[g], swap_in, swap_sem).start()

    def put_held(g):
        return pltpu.make_async_copy(held.at[g % depth], kept.at[g], held_sem.at[g % depth])

    def prepare(g, swap_in):
        @pl.when(g >= 0)
        def _():
            pltpu.make_async_copy(swap.at[g], swap_in, swap_sem).wait()

            def one(j, carry):
                held[g % depth, j] += swap_in[j].astype(jnp.float32)
                return carry

            lax.fori_loop(0, n, one, 0)
            put_held(g).start()

    def wait_put(g):
        @pl.when(g >= 0)
        def _():
            put_held(g).wait()

    def piece_copy(way, g, i, slot):
        shard = n - 1 - i if way == 0 else i
        return pltpu.make_async_copy(kept.at[g, shard], pieces.at[way, slot], piece_sem.at[way, slot])

    def box_copy(g):
        return pltpu.make_async_copy(kept.at[g, z], outbox.at[g % boxes], box_sem.at[g % boxes])

    def needs(way, t):
        distance = z if way == 0 else last - z
        m = t - LAG * distance
        g, i = m // last, m % last
        return g, i, (m >= 0) & (m < units * last) & (distance < last - i)

    def fetch_pieces(t):
        for way in range(2):
            g, i, needed = needs(way, t)

            @pl.when(needed)
            def _():
                piece_copy(way, g, i, t % 2).start()

        done = t - last * LAG

        @pl.when((done >= 0) & (done % last == 0))
        def _():
            g = done // last

            @pl.when(g >= boxes)
            def _():
                keep(g - boxes).wait()
                share(g - boxes, my_part).wait_send()

            box_copy(g).start()

    def scatter_step(way, t):
        distance = z if way == 0 else last - z
        m = t - LAG * distance
        g, i, needed = needs(way, t)
        slot = slot_of(way, i)

        @pl.when(needed)
        def _():
            piece_copy(way, g, i, t % 2).wait()

        @pl.when((m >= 0) & (m < units * last) & (distance > 0) & (distance <= last - i))
        def _():
            pass_on(way, g, i).wait_recv()

        @pl.when(needed)
        def _():
            @pl.when(distance == 0)
            def _():
                line[g, slot] = pieces[way, t % 2].astype(jnp.bfloat16)

            @pl.when(distance > 0)
            def _():
                line[g, slot] = (line[g, slot].astype(jnp.float32) + pieces[way, t % 2]).astype(jnp.bfloat16)

            pass_on(way, g, i).start()

    def finish(g):
        box = g % boxes
        box_copy(g).wait()

        @pl.when(z > 0)
        def _():
            outbox[box] += line[g, slot_of(0, n - 1 - z)].astype(jnp.float32)

        @pl.when(z < last)
        def _():
            outbox[box] += line[g, slot_of(1, z)].astype(jnp.float32)

        keep(g).start()
        share(g, my_part).start()

    def scatter_tick(t):
        fetch_pieces(t + 1)
        scatter_step(0, t)
        scatter_step(1, t)
        done = t - last * LAG

        @pl.when((done >= 0) & (done % last == 0))
        def _():
            finish(done // last)

    def run_ticks(gather_from, gather_count, scatter_from, scatter_count):
        def one_gather(i, carry):
            gather_tick(gather_from + i)
            return carry

        def one_scatter(i, carry):
            scatter_tick(scatter_from + i)
            return carry

        lax.fori_loop(0, gather_count, one_gather, 0)
        lax.fori_loop(0, scatter_count, one_scatter, 0)

    def forward_backward(
        normed, cot, stage, raw_in, raw_out, packed, wbuf, x, qg, dkv, back, dkv_tmp, mask, outgoing, swap_in
    ):

        def exchange(g):
            return exchange_from(outgoing.at[g % 2], g)

        ticks = run_ticks

        part = stage.shape[1]
        norm_blocks = rows_all // part

        def fetch_rows(i):
            rows = pl.ds(pl.multiple_of(i * part, part), part)
            return pltpu.make_async_copy(tokens.at[rows], stage.at[i % 2], rows_sem.at[i % 2])

        def normalize(i):
            @pl.when(i + 1 < norm_blocks)
            def _():
                fetch_rows(i + 1).start()

            fetch_rows(i).wait()

            def few(r, c):
                sub = pl.ds(pl.multiple_of(r * 64, 64), 64)
                there = pl.ds(pl.multiple_of(i * part + r * 64, 64), 64)
                inputs = stage[i % 2, sub, :].astype(jnp.float32)
                centered = inputs - jnp.mean(inputs, 1, keepdims=True)
                inv_dev = lax.rsqrt(jnp.mean(centered * centered, 1, keepdims=True) + norm_eps)
                normed[there, :] = (
                    centered * inv_dev * vec_ref[NIN + 1 : NIN + 2, :] + vec_ref[NIN + 2 : NIN + 3, :]
                ).astype(jnp.bfloat16)
                lane = lax.broadcasted_iota(jnp.int32, (64, LANES), 1)
                stats[there, :] = jnp.where(lane == 0, jnp.mean(inputs, 1, keepdims=True), inv_dev)
                return c

            lax.fori_loop(0, part // 64, few, 0)

        def hidden_place(i):
            return i * HID // cols_all, pl.multiple_of(i * HID % cols_all, HID)

        def fetch_raw(u, start):
            s, slot = u // 3, u % 2

            def each(copies):
                for copy in copies:
                    copy.start() if start else copy.wait()

            @pl.when(u % 3 == 1)
            def _():
                cols = pl.ds(pl.multiple_of(s * LANES, LANES), LANES)
                each(
                    [
                        pltpu.make_async_copy(
                            in_w.at[g, :, cols],
                            raw_in.at[slot, :, pl.ds(g * LANES, LANES)],
                            pack_sem.at[slot, g],
                        )
                        for g in range(3)
                    ]
                    + [
                        pltpu.make_async_copy(
                            out_w.at[0, cols], raw_out.at[slot, pl.ds(0, LANES)], pack_sem.at[slot, 3]
                        )
                    ]
                )

            @pl.when(u % 3 != 1)
            def _():
                group, first = hidden_place(2 * s + (u % 3) // 2)
                cols = pl.ds(first, HID)
                each(
                    [
                        pltpu.make_async_copy(
                            in_w.at[3 + group, :, cols],
                            raw_in.at[slot, :, pl.ds(0, HID)],
                            pack_sem.at[slot, 0],
                        ),
                        pltpu.make_async_copy(out_w.at[1 + group, cols], raw_out.at[slot], pack_sem.at[slot, 1]),
                    ]
                )

        def put_packed(u):
            return pltpu.make_async_copy(packed.at[u % 2], full.at[u, z], put_sem.at[u % 2])

        def pack(u):
            slot = u % 2
            fetch_raw(u, False)

            @pl.when(u % 3 == 1)
            def _():
                packed[slot, :, :ATT] = raw_in[slot].astype(jnp.bfloat16)
                packed[slot, :, ATT:] = raw_out[slot, :LANES, :].astype(jnp.bfloat16).T

            @pl.when(u % 3 != 1)
            def _():
                packed[slot, :, :HID] = raw_in[slot, :, :HID].astype(jnp.bfloat16)
                packed[slot, :, HID:] = raw_out[slot].astype(jnp.bfloat16).T

            put_packed(u).start()

        def fetch_weights(u):
            return pltpu.make_async_copy(full.at[u], wbuf, weight_sem)

        def next_weights(u):
            @pl.when(u < units)
            def _():
                need(u)
                fetch_weights(u).start()

        def column_sums(split):
            ones = jnp.ones((8, rows_all), jnp.bfloat16)
            return dot(ones, x[:, :split])[0:1, :]

        def save(u):
            return pltpu.make_async_copy(x, saved.at[u], save_sem)

        def wait_saved(u):
            @pl.when(u > 0)
            def _():
                save(u - 1).wait()

        def gradients(u, split):
            @pl.when(u >= 2)
            def _():
                exchange(u - 2).wait_send()

            def part(first, end, j):
                turns = [(first, min(end, split), normed), (max(first, split), end, cot)]
                return [
                    (low, high, dot(x[:, low:high], rows[:, pl.ds(pl.multiple_of(j * size, size), size)], TN))
                    for low, high, rows in turns
                    if low < high
                ]

            for core in range(2):

                @pl.when(k == core)
                def _():
                    def one(j, carry):
                        for low, high, value in part(core * HID, (core + 1) * HID, j):
                            held[u % depth, j, low - core * HID : high - core * HID] = value
                        for low, high, value in part((1 - core) * HID, (2 - core) * HID, j):
                            outgoing[u % 2, j, low - (1 - core) * HID : high - (1 - core) * HID] = value.astype(
                                jnp.bfloat16
                            )
                        return carry

                    lax.fori_loop(0, n, one, 0)

            exchange(u).start()

        block = min(512, rows_all)

        def hidden_unit(u, i_hidden, at, out_at):
            fetch_weights(u).wait()
            wait_saved(u)
            wait_put(u - 2)

            def one(i, carry):
                rows = pl.ds(pl.multiple_of(i * block, block), block)
                pre = dot(normed[rows, :], wbuf[:, :, :HID].reshape(width, HID)) + bias_ref[u][:, :HID]
                value, slope = gelu_both(pre)
                x[rows, HID:] = value.astype(jnp.bfloat16)
                grad = dot(cot[rows, :], wbuf[:, :, HID:].reshape(width, HID))
                x[rows, :HID] = (grad * slope).astype(jnp.bfloat16)
                return carry

            lax.fori_loop(0, rows_all // block, one, 0)
            save(u).start()
            fetch_swapped(u - 1, swap_in)

            ticks(at + lead, in_hidden, out_at - behind, out_hidden)
            next_weights(u + 1)
            prepare(u - 1, swap_in)
            group, first = hidden_place(i_hidden)
            vec[pl.ds(3 + group, 1), pl.ds(first, HID)] = column_sums(HID)
            gradients(u, HID)


        qblock = mask.shape[1]
        window = mask.shape[0]
        qblocks = rows_all // qblock

        def rope(v, rows, sign):
            half_rot = ROT // 2
            lane = lax.broadcasted_iota(jnp.int32, v.shape, 1) % HD
            ahead = pltpu.roll(v, LANES - half_rot, 1)
            behind = pltpu.roll(v, half_rot, 1)
            other = jnp.where(lane < half_rot, -ahead, behind)
            return v * cos_ref[rows, :] + other * (sign * sin_ref[rows, :])

        def recv_kv(s):
            rows = pl.ds(pl.multiple_of((1 - k) * rows_all, rows_all), rows_all)
            return pltpu.make_async_remote_copy(
                src_ref=kv.at[s, :, rows],
                dst_ref=kv.at[s, :, rows],
                send_sem=kvsend_sem.at[s],
                recv_sem=kvrecv_sem.at[s],
                device_id=other_core,
                device_id_type=MESH,
            )

        def send_dkv(s):
            return pltpu.make_async_remote_copy(
                src_ref=dkv.at[:, pl.ds(0, rows_all)],
                dst_ref=dkv_other.at[s],
                send_sem=dsend_sem.at[s],
                recv_sem=drecv_sem.at[s],
                device_id=other_core,
                device_id_type=MESH,
            )

        def send_first(s):
            return pltpu.make_async_remote_copy(
                src_ref=qg.at[:, pl.ds(0, qblock)],
                dst_ref=moved.at[s],
                send_sem=msend_sem.at[s],
                recv_sem=mrecv_sem.at[s],
                device_id=other_core,
                device_id_type=MESH,
            )

        def send_back(s):
            return pltpu.make_async_remote_copy(
                src_ref=back,
                dst_ref=returned.at[s],
                send_sem=bsend_sem.at[s],
                recv_sem=brecv_sem.at[s],
                device_id=other_core,
                device_id_type=MESH,
            )

        def send_extra(s):
            return pltpu.make_async_remote_copy(
                src_ref=dkv.at[:, pl.ds(rows_all, qblock)],
                dst_ref=extra.at[s],
                send_sem=esend_sem.at[s],
                recv_sem=erecv_sem.at[s],
                device_id=other_core,
                device_id_type=MESH,
            )

        def sent(s):
            @pl.when(k == 1)
            def _():
                send_dkv(s).wait_send()
                send_first(s).wait_send()

            @pl.when(k == 0)
            def _():
                send_back(s).wait_send()
                send_extra(s).wait_send()

        def attend(s, q_low, g_low, first_query, first_key, span):
            keys = pl.ds(first_key, span)
            key_at = first_key + lax.broadcasted_iota(jnp.int32, (span, qblock), 0)
            query_at = first_query + lax.broadcasted_iota(jnp.int32, (span, qblock), 1)
            begin = begin_ref[0:1, pl.ds(pl.multiple_of(first_query, qblock), qblock)]
            mask[:span] = jnp.where((key_at >= begin) & (key_at <= query_at), 0.0, -1e30)
            lane = lax.broadcasted_iota(jnp.int32, (qblock, LANES), 1)
            att = jnp.zeros((qblock, LANES), jnp.float32)
            dq = jnp.zeros((qblock, LANES), jnp.float32)
            for head in range(2):
                inside = (lane >= head * HD) & (lane < (head + 1) * HD)
                q_own = jnp.where(inside, q_low, jnp.zeros((qblock, LANES), jnp.bfloat16))
                g_own = jnp.where(inside, g_low, jnp.zeros((qblock, LANES), jnp.bfloat16))
                scores = dot(kv[s, 0, keys, :], q_own, NT) + mask[:span]
                weights = jnp.exp(scores - jnp.max(scores, 0, keepdims=True))
                probs = weights * (1.0 / jnp.sum(weights, 0, keepdims=True))
                probs_low = probs.astype(jnp.bfloat16)
                grad_probs = dot(kv[s, 1, keys, :], g_own, NT)
                inner = jnp.sum(probs * grad_probs, 0, keepdims=True)
                grad_scores = (probs * (grad_probs - inner)).astype(jnp.bfloat16)
                att = jnp.where(inside, dot(probs_low, kv[s, 1, keys, :], TN), att)
                dq = jnp.where(inside, dot(grad_scores, kv[s, 0, keys, :], TN), dq)
                dkv[1, keys, :] += dot(probs_low, g_own)
                dkv[0, keys, :] += dot(grad_scores, q_own)
            return att, dq * HD**-0.5

        def attend_own(s, b, first_key, span):
            rows = pl.ds(pl.multiple_of(b * qblock, qblock), qblock)
            att, dq = attend(s, qg[0, rows, :], qg[1, rows, :], k * rows_all + b * qblock, first_key, span)
            x[rows, ATT:] = att.astype(jnp.bfloat16)
            x[rows, :LANES] = rope(dq, rows, -1.0).astype(jnp.bfloat16)

        def attention_unit(u, s, at, out_at):
            fetch_weights(u).wait()
            wait_saved(u)
            wait_put(u - 2)

            @pl.when(s > 0)
            def _():
                sent(s - 1)

            def project(i, carry):
                rows = pl.ds(pl.multiple_of(i * block, block), block)
                there = pl.ds(pl.multiple_of(k * rows_all + i * block, block), block)
                pre = dot(normed[rows, :], wbuf[:, :, :ATT].reshape(width, ATT)) + bias_ref[u][:, :ATT]
                query = rope(pre[:, :LANES], rows, 1.0).astype(jnp.bfloat16)
                qg[0, rows, :] = query * jnp.bfloat16(HD**-0.5)
                kv[s, 0, there, :] = rope(pre[:, LANES : 2 * LANES], rows, 1.0).astype(jnp.bfloat16)
                kv[s, 1, there, :] = pre[:, 2 * LANES :].astype(jnp.bfloat16)
                return carry

            lax.fori_loop(0, rows_all // block, project, 0)
            send_kv(s).start()

            def project_grad(i, carry):
                rows = pl.ds(pl.multiple_of(i * block, block), block)
                grad = dot(cot[rows, :], wbuf[:, :, ATT:].reshape(width, LANES))
                qg[1, rows, :] = grad.astype(jnp.bfloat16)
                return carry

            lax.fori_loop(0, rows_all // block, project_grad, 0)

            @pl.when(k == 1)
            def _():
                send_first(s).start()

            dkv[...] = jnp.zeros_like(dkv)
            per_block = in_attention // qblocks
            early = in_attention - per_block * qblocks
            out_block = out_attention // qblocks
            out_early = out_attention - out_block * qblocks
            fetch_swapped(u - 1, swap_in)
            ticks(at + lead, early, out_at - behind, out_early)
            prepare(u - 1, swap_in)
            recv_kv(s).wait_recv()

            def turn_of(b, carry):
                @pl.when((k == 1) & (b < qblocks - 1))
                def _():
                    first_key = pl.multiple_of(rows_all + (b + 2) * qblock - window, qblock)
                    attend_own(s, b + 1, first_key, window)

                @pl.when((k == 1) & (b == qblocks - 2))
                def _():
                    send_dkv(s).start()

                for own in range(qblocks):

                    @pl.when((k == 0) & (b == (own if own > 1 else 0)))
                    def _():
                        attend_own(s, own, 0, (own + 1) * qblock)

                @pl.when((k == 0) & (b == 1))
                def _():
                    send_first(s).wait_recv()
                    att, dq = attend(s, moved[s, 0], moved[s, 1], rows_all, 0, window)
                    back[0], back[1] = att, dq
                    send_back(s).start()
                    send_extra(s).start()

                ticks(
                    at + early + b * per_block + lead,
                    per_block,
                    out_at + out_early + b * out_block - behind,
                    out_block,
                )
                return carry

            lax.fori_loop(0, qblocks, turn_of, 0)
            first_rows, own_rows = pl.ds(0, qblock), pl.ds(0, rows_all)

            @pl.when(k == 1)
            def _():
                send_back(s).wait_recv()
                send_extra(s).wait_recv()
                x[first_rows, ATT:] = returned[s, 0].astype(jnp.bfloat16)
                x[first_rows, :LANES] = rope(returned[s, 1], first_rows, -1.0).astype(jnp.bfloat16)
                dkv[:, pl.ds(rows_all, qblock)] += extra[s]

            @pl.when(k == 0)
            def _():
                send_dkv(s).wait_recv()
                copy = pltpu.make_async_copy(dkv_other.at[s], dkv_tmp, load_sem)
                copy.start()
                copy.wait()
                dkv[:, own_rows] += dkv_tmp[...]

            def turn(i, carry):
                rows = pl.ds(pl.multiple_of(i * qblock, qblock), qblock)
                there = pl.ds(pl.multiple_of(k * rows_all + i * qblock, qblock), qblock)
                x[rows, LANES : 2 * LANES] = rope(dkv[0, there, :], rows, -1.0).astype(jnp.bfloat16)
                x[rows, 2 * LANES : ATT] = dkv[1, there, :].astype(jnp.bfloat16)
                return carry

            lax.fori_loop(0, qblocks, turn, 0)
            save(u).start()
            next_weights(u + 1)
            bias_grad = column_sums(ATT)
            for g in range(3):
                vec[g : g + 1, pl.ds(pl.multiple_of(s * LANES, LANES), LANES)] = bias_grad[
                    :, g * LANES : (g + 1) * LANES
                ]
            gradients(u, ATT)


        cot_copy = pltpu.make_async_copy(cot_hbm, cot, save_sem)
        cot_copy.start()
        fetch_rows(0).start()
        fetch_raw(0, True)
        fetch_raw(1, True)
        for u in range(2):
            pack(u)
            put_packed(u).wait()
            if u == 0:
                send_own(0)
            fetch_raw(u + 2, True)

        def begin_step(i, carry):
            @pl.when(i + 2 < units)
            def _():
                pack(i + 2)

            @pl.when(i < norm_blocks)
            def _():
                normalize(i)

            @pl.when(i + 2 < units)
            def _():
                put_packed(i + 2).wait()

            @pl.when(i + 4 < units)
            def _():
                fetch_raw(i + 4, True)

            @pl.when(i < lead)
            def _():
                gather_tick(i)

            return carry

        lax.fori_loop(0, max(units - 2, norm_blocks, lead), begin_step, 0)
        cot_copy.wait()
        next_weights(0)
        vec[...] = jnp.zeros_like(vec)
        vec[NIN : NIN + 1, :] = dot(jnp.ones((8, rows_all), jnp.bfloat16), cot[:, columns])[0:1, :]

        def super_step(s, carry):
            at = s * per_step
            out_at = s * (2 * out_hidden + out_attention)
            hidden_unit(3 * s, 2 * s, at, out_at)
            attention_unit(3 * s + 1, s, at + in_hidden, out_at + out_hidden)
            hidden_unit(
                3 * s + 2, 2 * s + 1, at + in_hidden + in_attention, out_at + out_hidden + out_attention
            )
            return carry

        lax.fori_loop(0, steps, super_step, 0)

        save(units - 1).wait()
        exchange(units - 2).wait_send()
        exchange(units - 1).wait_send()

        sent(steps - 1)


    square = peers == 4
    upper, lower = pl.ds(0, rows_all // 2), pl.ds(rows_all // 2, rows_all // 2)

    def beside(axis):
        return tensor + 1 - 2 * (tensor % 2) if axis == 0 else tensor + 2 - 4 * (tensor // 2)

    def block_at(i):
        if not square:
            return lax.rem(tensor + 1 + i, peers)
        return jnp.where(
            i == 0, 3 - tensor, jnp.where(i == 1, beside(0), jnp.where(i == 2, beside(1), tensor))
        )

    def tensor_copy(blocks, what, message):
        if square:
            slot, rows, axis = ((0, upper, 0), (0, lower, 1), (1, upper, 0), (2, lower, 1), (1, lower, 0), (2, upper, 1))[
                message
            ]
            source, there = blocks.at[what, slot, rows], arrived.at[what, slot, rows]
            target = beside(axis)
        else:
            source, there = blocks.at[what, message], arrived.at[what, message]
            target = block_at(message)
        return pltpu.make_async_remote_copy(
            src_ref=source,
            dst_ref=there,
            send_sem=tsend_sem.at[what, message],
            recv_sem=trecv_sem.at[what, message],
            device_id={"tensor": target},
            device_id_type=MESH,
        )

    def sums_copy(i):
        return pltpu.make_async_remote_copy(
            src_ref=sums,
            dst_ref=sums_in.at[i],
            send_sem=ssend_sem.at[i],
            recv_sem=srecv_sem.at[i],
            device_id={"tensor": lax.rem(tensor + 1 + i, peers)},
            device_id_type=MESH,
        )

    def finals(xs, tile, blocks, swap_in, passing):
        part = size // 2
        tiles = 4 * peers
        remote = 2 * (peers - 1)

        def fetch_tile(q):
            i = jnp.where(q < remote, q, jnp.where(q < 2 * remote, q - remote, remote + q % 2)) // 2
            shard = block_at(i)
            rows = pl.ds(pl.multiple_of(q % 2 * part, part), part)
            return pltpu.make_async_copy(full.at[:, shard, rows], tile.at[q % 2], tile_sem.at[q % 2])

        fetch_xs = pltpu.make_async_copy(saved, xs.at[pl.ds(0, units)], load_sem)
        fetch_xs.start()
        fetch_tile(0).start()
        fetch_swapped(units - 1, swap_in)
        prepare(units - 1, swap_in)
        wait_put(units - 2)
        wait_put(units - 1)
        fetch_xs.wait()
        block = min(512, rows_all)

        def products(q, what, store):
            @pl.when(q + 1 < tiles)
            def _():
                fetch_tile(q + 1).start()

            fetch_tile(q).wait()

            def one(r, carry):
                rows = pl.ds(pl.multiple_of(r * block, block), block)
                value = None
                for u in range(units):
                    split = ATT if u % 3 == 1 else HID
                    part_of = slice(0, split) if what == 0 else slice(split, WIDE)
                    product = dot(xs[u, rows, part_of], tile[q % 2, u, :, part_of], NT)
                    value = product if value is None else value + product
                store(r, value)
                return carry

            lax.fori_loop(0, rows_all // block, one, 0)

        scatter_at = steps * (2 * out_hidden + out_attention) - behind
        scatter_count = (units - 1) * last + last * LAG + 1 - scatter_at
        tile_count = scatter_count * 2 // 5 // remote
        rest_at, rest_count = scatter_at + tile_count * remote, scatter_count - tile_count * remote
        cuts = [rest_at + rest_count * share_of // 16 for share_of in (0, 2, 5, 8, 11, 13, 16)]

        def rest(i):
            run_ticks(0, 0, cuts[i], cuts[i + 1] - cuts[i])

        def remote_tile(what, i):
            def one(h, carry):
                def store(r, value):
                    rows = pl.ds(pl.multiple_of(r * block, block), block)
                    cols = pl.ds(pl.multiple_of(h * part, part), part)
                    blocks[what, i, rows, cols] = value.astype(jnp.bfloat16)

                q = 2 * i + h
                products(q + what * remote, what, store)
                if what == 1:
                    run_ticks(0, 0, scatter_at + q * tile_count, tile_count)
                return carry

            lax.fori_loop(0, 2, one, 0)

        def send(what, *messages):
            for message in messages:
                tensor_copy(blocks, what, message).start()

        def add_half(what, slot, rows, message, onward):
            tensor_copy(blocks, what, message).wait_recv()
            copy = pltpu.make_async_copy(
                arrived.at[what, 0, rows], passing, load_sem
            )
            copy.start()
            copy.wait()
            blocks[what, slot, rows, :] = (
                blocks[what, slot, rows, :].astype(jnp.float32) + passing[...].astype(jnp.float32)
            ).astype(jnp.bfloat16)
            send(what, onward)

        if square:
            remote_tile(0, 0)
            send(0, 0, 1)
            remote_tile(0, 1)
            send(0, 2)
            remote_tile(0, 2)
            send(0, 3)
            remote_tile(1, 0)
            add_half(0, 1, lower, 1, 4)
            add_half(0, 2, upper, 0, 5)
            send(1, 0, 1)
            remote_tile(1, 1)
            send(1, 2)
            remote_tile(1, 2)
            send(1, 3)
        else:
            for what in range(2):

                def one_block(i, carry):
                    remote_tile(what, i)
                    send(what, i)
                    return carry

                lax.fori_loop(0, peers - 1, one_block, 0)

        for what in range(2):
            for h in range(2):

                def store(r, value):
                    for a in range(block // HID):
                        held[what, r * (block // HID) + a, :, h * part : (h + 1) * part] = value[
                            a * HID : (a + 1) * HID
                        ]

                products(2 * remote + 2 * what + h, what, store)

        rest(0)
        if square:
            add_half(1, 1, lower, 1, 4)
            add_half(1, 2, upper, 0, 5)

        tok_at, cot_at, out_at = 2 * (peers - 1), 2 * (peers - 1) + 1, 2 * (peers - 1) + 2
        bring = [
            pltpu.make_async_copy(tokens.at[:, columns], xs.at[tok_at, :, pl.ds(0, size)], tile_sem.at[0]),
            pltpu.make_async_copy(cot_hbm.at[:, columns], xs.at[cot_at, :, pl.ds(0, size)], tile_sem.at[1]),
        ]
        for copy in bring:
            copy.start()
        for copy in bring:
            copy.wait()

        first = 1 if square else 0
        count = peers - 1 - first

        def collect(what):
            for message in range(2, 6) if square else ():
                tensor_copy(blocks, what, message).wait_recv()

            def one(i, carry):
                if not square:
                    tensor_copy(blocks, what, i).wait_recv()
                copy = pltpu.make_async_copy(
                    arrived.at[what, first + i], xs.at[what * count + i, :, pl.ds(0, size)], load_sem
                )
                copy.start()
                copy.wait()
                return carry

            lax.fori_loop(0, count, one, 0)

        def summed(what, r, rows):
            value = held[what, r]
            for i in range(count):
                value += xs[what * count + i, rows, :size].astype(jnp.float32)
            return value

        gain = vec_ref[NIN + 1 : NIN + 2, columns]
        ones = jnp.ones((8, size), jnp.float32)

        def unit_of(rows):
            token = xs[tok_at, rows, :size].astype(jnp.float32)
            return (token - stats[rows, 0:1]) * stats[rows, 1:2]

        rest(1)
        collect(0)

        def first_pass(r, carry):
            rows = pl.ds(pl.multiple_of(r * HID, HID), HID)
            grad = summed(0, r, rows)
            held[0, r] = grad
            unit = unit_of(rows)
            scaled = grad * gain
            sums[0:8, rows] = lax.dot_general(
                ones, scaled, NT, precision=lax.Precision.HIGHEST, preferred_element_type=jnp.float32
            )
            sums[8:16, rows] = lax.dot_general(
                ones, scaled * unit, NT, precision=lax.Precision.HIGHEST, preferred_element_type=jnp.float32
            )
            vec[NIN + 1 : NIN + 2, :] += jnp.sum(grad * unit, 0, keepdims=True)
            vec[NIN + 2 : NIN + 3, :] += jnp.sum(grad, 0, keepdims=True)
            return carry

        lax.fori_loop(0, rows_all // HID, first_pass, 0)
        for i in range(peers - 1):
            sums_copy(i).start()
        to_core = pltpu.make_async_remote_copy(
            src_ref=vec, dst_ref=vec_core, send_sem=vsend_sem.at[0], recv_sem=vrecv_sem.at[0],
            device_id=other_core, device_id_type=MESH,
        )
        to_core.start()
        rest(2)
        for i in range(peers - 1):
            sums_copy(i).wait_recv()
        inv_width = 1.0 / width

        def second_pass(r, carry):
            rows = pl.ds(pl.multiple_of(r * HID, HID), HID)
            means = sums[:, rows]
            for i in range(peers - 1):
                means += sums_in[i, :, rows]
            means = (means * inv_width).T
            unit = unit_of(rows)
            held[0, r] = stats[rows, 1:2] * (
                held[0, r] * gain - means[:, 0:1] - unit * means[:, 8:9]
            ) + xs[cot_at, rows, :size].astype(jnp.float32)
            return carry

        lax.fori_loop(0, rows_all // HID, second_pass, 0)
        put_grad = pltpu.make_async_copy(held.at[0, pl.ds(0, rows_all // HID)], token_grad, out_sem.at[0])
        put_grad.start()

        rest(3)
        to_core.wait_recv()
        vec_line[z] = vec[...] + vec_core[...]

        def along_dp(i):
            return pltpu.make_async_remote_copy(
                src_ref=vec_line.at[z], dst_ref=vec_line.at[z],
                send_sem=vsend_sem.at[1 + i], recv_sem=vrecv_sem.at[1 + i],
                device_id={"dp": lax.rem(z + 1 + i, n)}, device_id_type=MESH,
            )

        def from_dp(i):
            there = lax.rem(z + n - 1 - i, n)
            return pltpu.make_async_remote_copy(
                src_ref=vec_line.at[there], dst_ref=vec_line.at[there],
                send_sem=vsend_sem.at[1 + i], recv_sem=vrecv_sem.at[1 + i],
                device_id={"dp": lax.rem(z + 1 + i, n)}, device_id_type=MESH,
            )

        for i in range(n - 1):
            along_dp(i).start()
        for i in range(n - 1):
            from_dp(i).wait_recv()
        vec_sum = vec_line[0]
        for i in range(1, n):
            vec_sum += vec_line[i]
        vec_all[tensor] = vec_sum

        def along_tensor(i):
            return pltpu.make_async_remote_copy(
                src_ref=vec_all.at[tensor], dst_ref=vec_all.at[tensor],
                send_sem=vsend_sem.at[n + i], recv_sem=vrecv_sem.at[n + i],
                device_id={"tensor": lax.rem(tensor + 1 + i, peers)}, device_id_type=MESH,
            )

        def from_tensor(i):
            there = lax.rem(tensor + peers - 1 - i, peers)
            return pltpu.make_async_remote_copy(
                src_ref=vec_all.at[there], dst_ref=vec_all.at[there],
                send_sem=vsend_sem.at[n + i], recv_sem=vrecv_sem.at[n + i],
                device_id={"tensor": lax.rem(tensor + 1 + i, peers)}, device_id_type=MESH,
            )

        for i in range(peers - 1):
            along_tensor(i).start()

        rest(4)
        collect(1)
        out_bias = vec_ref[NIN : NIN + 1, columns]

        def third_pass(r, carry):
            rows = pl.ds(pl.multiple_of(r * HID, HID), HID)
            value = xs[tok_at, rows, :size].astype(jnp.float32) + (summed(1, r, rows) + out_bias)
            xs[out_at, rows, :size] = value.astype(jnp.bfloat16)
            return carry

        lax.fori_loop(0, rows_all // HID, third_pass, 0)
        put_result = pltpu.make_async_copy(xs.at[out_at, :, pl.ds(0, size)], result, out_sem.at[1])
        put_result.start()
        rest(5)

        for i in range(peers - 1):
            from_tensor(i).wait_recv()
        vec_grad[...] = vec_all[...]
        put_grad.wait()
        put_result.wait()
        to_core.wait_send()
        for i in range(n - 1):
            along_dp(i).wait_send()
        for i in range(peers - 1):
            along_tensor(i).wait_send()
            sums_copy(i).wait_send()
        for i in range(6 if square else peers - 1):
            tensor_copy(blocks, 0, i).wait_send()
            tensor_copy(blocks, 1, i).wait_send()

    low, wide = jnp.bfloat16, jnp.float32
    window, qblock = rows_all + 256, 256
    pl.run_scoped(
        forward_backward,
        pltpu.VMEM((rows_all, width), low),
        pltpu.VMEM((rows_all, width), low),
        pltpu.VMEM((2, rows_all // 8, width), low),
        pltpu.VMEM((2, size, ATT), wide),
        pltpu.VMEM((2, HID, size), wide),
        pltpu.VMEM((2, size, WIDE), low),
        pltpu.VMEM((n, size, WIDE), low),
        pltpu.VMEM((rows_all, WIDE), low),
        pltpu.VMEM((2, rows_all, LANES), low),
        pltpu.VMEM((2, 2 * rows_all, LANES), wide),
        pltpu.VMEM((2, 256, LANES), wide),
        pltpu.VMEM((2, rows_all, LANES), wide),
        pltpu.VMEM((window, qblock), wide),
        pltpu.VMEM((2, n, HID, size), low),
        pltpu.VMEM((n, HID, size), low),
    )
    pl.run_scoped(
        finals,
        pltpu.VMEM((max(units, 2 * peers + 1), rows_all, WIDE), low),
        pltpu.VMEM((2, units, size // 2, WIDE), low),
        pltpu.VMEM((2, peers - 1, rows_all, size), low),
        pltpu.VMEM((n, HID, size), low),
        pltpu.VMEM((rows_all // 2, size), low),
    )


    def drain_kv(s, carry):
        send_kv(s).wait_send()
        return carry

    lax.fori_loop(0, steps, drain_kv, 0)

    def drain(m, carry):
        g, s = m // last, m % last + 1

        @pl.when(s == 1)
        def _():
            @pl.when(z < last)
            def _():
                hop(0, g, 0, z).wait_send()

            @pl.when(z > 0)
            def _():
                hop(1, g, 0, z).wait_send()

            @pl.when(g >= units - boxes)
            def _():
                keep(g).wait()
                share(g, my_part).wait_send()

            share(g, their_part).wait_recv()

        @pl.when(z >= s)
        def _():
            @pl.when(z < last)
            def _():
                hop(0, g, s, z - s).wait_send()

            across(0, g, s - 1, z - s, mine).wait_send()

        @pl.when(z + s <= last)
        def _():
            @pl.when(z > 0)
            def _():
                hop(1, g, s, z + s).wait_send()

            across(1, g, s - 1, z + s, mine).wait_send()

        for way in range(2):
            distance = z if way == 0 else last - z

            @pl.when(distance < last - (s - 1))
            def _():
                pass_on(way, g, s - 1).wait_send()

        return carry

    lax.fori_loop(0, units * last, drain, 0)


def run_block(in_weight, out_weight, tokens, cotangent, bias, vectors, cosine, sine, begin):
    n, peers = lax.axis_size("dp"), lax.axis_size("tensor")
    size, cols_all = in_weight.shape[1:]
    steps = cols_all // LANES
    units = 3 * steps
    rows, width = tokens.shape
    assert width == n * size == peers * cols_all and size == cols_all and rows <= n * HID
    low, wide = jnp.bfloat16, jnp.float32
    anywhere = pl.BlockSpec(memory_space=pl.ANY)
    vm = pl.BlockSpec(memory_space=pltpu.VMEM)
    dma = pltpu.SemaphoreType.DMA
    return pl.pallas_call(
        functools.partial(block_kernel, n, steps, peers),
        out_shape=(
            jax.ShapeDtypeStruct((units, n, size, WIDE), low),
            jax.ShapeDtypeStruct((units, rows, WIDE), low),
            jax.ShapeDtypeStruct((units, WIDE, size), wide),
            jax.ShapeDtypeStruct((units, n, HID, size), low),
            jax.ShapeDtypeStruct((units, n, HID, size), wide),
            jax.ShapeDtypeStruct((steps, 2, rows, LANES), wide),
            jax.ShapeDtypeStruct((2, peers - 1, rows, size), low),
            jax.ShapeDtypeStruct((rows, size), low),
            jax.ShapeDtypeStruct((rows // HID, HID, size), wide),
            jax.ShapeDtypeStruct((peers, 16, size), wide),
        ),
        in_specs=[anywhere] * 4 + [vm] * 5,
        out_specs=[anywhere] * 9 + [vm],
        scratch_shapes=[
            pltpu.VMEM((steps, 2, 2 * rows, LANES), low),
            pltpu.VMEM((steps, 2, 256, LANES), low),
            pltpu.VMEM((steps, 2, 256, LANES), wide),
            pltpu.VMEM((steps, 2, 256, LANES), wide),
            pltpu.VMEM((2, n, HID, size), wide),
            pltpu.VMEM((2, 2, HID, size), wide),
            pltpu.VMEM((units, n + 1, HID, size), low),
            pltpu.VMEM((3, HID, size), wide),
            pltpu.VMEM((rows, LANES), wide),
            pltpu.VMEM((16, size), wide),
            pltpu.VMEM((16, size), wide),
            pltpu.VMEM((n, 16, size), wide),
            pltpu.VMEM((peers, 16, size), wide),
            pltpu.VMEM((16, rows), wide),
            pltpu.VMEM((peers - 1, 16, rows), wide),
            dma((2, units, n)),
            dma((2, units, n)),
            dma((2, units, n)),
            dma((2, units, n)),
            dma((units,)),
            dma((units,)),
            dma((2, units, n - 1)),
            dma((2, units, n - 1)),
            dma((units,)),
            dma((units,)),
            dma((units,)),
            dma((steps,)),
            dma((steps,)),
            dma((steps,)),
            dma((steps,)),
            dma((steps,)),
            dma((steps,)),
            dma((steps,)),
            dma((steps,)),
            dma((steps,)),
            dma((steps,)),
            dma,
            dma,
            dma,
            dma((2, 4)),
            dma((2,)),
            dma((2,)),
            dma,
            dma((2,)),
            dma((2, 2)),
            dma((3,)),
            dma((2, 6 if peers == 4 else peers - 1)),
            dma((2, 6 if peers == 4 else peers - 1)),
            dma((peers - 1,)),
            dma((peers - 1,)),
            dma((n + peers - 1,)),
            dma((n + peers - 1,)),
            dma((2,)),
            dma((2,)),
        ],
        compiler_params=pltpu.CompilerParams(
            collective_id=1, has_side_effects=True, vmem_limit_bytes=VMEM_LIMIT
        ),
        name="parallel_block",
    )(in_weight, out_weight, tokens, cotangent, bias, vectors, cosine, sine, begin)


def adam_kernel(into, chunks, *refs):
    pieces, refs = refs[:chunks], refs[chunks:]
    g = pl.program_id(0)

    def update(weights, turned):
        w, m, v, new_w, new_m, new_v = weights
        for c, piece in enumerate(pieces):
            part = slice(c * LANES, (c + 1) * LANES)
            at = (0, part) if turned else (0, slice(None), part)
            gradient = piece[0] if turned else piece[0].T
            new_w[at], new_m[at], new_v[at] = adamw(
                w[at], gradient, m[at], v[at], rate_matrix, weight_decay
            )

    @pl.when(g < into)
    def _():
        update(refs[:3] + refs[6:9], False)

    @pl.when(g >= into)
    def _():
        update(refs[3:6] + refs[9:], True)


def adam_weights(total, in_arrays, out_arrays):
    into, size, cols_all = in_arrays[0].shape
    outof = out_arrays[0].shape[0]
    chunks = cols_all // LANES

    def place(c, g):
        is_in = g < into
        group = jnp.where(is_in, g, g - into)
        lead = jnp.where(is_in, 3, 1)
        i = jnp.maximum((group - lead) * cols_all + c * LANES, 0) // HID
        unit = jnp.where(group < lead, 3 * c + 1, 3 * (i // 2) + 2 * (i % 2))
        lane = jnp.where(
            group < lead, jnp.where(is_in, group, 3), c % 2 + jnp.where(is_in, 0, 2)
        )
        return unit, lane, 0

    in_spec = pl.BlockSpec((1, size, cols_all), lambda g: (jnp.minimum(g, into - 1), 0, 0))
    out_spec = pl.BlockSpec((1, cols_all, size), lambda g: (jnp.maximum(g - into, 0), 0, 0))
    results = pl.pallas_call(
        functools.partial(adam_kernel, into, chunks),
        grid=(into + outof,),
        out_shape=tuple(jax.ShapeDtypeStruct(v.shape, jnp.float32) for v in in_arrays + out_arrays),
        in_specs=[pl.BlockSpec((1, LANES, size), functools.partial(place, c)) for c in range(chunks)]
        + [in_spec] * 3
        + [out_spec] * 3,
        out_specs=[in_spec] * 3 + [out_spec] * 3,
        compiler_params=pltpu.CompilerParams(vmem_limit_bytes=VMEM_LIMIT),
        name="adam_weights",
    )(*[total] * chunks, *in_arrays, *out_arrays)
    return results[:3], results[3:]


def layout(lengths_row, row_span):
    seg_ends = jnp.cumsum(lengths_row)
    seg_starts = seg_ends - lengths_row
    places = jnp.arange(row_span, dtype=jnp.int32)
    segment = jnp.sum((places[:, None] >= seg_ends[None, :]).astype(jnp.int32), 1)
    numbers = jnp.arange(lengths_row.shape[0], dtype=jnp.int32)
    return jnp.sum(jnp.where(segment[:, None] == numbers[None, :], seg_starts[None, :], 0), 1)


def rope_tables(places):
    half_rot = ROT // 2
    lane = jnp.arange(2 * HD, dtype=jnp.int32) % HD
    exponent = (lane % half_rot).astype(jnp.float32)
    frequency = 10000.0 ** (-2.0 * exponent / ROT)
    angles = places.astype(jnp.float32)[:, None] * frequency[None, :]
    turned = (lane < ROT)[None, :]
    cosine = jnp.where(turned, jnp.cos(angles), 1.0)
    sine = jnp.where(turned, jnp.sin(angles), 0.0)
    return cosine, sine


def body(
    tokens,
    cotangent,
    lengths,
    in_weight,
    out_weight,
    vectors,
    in_first,
    in_second,
    out_first,
    out_second,
    vec_first,
    vec_second,
):
    local_rows, model_width = tokens.shape
    slice_width = in_weight.shape[2]
    context_count = lax.axis_size("context")
    context_index = lax.axis_index("context")
    tensor_index = lax.axis_index("tensor")
    row_span = local_rows * context_count
    first_row = context_index * local_rows
    begin_all = layout(lengths[0], row_span)
    begin = lax.dynamic_slice_in_dim(begin_all, first_row, local_rows, 0)
    places = first_row + jnp.arange(local_rows, dtype=jnp.int32) - begin
    tables = rope_tables(places)

    column = tensor_index * slice_width
    in_bias = lax.dynamic_slice_in_dim(vectors[:NIN], column, slice_width, 1)
    steps = slice_width // LANES
    hid_bias = in_bias[3:].reshape(steps, 2, HID)
    att_bias = in_bias[:3].reshape(3, steps, LANES).transpose(1, 0, 2).reshape(steps, ATT)
    bias = jnp.stack(
        [
            jnp.pad(hid_bias[:, 0], ((0, 0), (0, WIDE - HID))),
            jnp.pad(att_bias, ((0, 0), (0, WIDE - ATT))),
            jnp.pad(hid_bias[:, 1], ((0, 0), (0, WIDE - HID))),
        ],
        1,
    ).reshape(3 * steps, 1, WIDE)
    by_group = jnp.transpose(in_weight, (1, 0, 2))
    _, _, total, _, _, _, _, result, token_grad, vec_grad = run_block(
        by_group, out_weight, tokens, cotangent, bias, vectors, tables[0], tables[1], begin_all[None]
    )
    token_grad = token_grad.reshape(local_rows, slice_width)
    vector_grad = jnp.transpose(vec_grad, (1, 0, 2)).reshape(-1, model_width)[: NIN + 3]
    new_vectors, new_vec_first, new_vec_second = adamw(
        vectors, vector_grad, vec_first, vec_second, rate_vector, 0.0
    )
    by_group_moments = [jnp.transpose(v, (1, 0, 2)) for v in (in_first, in_second)]
    new_by_group, (new_out, new_out_first, new_out_second) = adam_weights(
        total, [by_group] + by_group_moments, [out_weight, out_first, out_second]
    )
    new_in, new_in_first, new_in_second = (jnp.transpose(v, (1, 0, 2)) for v in new_by_group)
    return (
        result,
        token_grad,
        new_in,
        new_in_first,
        new_in_second,
        new_out,
        new_out_first,
        new_out_second,
        new_vectors,
        new_vec_first,
        new_vec_second,
    )


def solution(mesh):
    return jax.shard_map(
        body,
        mesh=mesh,
        in_specs=(
            P(("dp", "context"), None),
            P(("dp", "context"), None),
            P("dp", None),
            P("dp", None, "tensor"),
            P(None, "tensor", "dp"),
            P(),
            P("dp", None, "tensor"),
            P("dp", None, "tensor"),
            P(None, "tensor", "dp"),
            P(None, "tensor", "dp"),
            P(),
            P(),
        ),
        out_specs=(
            P(("dp", "context"), "tensor"),
            P(("dp", "context"), "tensor"),
            P("dp", None, "tensor"),
            P("dp", None, "tensor"),
            P("dp", None, "tensor"),
            P(None, "tensor", "dp"),
            P(None, "tensor", "dp"),
            P(None, "tensor", "dp"),
            P(),
            P(),
            P(),
        ),
        check_vma=False,
    )
```

```python
import functools

import jax
import jax.numpy as jnp
from jax import lax
from jax.experimental import pallas as pl
from jax.experimental.pallas import tpu as pltpu
from jax.sharding import PartitionSpec as P

HD = 64
ROT = 32
STEP = 10
NIN = 7
MESH = pl.DeviceIdType.MESH
VMEM_LIMIT = 60 * 2**20

norm_eps = 1e-05
beta_one = 0.9
beta_two = 0.95
adam_eps = 1e-08
weight_decay = 0.1
rate_matrix = 0.02
rate_vector = 0.4


def adamw(master, gradient, moment_one, moment_two, step_rate, decay_rate):
    first_new = beta_one * moment_one + (1.0 - beta_one) * gradient
    second_new = beta_two * moment_two + (1.0 - beta_two) * gradient * gradient
    first_hat = first_new * (1.0 / (1.0 - beta_one**STEP))
    second_hat = second_new * (1.0 / (1.0 - beta_two**STEP))
    updated = master - step_rate * (
        first_hat / (jnp.sqrt(second_hat) + adam_eps) + decay_rate * master
    )
    return (updated, first_new, second_new)


LANES = 2 * HD
WIDE = 4 * LANES
HID = WIDE // 2
ATT = 3 * LANES
LAG = 5

NT = (((1,), (1,)), ((), ()))
NN = (((1,), (0,)), ((), ()))
TN = (((0,), (0,)), ((), ()))


def dot(x, y, dims=NN):
    return lax.dot_general(x, y, dims, preferred_element_type=jnp.float32)


def greet(n, peers):
    z = lax.axis_index("dp")
    k = lax.axis_index("context")
    t = lax.axis_index("tensor")
    barrier = pltpu.get_barrier_semaphore()
    pl.semaphore_signal(barrier, inc=1, device_id={"context": 1 - k}, device_id_type=MESH)
    for i in range(1, n):
        pl.semaphore_signal(barrier, inc=1, device_id={"dp": lax.rem(z + i, n)}, device_id_type=MESH)
    for i in range(1, peers):
        pl.semaphore_signal(
            barrier, inc=1, device_id={"tensor": lax.rem(t + i, peers)}, device_id_type=MESH
        )
    pl.semaphore_wait(barrier, n + peers - 1)


def gelu_both(v):
    rate = 0.7978845608028654
    t = jnp.tanh(rate * (v + 0.044715 * (v * v * v)))
    value = 0.5 * v * (1.0 + t)
    slope = 0.5 * (1.0 + t) + 0.5 * v * (1.0 - t * t) * (rate * (1.0 + 3.0 * 0.044715 * (v * v)))
    return value, slope


def schedule(n):
    last = n - 1
    per_step = 3 * last
    in_hidden = 2 * per_step // 9
    in_attention = per_step - 2 * in_hidden
    done = (in_hidden, in_hidden + in_attention, per_step)
    lead = max([last * (n + i) - done[i] for i in range(3)] + [last * (n - 1)])
    out_hidden, out_attention = in_hidden, in_attention
    behind = 1 + max(out_hidden + last, out_hidden + out_attention, 2 * out_hidden + out_attention - last)
    return per_step, in_hidden, in_attention, lead, out_hidden, out_attention, behind


def block_kernel(
    n, steps, peers,
    in_w, out_w, tokens, cot_hbm, bias_ref, vec_ref, cos_ref, sin_ref, begin_ref,
    full, saved, total, swap, kept, dkv_other, arrived, result, token_grad, vec_grad,
    kv, moved, returned, extra, held, pieces, line, outbox, stats, vec, vec_core, vec_line, vec_all, sums, sums_in,
    send_sem, recv_sem, psend_sem, precv_sem,
    xsend_sem, xrecv_sem, lsend_sem, lrecv_sem, keep_sem, fsend_sem, frecv_sem,
    kvsend_sem, kvrecv_sem, dsend_sem, drecv_sem, msend_sem, mrecv_sem, bsend_sem, brecv_sem, esend_sem, erecv_sem, load_sem, save_sem, weight_sem, pack_sem, put_sem, rows_sem, swap_sem, held_sem, piece_sem, box_sem,
    tsend_sem, trecv_sem, ssend_sem, srecv_sem, vsend_sem, vrecv_sem, tile_sem, out_sem,
):
    units = 3 * steps
    last = n - 1
    per_step, in_hidden, in_attention, lead, out_hidden, out_attention, behind = schedule(n)
    depth, boxes = 2, 3
    size, cols_all = in_w.shape[1], in_w.shape[2]
    half = size // 2
    rows_all, width = tokens.shape
    tensor = lax.axis_index("tensor")
    columns = pl.ds(pl.multiple_of(tensor * size, size), size)
    z = lax.axis_index("dp")
    k = lax.axis_index("context")
    mine = pl.ds(pl.multiple_of(k * half, half), half)
    theirs = pl.ds(pl.multiple_of((1 - k) * half, half), half)
    other_core = {"context": 1 - k}
    greet(n, peers)


    def hop(way, g, h, shard):
        return pltpu.make_async_remote_copy(
            src_ref=full.at[g, shard, mine],
            dst_ref=full.at[g, shard, mine],
            send_sem=send_sem.at[way, g, h],
            recv_sem=recv_sem.at[way, g, h],
            device_id={"dp": z + 1 - 2 * way},
            device_id_type=MESH,
        )

    def across(way, g, h, shard, rows):
        return pltpu.make_async_remote_copy(
            src_ref=full.at[g, shard, rows],
            dst_ref=full.at[g, shard, rows],
            send_sem=psend_sem.at[way, g, h],
            recv_sem=precv_sem.at[way, g, h],
            device_id=other_core,
            device_id_type=MESH,
        )

    def send_own(g):
        @pl.when(z < last)
        def _():
            hop(0, g, 0, z).start()

        @pl.when(z > 0)
        def _():
            hop(1, g, 0, z).start()

    def gather_tick(m):
        s = m % last + 1
        g = m // last - (s - 1)

        @pl.when((s == 1) & (g < units - 1))
        def _():
            send_own(g + 1)

        @pl.when((g >= 0) & (g < units))
        def _():
            @pl.when(z >= s)
            def _():
                hop(0, g, s - 1, z - s).wait_recv()

                @pl.when(z < last)
                def _():
                    hop(0, g, s, z - s).start()

                across(0, g, s - 1, z - s, mine).start()

            @pl.when(z + s <= last)
            def _():
                hop(1, g, s - 1, z + s).wait_recv()

                @pl.when(z > 0)
                def _():
                    hop(1, g, s, z + s).start()

                across(1, g, s - 1, z + s, mine).start()

    def need(u):
        def one(i, carry):
            s = i + 1

            @pl.when(z >= s)
            def _():
                across(0, u, s - 1, z - s, theirs).wait_recv()

            @pl.when(z + s <= last)
            def _():
                across(1, u, s - 1, z + s, theirs).wait_recv()

            return carry

        lax.fori_loop(0, last, one, 0)

    def send_kv(s):
        rows = pl.ds(pl.multiple_of(k * rows_all, rows_all), rows_all)
        return pltpu.make_async_remote_copy(
            src_ref=kv.at[s, :, rows],
            dst_ref=kv.at[s, :, rows],
            send_sem=kvsend_sem.at[s],
            recv_sem=kvrecv_sem.at[s],
            device_id=other_core,
            device_id_type=MESH,
        )


    def exchange_from(outgoing, g):
        return pltpu.make_async_remote_copy(
            src_ref=outgoing,
            dst_ref=swap.at[g],
            send_sem=xsend_sem.at[g],
            recv_sem=xrecv_sem.at[g],
            device_id=other_core,
            device_id_type=MESH,
        )

    def slot_of(way, i):
        return i if way == 0 else n - i

    def pass_on(way, g, i):
        slot = slot_of(way, i)
        return pltpu.make_async_remote_copy(
            src_ref=line.at[g, slot],
            dst_ref=line.at[g, slot],
            send_sem=lsend_sem.at[way, g, i],
            recv_sem=lrecv_sem.at[way, g, i],
            device_id={"dp": z + 1 - 2 * way},
            device_id_type=MESH,
        )

    my_part = pl.ds(pl.multiple_of(k * HID, HID), HID)
    their_part = pl.ds(pl.multiple_of((1 - k) * HID, HID), HID)

    def keep(g):
        return pltpu.make_async_copy(outbox.at[g % boxes], total.at[g, my_part], keep_sem.at[g])

    def share(g, rows):
        return pltpu.make_async_remote_copy(
            src_ref=outbox.at[g % boxes],
            dst_ref=total.at[g, rows],
            send_sem=fsend_sem.at[g],
            recv_sem=frecv_sem.at[g],
            device_id=other_core,
            device_id_type=MESH,
        )

    def fetch_swapped(g, swap_in):
        @pl.when(g >= 0)
        def _():
            exchange_from(swap_in, g).wait_recv()
            pltpu.make_async_copy(swap.at[g], swap_in, swap_sem).start()

    def put_held(g):
        return pltpu.make_async_copy(held.at[g % depth], kept.at[g], held_sem.at[g % depth])

    def prepare(g, swap_in):
        @pl.when(g >= 0)
        def _():
            pltpu.make_async_copy(swap.at[g], swap_in, swap_sem).wait()

            def one(j, carry):
                held[g % depth, j] += swap_in[j].astype(jnp.float32)
                return carry

            lax.fori_loop(0, n, one, 0)
            put_held(g).start()

    def wait_put(g):
        @pl.when(g >= 0)
        def _():
            put_held(g).wait()

    def piece_copy(way, g, i, slot):
        shard = n - 1 - i if way == 0 else i
        return pltpu.make_async_copy(kept.at[g, shard], pieces.at[way, slot], piece_sem.at[way, slot])

    def box_copy(g):
        return pltpu.make_async_copy(kept.at[g, z], outbox.at[g % boxes], box_sem.at[g % boxes])

    def needs(way, t):
        distance = z if way == 0 else last - z
        m = t - LAG * distance
        g, i = m // last, m % last
        return g, i, (m >= 0) & (m < units * last) & (distance < last - i)

    def fetch_pieces(t):
        for way in range(2):
            g, i, needed = needs(way, t)

            @pl.when(needed)
            def _():
                piece_copy(way, g, i, t % 2).start()

        done = t - last * LAG

        @pl.when((done >= 0) & (done % last == 0))
        def _():
            g = done // last

            @pl.when(g >= boxes)
            def _():
                keep(g - boxes).wait()
                share(g - boxes, my_part).wait_send()

            box_copy(g).start()

    def scatter_step(way, t):
        distance = z if way == 0 else last - z
        m = t - LAG * distance
        g, i, needed = needs(way, t)
        slot = slot_of(way, i)

        @pl.when(needed)
        def _():
            piece_copy(way, g, i, t % 2).wait()

        @pl.when((m >= 0) & (m < units * last) & (distance > 0) & (distance <= last - i))
        def _():
            pass_on(way, g, i).wait_recv()

        @pl.when(needed)
        def _():
            @pl.when(distance == 0)
            def _():
                line[g, slot] = pieces[way, t % 2].astype(jnp.bfloat16)

            @pl.when(distance > 0)
            def _():
                line[g, slot] = (line[g, slot].astype(jnp.float32) + pieces[way, t % 2]).astype(jnp.bfloat16)

            pass_on(way, g, i).start()

    def finish(g):
        box = g % boxes
        box_copy(g).wait()

        @pl.when(z > 0)
        def _():
            outbox[box] += line[g, slot_of(0, n - 1 - z)].astype(jnp.float32)

        @pl.when(z < last)
        def _():
            outbox[box] += line[g, slot_of(1, z)].astype(jnp.float32)

        keep(g).start()
        share(g, my_part).start()

    def scatter_tick(t):
        fetch_pieces(t + 1)
        scatter_step(0, t)
        scatter_step(1, t)
        done = t - last * LAG

        @pl.when((done >= 0) & (done % last == 0))
        def _():
            finish(done // last)

    def run_ticks(gather_from, gather_count, scatter_from, scatter_count):
        def one_gather(i, carry):
            gather_tick(gather_from + i)
            return carry

        def one_scatter(i, carry):
            scatter_tick(scatter_from + i)
            return carry

        lax.fori_loop(0, gather_count, one_gather, 0)
        lax.fori_loop(0, scatter_count, one_scatter, 0)

    def forward_backward(
        normed, cot, stage, raw_in, raw_out, packed, wbuf, x, qg, dkv, back, dkv_tmp, mask, outgoing, swap_in
    ):

        def exchange(g):
            return exchange_from(outgoing.at[g % 2], g)

        ticks = run_ticks

        part = stage.shape[1]
        norm_blocks = rows_all // part

        def fetch_rows(i):
            rows = pl.ds(pl.multiple_of(i * part, part), part)
            return pltpu.make_async_copy(tokens.at[rows], stage.at[i % 2], rows_sem.at[i % 2])

        def normalize(i):
            @pl.when(i + 1 < norm_blocks)
            def _():
                fetch_rows(i + 1).start()

            fetch_rows(i).wait()

            def few(r, c):
                sub = pl.ds(pl.multiple_of(r * 64, 64), 64)
                there = pl.ds(pl.multiple_of(i * part + r * 64, 64), 64)
                inputs = stage[i % 2, sub, :].astype(jnp.float32)
                centered = inputs - jnp.mean(inputs, 1, keepdims=True)
                inv_dev = lax.rsqrt(jnp.mean(centered * centered, 1, keepdims=True) + norm_eps)
                normed[there, :] = (
                    centered * inv_dev * vec_ref[NIN + 1 : NIN + 2, :] + vec_ref[NIN + 2 : NIN + 3, :]
                ).astype(jnp.bfloat16)
                lane = lax.broadcasted_iota(jnp.int32, (64, LANES), 1)
                stats[there, :] = jnp.where(lane == 0, jnp.mean(inputs, 1, keepdims=True), inv_dev)
                return c

            lax.fori_loop(0, part // 64, few, 0)

        def hidden_place(i):
            return i * HID // cols_all, pl.multiple_of(i * HID % cols_all, HID)

        def fetch_raw(u, start):
            s, slot = u // 3, u % 2

            def each(copies):
                for copy in copies:
                    copy.start() if start else copy.wait()

            @pl.when(u % 3 == 1)
            def _():
                cols = pl.ds(pl.multiple_of(s * LANES, LANES), LANES)
                each(
                    [
                        pltpu.make_async_copy(
                            in_w.at[g, :, cols],
                            raw_in.at[slot, :, pl.ds(g * LANES, LANES)],
                            pack_sem.at[slot, g],
                        )
                        for g in range(3)
                    ]
                    + [
                        pltpu.make_async_copy(
                            out_w.at[0, cols], raw_out.at[slot, pl.ds(0, LANES)], pack_sem.at[slot, 3]
                        )
                    ]
                )

            @pl.when(u % 3 != 1)
            def _():
                group, first = hidden_place(2 * s + (u % 3) // 2)
                cols = pl.ds(first, HID)
                each(
                    [
                        pltpu.make_async_copy(
                            in_w.at[3 + group, :, cols],
                            raw_in.at[slot, :, pl.ds(0, HID)],
                            pack_sem.at[slot, 0],
                        ),
                        pltpu.make_async_copy(out_w.at[1 + group, cols], raw_out.at[slot], pack_sem.at[slot, 1]),
                    ]
                )

        def put_packed(u):
            return pltpu.make_async_copy(packed.at[u % 2], full.at[u, z], put_sem.at[u % 2])

        def pack(u):
            slot = u % 2
            fetch_raw(u, False)

            @pl.when(u % 3 == 1)
            def _():
                packed[slot, :, :ATT] = raw_in[slot].astype(jnp.bfloat16)
                packed[slot, :, ATT:] = raw_out[slot, :LANES, :].astype(jnp.bfloat16).T

            @pl.when(u % 3 != 1)
            def _():
                packed[slot, :, :HID] = raw_in[slot, :, :HID].astype(jnp.bfloat16)
                packed[slot, :, HID:] = raw_out[slot].astype(jnp.bfloat16).T

            put_packed(u).start()

        def fetch_weights(u):
            return pltpu.make_async_copy(full.at[u], wbuf, weight_sem)

        def next_weights(u):
            @pl.when(u < units)
            def _():
                need(u)
                fetch_weights(u).start()

        def column_sums(split):
            ones = jnp.ones((8, rows_all), jnp.bfloat16)
            return dot(ones, x[:, :split])[0:1, :]

        def save(u):
            return pltpu.make_async_copy(x, saved.at[u], save_sem)

        def wait_saved(u):
            @pl.when(u > 0)
            def _():
                save(u - 1).wait()

        def gradients(u, split):
            @pl.when(u >= 2)
            def _():
                exchange(u - 2).wait_send()

            def part(first, end, j):
                turns = [(first, min(end, split), normed), (max(first, split), end, cot)]
                return [
                    (low, high, dot(x[:, low:high], rows[:, pl.ds(pl.multiple_of(j * size, size), size)], TN))
                    for low, high, rows in turns
                    if low < high
                ]

            for core in range(2):

                @pl.when(k == core)
                def _():
                    def one(j, carry):
                        for low, high, value in part(core * HID, (core + 1) * HID, j):
                            held[u % depth, j, low - core * HID : high - core * HID] = value
                        for low, high, value in part((1 - core) * HID, (2 - core) * HID, j):
                            outgoing[u % 2, j, low - (1 - core) * HID : high - (1 - core) * HID] = value.astype(
                                jnp.bfloat16
                            )
                        return carry

                    lax.fori_loop(0, n, one, 0)

            exchange(u).start()

        block = min(512, rows_all)

        def hidden_unit(u, i_hidden, at, out_at):
            fetch_weights(u).wait()
            wait_saved(u)
            wait_put(u - 2)

            def one(i, carry):
                rows = pl.ds(pl.multiple_of(i * block, block), block)
                pre = dot(normed[rows, :], wbuf[:, :, :HID].reshape(width, HID)) + bias_ref[u][:, :HID]
                value, slope = gelu_both(pre)
                x[rows, HID:] = value.astype(jnp.bfloat16)
                grad = dot(cot[rows, :], wbuf[:, :, HID:].reshape(width, HID))
                x[rows, :HID] = (grad * slope).astype(jnp.bfloat16)
                return carry

            lax.fori_loop(0, rows_all // block, one, 0)
            save(u).start()
            fetch_swapped(u - 1, swap_in)

            ticks(at + lead, in_hidden, out_at - behind, out_hidden)
            next_weights(u + 1)
            prepare(u - 1, swap_in)
            group, first = hidden_place(i_hidden)
            vec[pl.ds(3 + group, 1), pl.ds(first, HID)] = column_sums(HID)
            gradients(u, HID)


        qblock = mask.shape[1]
        window = mask.shape[0]
        qblocks = rows_all // qblock

        def rope(v, rows, sign):
            half_rot = ROT // 2
            lane = lax.broadcasted_iota(jnp.int32, v.shape, 1) % HD
            ahead = pltpu.roll(v, LANES - half_rot, 1)
            behind = pltpu.roll(v, half_rot, 1)
            other = jnp.where(lane < half_rot, -ahead, behind)
            return v * cos_ref[rows, :] + other * (sign * sin_ref[rows, :])

        def recv_kv(s):
            rows = pl.ds(pl.multiple_of((1 - k) * rows_all, rows_all), rows_all)
            return pltpu.make_async_remote_copy(
                src_ref=kv.at[s, :, rows],
                dst_ref=kv.at[s, :, rows],
                send_sem=kvsend_sem.at[s],
                recv_sem=kvrecv_sem.at[s],
                device_id=other_core,
                device_id_type=MESH,
            )

        def send_dkv(s):
            return pltpu.make_async_remote_copy(
                src_ref=dkv.at[:, pl.ds(0, rows_all)],
                dst_ref=dkv_other.at[s],
                send_sem=dsend_sem.at[s],
                recv_sem=drecv_sem.at[s],
                device_id=other_core,
                device_id_type=MESH,
            )

        def send_first(s):
            return pltpu.make_async_remote_copy(
                src_ref=qg.at[:, pl.ds(0, qblock)],
                dst_ref=moved.at[s],
                send_sem=msend_sem.at[s],
                recv_sem=mrecv_sem.at[s],
                device_id=other_core,
                device_id_type=MESH,
            )

        def send_back(s):
            return pltpu.make_async_remote_copy(
                src_ref=back,
                dst_ref=returned.at[s],
                send_sem=bsend_sem.at[s],
                recv_sem=brecv_sem.at[s],
                device_id=other_core,
                device_id_type=MESH,
            )

        def send_extra(s):
            return pltpu.make_async_remote_copy(
                src_ref=dkv.at[:, pl.ds(rows_all, qblock)],
                dst_ref=extra.at[s],
                send_sem=esend_sem.at[s],
                recv_sem=erecv_sem.at[s],
                device_id=other_core,
                device_id_type=MESH,
            )

        def sent(s):
            @pl.when(k == 1)
            def _():
                send_dkv(s).wait_send()
                send_first(s).wait_send()

            @pl.when(k == 0)
            def _():
                send_back(s).wait_send()
                send_extra(s).wait_send()

        def attend(s, q_low, g_low, first_query, first_key, span):
            keys = pl.ds(first_key, span)
            key_at = first_key + lax.broadcasted_iota(jnp.int32, (span, qblock), 0)
            query_at = first_query + lax.broadcasted_iota(jnp.int32, (span, qblock), 1)
            begin = begin_ref[0:1, pl.ds(pl.multiple_of(first_query, qblock), qblock)]
            mask[:span] = jnp.where((key_at >= begin) & (key_at <= query_at), 0.0, -1e30)
            lane = lax.broadcasted_iota(jnp.int32, (qblock, LANES), 1)
            att = jnp.zeros((qblock, LANES), jnp.float32)
            dq = jnp.zeros((qblock, LANES), jnp.float32)
            for head in range(2):
                inside = (lane >= head * HD) & (lane < (head + 1) * HD)
                q_own = jnp.where(inside, q_low, jnp.zeros((qblock, LANES), jnp.bfloat16))
                g_own = jnp.where(inside, g_low, jnp.zeros((qblock, LANES), jnp.bfloat16))
                scores = dot(kv[s, 0, keys, :], q_own, NT) + mask[:span]
                weights = jnp.exp(scores - jnp.max(scores, 0, keepdims=True))
                probs = weights * (1.0 / jnp.sum(weights, 0, keepdims=True))
                probs_low = probs.astype(jnp.bfloat16)
                grad_probs = dot(kv[s, 1, keys, :], g_own, NT)
                inner = jnp.sum(probs * grad_probs, 0, keepdims=True)
                grad_scores = (probs * (grad_probs - inner)).astype(jnp.bfloat16)
                att = jnp.where(inside, dot(probs_low, kv[s, 1, keys, :], TN), att)
                dq = jnp.where(inside, dot(grad_scores, kv[s, 0, keys, :], TN), dq)
                dkv[1, keys, :] += dot(probs_low, g_own)
                dkv[0, keys, :] += dot(grad_scores, q_own)
            return att, dq * HD**-0.5

        def attend_own(s, b, first_key, span):
            rows = pl.ds(pl.multiple_of(b * qblock, qblock), qblock)
            att, dq = attend(s, qg[0, rows, :], qg[1, rows, :], k * rows_all + b * qblock, first_key, span)
            x[rows, ATT:] = att.astype(jnp.bfloat16)
            x[rows, :LANES] = rope(dq, rows, -1.0).astype(jnp.bfloat16)

        def attention_unit(u, s, at, out_at):
            fetch_weights(u).wait()
            wait_saved(u)
            wait_put(u - 2)

            @pl.when(s > 0)
            def _():
                sent(s - 1)

            def project(i, carry):
                rows = pl.ds(pl.multiple_of(i * block, block), block)
                there = pl.ds(pl.multiple_of(k * rows_all + i * block, block), block)
                pre = dot(normed[rows, :], wbuf[:, :, :ATT].reshape(width, ATT)) + bias_ref[u][:, :ATT]
                query = rope(pre[:, :LANES], rows, 1.0).astype(jnp.bfloat16)
                qg[0, rows, :] = query * jnp.bfloat16(HD**-0.5)
                kv[s, 0, there, :] = rope(pre[:, LANES : 2 * LANES], rows, 1.0).astype(jnp.bfloat16)
                kv[s, 1, there, :] = pre[:, 2 * LANES :].astype(jnp.bfloat16)
                return carry

            lax.fori_loop(0, rows_all // block, project, 0)
            send_kv(s).start()

            def project_grad(i, carry):
                rows = pl.ds(pl.multiple_of(i * block, block), block)
                grad = dot(cot[rows, :], wbuf[:, :, ATT:].reshape(width, LANES))
                qg[1, rows, :] = grad.astype(jnp.bfloat16)
                return carry

            lax.fori_loop(0, rows_all // block, project_grad, 0)

            @pl.when(k == 1)
            def _():
                send_first(s).start()

            dkv[...] = jnp.zeros_like(dkv)
            per_block = in_attention // qblocks
            early = in_attention - per_block * qblocks
            out_block = out_attention // qblocks
            out_early = out_attention - out_block * qblocks
            fetch_swapped(u - 1, swap_in)
            ticks(at + lead, early, out_at - behind, out_early)
            prepare(u - 1, swap_in)
            recv_kv(s).wait_recv()

            def turn_of(b, carry):
                @pl.when((k == 1) & (b < qblocks - 1))
                def _():
                    first_key = pl.multiple_of(rows_all + (b + 2) * qblock - window, qblock)
                    attend_own(s, b + 1, first_key, window)

                @pl.when((k == 1) & (b == qblocks - 2))
                def _():
                    send_dkv(s).start()

                for own in range(qblocks):

                    @pl.when((k == 0) & (b == (own if own > 1 else 0)))
                    def _():
                        attend_own(s, own, 0, (own + 1) * qblock)

                @pl.when((k == 0) & (b == 1))
                def _():
                    send_first(s).wait_recv()
                    att, dq = attend(s, moved[s, 0], moved[s, 1], rows_all, 0, window)
                    back[0], back[1] = att, dq
                    send_back(s).start()
                    send_extra(s).start()

                ticks(
                    at + early + b * per_block + lead,
                    per_block,
                    out_at + out_early + b * out_block - behind,
                    out_block,
                )
                return carry

            lax.fori_loop(0, qblocks, turn_of, 0)
            first_rows, own_rows = pl.ds(0, qblock), pl.ds(0, rows_all)

            @pl.when(k == 1)
            def _():
                send_back(s).wait_recv()
                send_extra(s).wait_recv()
                x[first_rows, ATT:] = returned[s, 0].astype(jnp.bfloat16)
                x[first_rows, :LANES] = rope(returned[s, 1], first_rows, -1.0).astype(jnp.bfloat16)
                dkv[:, pl.ds(rows_all, qblock)] += extra[s]

            @pl.when(k == 0)
            def _():
                send_dkv(s).wait_recv()
                copy = pltpu.make_async_copy(dkv_other.at[s], dkv_tmp, load_sem)
                copy.start()
                copy.wait()
                dkv[:, own_rows] += dkv_tmp[...]

            def turn(i, carry):
                rows = pl.ds(pl.multiple_of(i * qblock, qblock), qblock)
                there = pl.ds(pl.multiple_of(k * rows_all + i * qblock, qblock), qblock)
                x[rows, LANES : 2 * LANES] = rope(dkv[0, there, :], rows, -1.0).astype(jnp.bfloat16)
                x[rows, 2 * LANES : ATT] = dkv[1, there, :].astype(jnp.bfloat16)
                return carry

            lax.fori_loop(0, qblocks, turn, 0)
            save(u).start()
            next_weights(u + 1)
            bias_grad = column_sums(ATT)
            for g in range(3):
                vec[g : g + 1, pl.ds(pl.multiple_of(s * LANES, LANES), LANES)] = bias_grad[
                    :, g * LANES : (g + 1) * LANES
                ]
            gradients(u, ATT)


        cot_copy = pltpu.make_async_copy(cot_hbm, cot, save_sem)
        cot_copy.start()
        fetch_rows(0).start()
        fetch_raw(0, True)
        fetch_raw(1, True)
        for u in range(2):
            pack(u)
            put_packed(u).wait()
            if u == 0:
                send_own(0)
            fetch_raw(u + 2, True)

        def begin_step(i, carry):
            @pl.when(i + 2 < units)
            def _():
                pack(i + 2)

            @pl.when(i < norm_blocks)
            def _():
                normalize(i)

            @pl.when(i + 2 < units)
            def _():
                put_packed(i + 2).wait()

            @pl.when(i + 4 < units)
            def _():
                fetch_raw(i + 4, True)

            @pl.when(i < lead)
            def _():
                gather_tick(i)

            return carry

        lax.fori_loop(0, max(units - 2, norm_blocks, lead), begin_step, 0)
        cot_copy.wait()
        next_weights(0)
        vec[...] = jnp.zeros_like(vec)
        vec[NIN : NIN + 1, :] = dot(jnp.ones((8, rows_all), jnp.bfloat16), cot[:, columns])[0:1, :]

        def super_step(s, carry):
            at = s * per_step
            out_at = s * (2 * out_hidden + out_attention)
            hidden_unit(3 * s, 2 * s, at, out_at)
            attention_unit(3 * s + 1, s, at + in_hidden, out_at + out_hidden)
            hidden_unit(
                3 * s + 2, 2 * s + 1, at + in_hidden + in_attention, out_at + out_hidden + out_attention
            )
            return carry

        lax.fori_loop(0, steps, super_step, 0)

        save(units - 1).wait()
        exchange(units - 2).wait_send()
        exchange(units - 1).wait_send()

        sent(steps - 1)


    square = peers == 4
    upper, lower = pl.ds(0, rows_all // 2), pl.ds(rows_all // 2, rows_all // 2)

    def beside(axis):
        return tensor + 1 - 2 * (tensor % 2) if axis == 0 else tensor + 2 - 4 * (tensor // 2)

    def block_at(i):
        if not square:
            return lax.rem(tensor + 1 + i, peers)
        return jnp.where(
            i == 0, 3 - tensor, jnp.where(i == 1, beside(0), jnp.where(i == 2, beside(1), tensor))
        )

    def tensor_copy(blocks, what, message):
        if square:
            slot, rows, axis = ((0, upper, 0), (0, lower, 1), (1, upper, 0), (2, lower, 1), (1, lower, 0), (2, upper, 1))[
                message
            ]
            source, there = blocks.at[what, slot, rows], arrived.at[what, slot, rows]
            target = beside(axis)
        else:
            source, there = blocks.at[what, message], arrived.at[what, message]
            target = block_at(message)
        return pltpu.make_async_remote_copy(
            src_ref=source,
            dst_ref=there,
            send_sem=tsend_sem.at[what, message],
            recv_sem=trecv_sem.at[what, message],
            device_id={"tensor": target},
            device_id_type=MESH,
        )

    def sums_copy(i):
        return pltpu.make_async_remote_copy(
            src_ref=sums,
            dst_ref=sums_in.at[i],
            send_sem=ssend_sem.at[i],
            recv_sem=srecv_sem.at[i],
            device_id={"tensor": lax.rem(tensor + 1 + i, peers)},
            device_id_type=MESH,
        )

    def finals(xs, tile, blocks, swap_in, passing):
        part = size // 2
        tiles = 4 * peers
        remote = 2 * (peers - 1)

        def fetch_tile(q):
            i = jnp.where(q < remote, q, jnp.where(q < 2 * remote, q - remote, remote + q % 2)) // 2
            shard = block_at(i)
            rows = pl.ds(pl.multiple_of(q % 2 * part, part), part)
            return pltpu.make_async_copy(full.at[:, shard, rows], tile.at[q % 2], tile_sem.at[q % 2])

        fetch_xs = pltpu.make_async_copy(saved, xs.at[pl.ds(0, units)], load_sem)
        fetch_xs.start()
        fetch_tile(0).start()
        fetch_swapped(units - 1, swap_in)
        prepare(units - 1, swap_in)
        wait_put(units - 2)
        wait_put(units - 1)
        fetch_xs.wait()
        block = min(512, rows_all)

        def products(q, what, store):
            @pl.when(q + 1 < tiles)
            def _():
                fetch_tile(q + 1).start()

            fetch_tile(q).wait()

            def one(r, carry):
                rows = pl.ds(pl.multiple_of(r * block, block), block)
                value = None
                for u in range(units):
                    split = ATT if u % 3 == 1 else HID
                    part_of = slice(0, split) if what == 0 else slice(split, WIDE)
                    product = dot(xs[u, rows, part_of], tile[q % 2, u, :, part_of], NT)
                    value = product if value is None else value + product
                store(r, value)
                return carry

            lax.fori_loop(0, rows_all // block, one, 0)

        scatter_at = steps * (2 * out_hidden + out_attention) - behind
        scatter_count = (units - 1) * last + last * LAG + 1 - scatter_at
        tile_count = scatter_count * 2 // 5 // remote
        rest_at, rest_count = scatter_at + tile_count * remote, scatter_count - tile_count * remote
        cuts = [rest_at + rest_count * share_of // 16 for share_of in (0, 2, 5, 8, 11, 13, 16)]

        def rest(i):
            run_ticks(0, 0, cuts[i], cuts[i + 1] - cuts[i])

        def remote_tile(what, i):
            def one(h, carry):
                def store(r, value):
                    rows = pl.ds(pl.multiple_of(r * block, block), block)
                    cols = pl.ds(pl.multiple_of(h * part, part), part)
                    blocks[what, i, rows, cols] = value.astype(jnp.bfloat16)

                q = 2 * i + h
                products(q + what * remote, what, store)
                if what == 1:
                    run_ticks(0, 0, scatter_at + q * tile_count, tile_count)
                return carry

            lax.fori_loop(0, 2, one, 0)

        def send(what, *messages):
            for message in messages:
                tensor_copy(blocks, what, message).start()

        def add_half(what, slot, rows, message, onward):
            tensor_copy(blocks, what, message).wait_recv()
            copy = pltpu.make_async_copy(
                arrived.at[what, 0, rows], passing, load_sem
            )
            copy.start()
            copy.wait()
            blocks[what, slot, rows, :] = (
                blocks[what, slot, rows, :].astype(jnp.float32) + passing[...].astype(jnp.float32)
            ).astype(jnp.bfloat16)
            send(what, onward)

        if square:
            remote_tile(0, 0)
            send(0, 0, 1)
            remote_tile(0, 1)
            send(0, 2)
            remote_tile(0, 2)
            send(0, 3)
            remote_tile(1, 0)
            add_half(0, 1, lower, 1, 4)
            add_half(0, 2, upper, 0, 5)
            send(1, 0, 1)
            remote_tile(1, 1)
            send(1, 2)
            remote_tile(1, 2)
            send(1, 3)
        else:
            for what in range(2):

                def one_block(i, carry):
                    remote_tile(what, i)
                    send(what, i)
                    return carry

                lax.fori_loop(0, peers - 1, one_block, 0)

        for what in range(2):
            for h in range(2):

                def store(r, value):
                    for a in range(block // HID):
                        held[what, r * (block // HID) + a, :, h * part : (h + 1) * part] = value[
                            a * HID : (a + 1) * HID
                        ]

                products(2 * remote + 2 * what + h, what, store)

        rest(0)
        if square:
            add_half(1, 1, lower, 1, 4)
            add_half(1, 2, upper, 0, 5)

        tok_at, cot_at, out_at = 2 * (peers - 1), 2 * (peers - 1) + 1, 2 * (peers - 1) + 2
        bring = [
            pltpu.make_async_copy(tokens.at[:, columns], xs.at[tok_at, :, pl.ds(0, size)], tile_sem.at[0]),
            pltpu.make_async_copy(cot_hbm.at[:, columns], xs.at[cot_at, :, pl.ds(0, size)], tile_sem.at[1]),
        ]
        for copy in bring:
            copy.start()
        for copy in bring:
            copy.wait()

        first = 1 if square else 0
        count = peers - 1 - first

        def collect(what):
            for message in range(2, 6) if square else ():
                tensor_copy(blocks, what, message).wait_recv()

            def one(i, carry):
                if not square:
                    tensor_copy(blocks, what, i).wait_recv()
                copy = pltpu.make_async_copy(
                    arrived.at[what, first + i], xs.at[what * count + i, :, pl.ds(0, size)], load_sem
                )
                copy.start()
                copy.wait()
                return carry

            lax.fori_loop(0, count, one, 0)

        def summed(what, r, rows):
            value = held[what, r]
            for i in range(count):
                value += xs[what * count + i, rows, :size].astype(jnp.float32)
            return value

        gain = vec_ref[NIN + 1 : NIN + 2, columns]
        ones = jnp.ones((8, size), jnp.float32)

        def unit_of(rows):
            token = xs[tok_at, rows, :size].astype(jnp.float32)
            return (token - stats[rows, 0:1]) * stats[rows, 1:2]

        rest(1)
        collect(0)

        def first_pass(r, carry):
            rows = pl.ds(pl.multiple_of(r * HID, HID), HID)
            grad = summed(0, r, rows)
            held[0, r] = grad
            unit = unit_of(rows)
            scaled = grad * gain
            sums[0:8, rows] = lax.dot_general(
                ones, scaled, NT, precision=lax.Precision.HIGHEST, preferred_element_type=jnp.float32
            )
            sums[8:16, rows] = lax.dot_general(
                ones, scaled * unit, NT, precision=lax.Precision.HIGHEST, preferred_element_type=jnp.float32
            )
            vec[NIN + 1 : NIN + 2, :] += jnp.sum(grad * unit, 0, keepdims=True)
            vec[NIN + 2 : NIN + 3, :] += jnp.sum(grad, 0, keepdims=True)
            return carry

        lax.fori_loop(0, rows_all // HID, first_pass, 0)
        for i in range(peers - 1):
            sums_copy(i).start()
        to_core = pltpu.make_async_remote_copy(
            src_ref=vec, dst_ref=vec_core, send_sem=vsend_sem.at[0], recv_sem=vrecv_sem.at[0],
            device_id=other_core, device_id_type=MESH,
        )
        to_core.start()
        rest(2)
        for i in range(peers - 1):
            sums_copy(i).wait_recv()
        inv_width = 1.0 / width

        def second_pass(r, carry):
            rows = pl.ds(pl.multiple_of(r * HID, HID), HID)
            means = sums[:, rows]
            for i in range(peers - 1):
                means += sums_in[i, :, rows]
            means = (means * inv_width).T
            unit = unit_of(rows)
            held[0, r] = stats[rows, 1:2] * (
                held[0, r] * gain - means[:, 0:1] - unit * means[:, 8:9]
            ) + xs[cot_at, rows, :size].astype(jnp.float32)
            return carry

        lax.fori_loop(0, rows_all // HID, second_pass, 0)
        put_grad = pltpu.make_async_copy(held.at[0, pl.ds(0, rows_all // HID)], token_grad, out_sem.at[0])
        put_grad.start()

        rest(3)
        to_core.wait_recv()
        vec_line[z] = vec[...] + vec_core[...]

        def along_dp(i):
            return pltpu.make_async_remote_copy(
                src_ref=vec_line.at[z], dst_ref=vec_line.at[z],
                send_sem=vsend_sem.at[1 + i], recv_sem=vrecv_sem.at[1 + i],
                device_id={"dp": lax.rem(z + 1 + i, n)}, device_id_type=MESH,
            )

        def from_dp(i):
            there = lax.rem(z + n - 1 - i, n)
            return pltpu.make_async_remote_copy(
                src_ref=vec_line.at[there], dst_ref=vec_line.at[there],
                send_sem=vsend_sem.at[1 + i], recv_sem=vrecv_sem.at[1 + i],
                device_id={"dp": lax.rem(z + 1 + i, n)}, device_id_type=MESH,
            )

        for i in range(n - 1):
            along_dp(i).start()
        for i in range(n - 1):
            from_dp(i).wait_recv()
        vec_sum = vec_line[0]
        for i in range(1, n):
            vec_sum += vec_line[i]
        vec_all[tensor] = vec_sum

        def along_tensor(i):
            return pltpu.make_async_remote_copy(
                src_ref=vec_all.at[tensor], dst_ref=vec_all.at[tensor],
                send_sem=vsend_sem.at[n + i], recv_sem=vrecv_sem.at[n + i],
                device_id={"tensor": lax.rem(tensor + 1 + i, peers)}, device_id_type=MESH,
            )

        def from_tensor(i):
            there = lax.rem(tensor + peers - 1 - i, peers)
            return pltpu.make_async_remote_copy(
                src_ref=vec_all.at[there], dst_ref=vec_all.at[there],
                send_sem=vsend_sem.at[n + i], recv_sem=vrecv_sem.at[n + i],
                device_id={"tensor": lax.rem(tensor + 1 + i, peers)}, device_id_type=MESH,
            )

        for i in range(peers - 1):
            along_tensor(i).start()

        rest(4)
        collect(1)
        out_bias = vec_ref[NIN : NIN + 1, columns]

        def third_pass(r, carry):
            rows = pl.ds(pl.multiple_of(r * HID, HID), HID)
            value = xs[tok_at, rows, :size].astype(jnp.float32) + (summed(1, r, rows) + out_bias)
            xs[out_at, rows, :size] = value.astype(jnp.bfloat16)
            return carry

        lax.fori_loop(0, rows_all // HID, third_pass, 0)
        put_result = pltpu.make_async_copy(xs.at[out_at, :, pl.ds(0, size)], result, out_sem.at[1])
        put_result.start()
        rest(5)

        for i in range(peers - 1):
            from_tensor(i).wait_recv()
        vec_grad[...] = vec_all[...]
        put_grad.wait()
        put_result.wait()
        to_core.wait_send()
        for i in range(n - 1):
            along_dp(i).wait_send()
        for i in range(peers - 1):
            along_tensor(i).wait_send()
            sums_copy(i).wait_send()
        for i in range(6 if square else peers - 1):
            tensor_copy(blocks, 0, i).wait_send()
            tensor_copy(blocks, 1, i).wait_send()

    low, wide = jnp.bfloat16, jnp.float32
    window, qblock = rows_all + 256, 256
    pl.run_scoped(
        forward_backward,
        pltpu.VMEM((rows_all, width), low),
        pltpu.VMEM((rows_all, width), low),
        pltpu.VMEM((2, rows_all // 8, width), low),
        pltpu.VMEM((2, size, ATT), wide),
        pltpu.VMEM((2, HID, size), wide),
        pltpu.VMEM((2, size, WIDE), low),
        pltpu.VMEM((n, size, WIDE), low),
        pltpu.VMEM((rows_all, WIDE), low),
        pltpu.VMEM((2, rows_all, LANES), low),
        pltpu.VMEM((2, 2 * rows_all, LANES), wide),
        pltpu.VMEM((2, 256, LANES), wide),
        pltpu.VMEM((2, rows_all, LANES), wide),
        pltpu.VMEM((window, qblock), wide),
        pltpu.VMEM((2, n, HID, size), low),
        pltpu.VMEM((n, HID, size), low),
    )
    pl.run_scoped(
        finals,
        pltpu.VMEM((max(units, 2 * peers + 1), rows_all, WIDE), low),
        pltpu.VMEM((2, units, size // 2, WIDE), low),
        pltpu.VMEM((2, peers - 1, rows_all, size), low),
        pltpu.VMEM((n, HID, size), low),
        pltpu.VMEM((rows_all // 2, size), low),
    )


    def drain_kv(s, carry):
        send_kv(s).wait_send()
        return carry

    lax.fori_loop(0, steps, drain_kv, 0)

    def drain(m, carry):
        g, s = m // last, m % last + 1

        @pl.when(s == 1)
        def _():
            @pl.when(z < last)
            def _():
                hop(0, g, 0, z).wait_send()

            @pl.when(z > 0)
            def _():
                hop(1, g, 0, z).wait_send()

            @pl.when(g >= units - boxes)
            def _():
                keep(g).wait()
                share(g, my_part).wait_send()

            share(g, their_part).wait_recv()

        @pl.when(z >= s)
        def _():
            @pl.when(z < last)
            def _():
                hop(0, g, s, z - s).wait_send()

            across(0, g, s - 1, z - s, mine).wait_send()

        @pl.when(z + s <= last)
        def _():
            @pl.when(z > 0)
            def _():
                hop(1, g, s, z + s).wait_send()

            across(1, g, s - 1, z + s, mine).wait_send()

        for way in range(2):
            distance = z if way == 0 else last - z

            @pl.when(distance < last - (s - 1))
            def _():
                pass_on(way, g, s - 1).wait_send()

        return carry

    lax.fori_loop(0, units * last, drain, 0)


def run_block(in_weight, out_weight, tokens, cotangent, bias, vectors, cosine, sine, begin):
    n, peers = lax.axis_size("dp"), lax.axis_size("tensor")
    size, cols_all = in_weight.shape[1:]
    steps = cols_all // LANES
    units = 3 * steps
    rows, width = tokens.shape
    assert width == n * size == peers * cols_all and size == cols_all and rows <= n * HID
    low, wide = jnp.bfloat16, jnp.float32
    anywhere = pl.BlockSpec(memory_space=pl.ANY)
    vm = pl.BlockSpec(memory_space=pltpu.VMEM)
    dma = pltpu.SemaphoreType.DMA
    return pl.pallas_call(
        functools.partial(block_kernel, n, steps, peers),
        out_shape=(
            jax.ShapeDtypeStruct((units, n, size, WIDE), low),
            jax.ShapeDtypeStruct((units, rows, WIDE), low),
            jax.ShapeDtypeStruct((units, WIDE, size), wide),
            jax.ShapeDtypeStruct((units, n, HID, size), low),
            jax.ShapeDtypeStruct((units, n, HID, size), wide),
            jax.ShapeDtypeStruct((steps, 2, rows, LANES), wide),
            jax.ShapeDtypeStruct((2, peers - 1, rows, size), low),
            jax.ShapeDtypeStruct((rows, size), low),
            jax.ShapeDtypeStruct((rows // HID, HID, size), wide),
            jax.ShapeDtypeStruct((peers, 16, size), wide),
        ),
        in_specs=[anywhere] * 4 + [vm] * 5,
        out_specs=[anywhere] * 9 + [vm],
        scratch_shapes=[
            pltpu.VMEM((steps, 2, 2 * rows, LANES), low),
            pltpu.VMEM((steps, 2, 256, LANES), low),
            pltpu.VMEM((steps, 2, 256, LANES), wide),
            pltpu.VMEM((steps, 2, 256, LANES), wide),
            pltpu.VMEM((2, n, HID, size), wide),
            pltpu.VMEM((2, 2, HID, size), wide),
            pltpu.VMEM((units, n + 1, HID, size), low),
            pltpu.VMEM((3, HID, size), wide),
            pltpu.VMEM((rows, LANES), wide),
            pltpu.VMEM((16, size), wide),
            pltpu.VMEM((16, size), wide),
            pltpu.VMEM((n, 16, size), wide),
            pltpu.VMEM((peers, 16, size), wide),
            pltpu.VMEM((16, rows), wide),
            pltpu.VMEM((peers - 1, 16, rows), wide),
            dma((2, units, n)),
            dma((2, units, n)),
            dma((2, units, n)),
            dma((2, units, n)),
            dma((units,)),
            dma((units,)),
            dma((2, units, n - 1)),
            dma((2, units, n - 1)),
            dma((units,)),
            dma((units,)),
            dma((units,)),
            dma((steps,)),
            dma((steps,)),
            dma((steps,)),
            dma((steps,)),
            dma((steps,)),
            dma((steps,)),
            dma((steps,)),
            dma((steps,)),
            dma((steps,)),
            dma((steps,)),
            dma,
            dma,
            dma,
            dma((2, 4)),
            dma((2,)),
            dma((2,)),
            dma,
            dma((2,)),
            dma((2, 2)),
            dma((3,)),
            dma((2, 6 if peers == 4 else peers - 1)),
            dma((2, 6 if peers == 4 else peers - 1)),
            dma((peers - 1,)),
            dma((peers - 1,)),
            dma((n + peers - 1,)),
            dma((n + peers - 1,)),
            dma((2,)),
            dma((2,)),
        ],
        compiler_params=pltpu.CompilerParams(
            collective_id=1, has_side_effects=True, vmem_limit_bytes=VMEM_LIMIT
        ),
        name="parallel_block",
    )(in_weight, out_weight, tokens, cotangent, bias, vectors, cosine, sine, begin)


def adam_kernel(into, chunks, *refs):
    pieces, refs = refs[:chunks], refs[chunks:]
    g = pl.program_id(0)

    def update(weights, turned):
        w, m, v, new_w, new_m, new_v = weights
        for c, piece in enumerate(pieces):
            part = slice(c * LANES, (c + 1) * LANES)
            at = (0, part) if turned else (0, slice(None), part)
            gradient = piece[0] if turned else piece[0].T
            new_w[at], new_m[at], new_v[at] = adamw(
                w[at], gradient, m[at], v[at], rate_matrix, weight_decay
            )

    @pl.when(g < into)
    def _():
        update(refs[:3] + refs[6:9], False)

    @pl.when(g >= into)
    def _():
        update(refs[3:6] + refs[9:], True)


def adam_weights(total, in_arrays, out_arrays):
    into, size, cols_all = in_arrays[0].shape
    outof = out_arrays[0].shape[0]
    chunks = cols_all // LANES

    def place(c, g, h):
        is_in = g < into
        group = jnp.where(is_in, g, g - into)
        lead = jnp.where(is_in, 3, 1)
        i = jnp.maximum((group - lead) * cols_all + c * LANES, 0) // HID
        unit = jnp.where(group < lead, 3 * c + 1, 3 * (i // 2) + 2 * (i % 2))
        lane = jnp.where(
            group < lead, jnp.where(is_in, group, 3), c % 2 + jnp.where(is_in, 0, 2)
        )
        return unit, lane, h

    in_spec = pl.BlockSpec(
        (1, size // 2, cols_all), lambda g, h: (jnp.minimum(g, into - 1), jnp.where(g < into, h, 1), 0)
    )
    out_spec = pl.BlockSpec(
        (1, cols_all, size // 2), lambda g, h: (jnp.maximum(g - into, 0), 0, jnp.where(g < into, 0, h))
    )
    results = pl.pallas_call(
        functools.partial(adam_kernel, into, chunks),
        grid=(into + outof, 2),
        out_shape=tuple(jax.ShapeDtypeStruct(v.shape, jnp.float32) for v in in_arrays + out_arrays),
        in_specs=[pl.BlockSpec((1, LANES, size // 2), functools.partial(place, c)) for c in range(chunks)]
        + [in_spec] * 3
        + [out_spec] * 3,
        out_specs=[in_spec] * 3 + [out_spec] * 3,
        compiler_params=pltpu.CompilerParams(vmem_limit_bytes=VMEM_LIMIT),
        name="adam_weights",
    )(*[total] * chunks, *in_arrays, *out_arrays)
    return results[:3], results[3:]


def layout(lengths_row, row_span):
    seg_ends = jnp.cumsum(lengths_row)
    seg_starts = seg_ends - lengths_row
    places = jnp.arange(row_span, dtype=jnp.int32)
    segment = jnp.sum((places[:, None] >= seg_ends[None, :]).astype(jnp.int32), 1)
    numbers = jnp.arange(lengths_row.shape[0], dtype=jnp.int32)
    return jnp.sum(jnp.where(segment[:, None] == numbers[None, :], seg_starts[None, :], 0), 1)


def rope_tables(places):
    half_rot = ROT // 2
    lane = jnp.arange(2 * HD, dtype=jnp.int32) % HD
    exponent = (lane % half_rot).astype(jnp.float32)
    frequency = 10000.0 ** (-2.0 * exponent / ROT)
    angles = places.astype(jnp.float32)[:, None] * frequency[None, :]
    turned = (lane < ROT)[None, :]
    cosine = jnp.where(turned, jnp.cos(angles), 1.0)
    sine = jnp.where(turned, jnp.sin(angles), 0.0)
    return cosine, sine


def body(
    tokens,
    cotangent,
    lengths,
    in_weight,
    out_weight,
    vectors,
    in_first,
    in_second,
    out_first,
    out_second,
    vec_first,
    vec_second,
):
    local_rows, model_width = tokens.shape
    slice_width = in_weight.shape[2]
    context_count = lax.axis_size("context")
    context_index = lax.axis_index("context")
    tensor_index = lax.axis_index("tensor")
    row_span = local_rows * context_count
    first_row = context_index * local_rows
    begin_all = layout(lengths[0], row_span)
    begin = lax.dynamic_slice_in_dim(begin_all, first_row, local_rows, 0)
    places = first_row + jnp.arange(local_rows, dtype=jnp.int32) - begin
    tables = rope_tables(places)

    column = tensor_index * slice_width
    in_bias = lax.dynamic_slice_in_dim(vectors[:NIN], column, slice_width, 1)
    steps = slice_width // LANES
    hid_bias = in_bias[3:].reshape(steps, 2, HID)
    att_bias = in_bias[:3].reshape(3, steps, LANES).transpose(1, 0, 2).reshape(steps, ATT)
    bias = jnp.stack(
        [
            jnp.pad(hid_bias[:, 0], ((0, 0), (0, WIDE - HID))),
            jnp.pad(att_bias, ((0, 0), (0, WIDE - ATT))),
            jnp.pad(hid_bias[:, 1], ((0, 0), (0, WIDE - HID))),
        ],
        1,
    ).reshape(3 * steps, 1, WIDE)
    by_group = jnp.transpose(in_weight, (1, 0, 2))
    _, _, total, _, _, _, _, result, token_grad, vec_grad = run_block(
        by_group, out_weight, tokens, cotangent, bias, vectors, tables[0], tables[1], begin_all[None]
    )
    token_grad = token_grad.reshape(local_rows, slice_width)
    vector_grad = jnp.transpose(vec_grad, (1, 0, 2)).reshape(-1, model_width)[: NIN + 3]
    new_vectors, new_vec_first, new_vec_second = adamw(
        vectors, vector_grad, vec_first, vec_second, rate_vector, 0.0
    )
    by_group_moments = [jnp.transpose(v, (1, 0, 2)) for v in (in_first, in_second)]
    new_by_group, (new_out, new_out_first, new_out_second) = adam_weights(
        total, [by_group] + by_group_moments, [out_weight, out_first, out_second]
    )
    new_in, new_in_first, new_in_second = (jnp.transpose(v, (1, 0, 2)) for v in new_by_group)
    return (
        result,
        token_grad,
        new_in,
        new_in_first,
        new_in_second,
        new_out,
        new_out_first,
        new_out_second,
        new_vectors,
        new_vec_first,
        new_vec_second,
    )


def solution(mesh):
    return jax.shard_map(
        body,
        mesh=mesh,
        in_specs=(
            P(("dp", "context"), None),
            P(("dp", "context"), None),
            P("dp", None),
            P("dp", None, "tensor"),
            P(None, "tensor", "dp"),
            P(),
            P("dp", None, "tensor"),
            P("dp", None, "tensor"),
            P(None, "tensor", "dp"),
            P(None, "tensor", "dp"),
            P(),
            P(),
        ),
        out_specs=(
            P(("dp", "context"), "tensor"),
            P(("dp", "context"), "tensor"),
            P("dp", None, "tensor"),
            P("dp", None, "tensor"),
            P("dp", None, "tensor"),
            P(None, "tensor", "dp"),
            P(None, "tensor", "dp"),
            P(None, "tensor", "dp"),
            P(),
            P(),
            P(),
        ),
        check_vma=False,
    )
```
